128 devices in a mesh: grp: 16 (over y, x), dev: 8 (over z, core).
Axes of the slice: x: 4, y: 4, z: 4, core: 2. Of those that a mesh axis runs over, the one named last changes fastest.
Arguments:
- panel: float32 [16384, 512], P(('grp', 'dev')), may hold values from -9 to 9
- trailing: float32 [16384, 1792], P(('grp', 'dev')), may hold values from -32 to 32
- counts: int32 [16384], P(('grp', 'dev')), may hold values from 1 to 16
Outputs:
- r_factor: float32 [512, 512], P('dev')
- coupling: float32 [512, 1792], P('dev')
- updated: float32 [16384, 1792], P(('grp', 'dev'))
The draws below stay inside these ranges and needn't reach their ends.
All inputs are finite; a program needn't handle non-finite values.
Results may differ from the reference program's by a relative error of at most 0.00025.
Values sent between devices are 32-bit elements; how exact they have to be, the bound alone decides.
No kernel may reach another device: no remote copies, remote signals or barrier semaphores. Data moves between devices by JAX's collectives and lax.ppermute only.
A program may use at most 320 MiB of HBM per device.

```python
import jax
import jax.numpy as jnp
from jax import lax

PANEL = 512
TRAIL = 1792
ROWS = 16384


def base_panel(key):
    factor_key = jax.random.fold_in(key, 11)
    factors = jnp.clip(jax.random.normal(factor_key, (ROWS, PANEL), jnp.float32), -5.0, 5.0)
    return factors + 0.45 * jnp.roll(factors, -1, axis=1) + 0.3 * jnp.roll(factors, -4, axis=1)


def draw_panel(key, part):
    return base_panel(key)


def draw_trailing(key, part):
    panel_vals = base_panel(key)
    pick_first = jax.random.randint(jax.random.fold_in(key, 21), (TRAIL,), 0, PANEL)
    pick_second = jax.random.randint(jax.random.fold_in(key, 22), (TRAIL,), 0, PANEL)
    coef_first = jax.random.uniform(jax.random.fold_in(key, 23), (TRAIL,), jnp.float32, -1.5, 1.5)
    coef_second = jax.random.uniform(jax.random.fold_in(key, 24), (TRAIL,), jnp.float32, -1.5, 1.5)
    noise_key = jax.random.fold_in(key, 25)
    noise = jnp.clip(jax.random.normal(noise_key, (ROWS, TRAIL), jnp.float32), -5.0, 5.0)
    first = jnp.take(panel_vals, pick_first, axis=1)
    second = jnp.take(panel_vals, pick_second, axis=1)
    return coef_first[None, :] * first + coef_second[None, :] * second + noise


def plant(array, rng, least, high):
    place = [jax.random.randint(jax.random.fold_in(rng, axis), (), 0, length) for axis, length in enumerate(array.shape)]
    main_axis = array.shape.index(max(array.shape))
    next_to = place[:main_axis] + [(place[main_axis] + 1) % array.shape[main_axis]] + place[main_axis + 1:]
    return array.at[tuple(place)].set(least).at[tuple(next_to)].set(high)


def setup_inputs(seed: int = 0) -> dict:
    arg_keys = jax.random.split(jax.random.key(seed), 4)
    panel = draw_panel(jax.random.fold_in(arg_keys[3], 71), 0)
    trailing = draw_trailing(jax.random.fold_in(arg_keys[3], 71), 0)
    counts = plant(jax.random.randint(arg_keys[2], (ROWS,), 1, 17), jax.random.fold_in(arg_keys[2], 1), 1, 16).astype(jnp.int32)
    return dict(panel=panel, trailing=trailing, counts=counts)


ridge_shift = 0.05

def reference(panel, trailing, counts):
    highest = lax.Precision.HIGHEST
    weights = counts.astype(jnp.float32) / ROWS
    weighted = panel * weights[:, None]
    gram = jnp.dot(panel.T.astype(jnp.float32), weighted.astype(jnp.float32), precision=highest, preferred_element_type=jnp.float32)
    gram = gram + ridge_shift * jnp.eye(PANEL, dtype=jnp.float32)
    cross = jnp.dot(weighted.T.astype(jnp.float32), trailing.astype(jnp.float32), precision=highest, preferred_element_type=jnp.float32)
    lower_factor = jnp.linalg.cholesky(gram)
    coupling = jax.scipy.linalg.solve_triangular(lower_factor, cross, lower=True)
    mixing = jax.scipy.linalg.solve_triangular(lower_factor.T, coupling, lower=False)
    updated = trailing - jnp.dot(panel.astype(jnp.float32), mixing.astype(jnp.float32), precision=highest, preferred_element_type=jnp.float32)
    return (lower_factor.T, coupling, updated)
```

```python
import jax
import jax.numpy as jnp
from jax import lax
from jax.experimental import pallas as pl
from jax.experimental.pallas import tpu as pltpu
from jax.sharding import Mesh, PartitionSpec as P

ridge_shift = 0.05
HIGHEST = lax.Precision.HIGHEST
tile = 128
chips = ("grp", "z")


def product(left, right, left_dim=1, right_dim=0):
    return lax.dot_general(
        left,
        right,
        (((left_dim,), (right_dim,)), ((), ())),
        precision=HIGHEST,
        preferred_element_type=jnp.float32,
    )


def factor_diagonal(work):
    sub = lax.broadcasted_iota(jnp.int32, (8, tile), 0)
    for r in range(0, tile, 8):
        left = work[r : r + 8, 0:tile]
        right = work[r : r + 8, tile : 2 * tile]
        a = {}
        for k in range(8):
            for j in range(k, 8):
                a[j, k] = jnp.broadcast_to(left[k : k + 1, r + j : r + j + 1], (8, tile))
        low, inv = {}, {}
        for k in range(8):
            inv[k] = lax.rsqrt(a[k, k])
            for j in range(k + 1, 8):
                low[j, k] = a[j, k] * inv[k]
            for j in range(k + 1, 8):
                for i in range(k + 1, j + 1):
                    a[j, i] = a[j, i] - low[j, k] * low[i, k]
        t = {}
        new_left = jnp.zeros((8, tile), jnp.float32)
        new_right = jnp.zeros((8, tile), jnp.float32)
        for k in range(8):
            t[k, k] = inv[k]
            column = jnp.where(sub == k, inv[k], 0.0)
            for j in range(k + 1, 8):
                total = low[j, k] * t[k, k]
                for i in range(k + 1, j):
                    total = total + low[j, i] * t[i, k]
                t[j, k] = -inv[j] * total
                column = jnp.where(sub == j, t[j, k], column)
            new_left = new_left + column * left[k : k + 1, :]
            new_right = new_right + column * right[k : k + 1, :]
        work[r : r + 8, 0:tile] = new_left
        work[r : r + 8, tile : 2 * tile] = new_right
        if r + 8 < tile:
            update = product(new_left, jnp.concatenate([new_left, new_right], 1), 0, 0)
            work[r + 8 : tile, :] = work[r + 8 : tile, :] - update[r + 8 : tile, :]


def factor_kernel(start_ref, gram_ref, panel_ref, upper_ref, mixed_ref, a_ref, work, tinv, rows_ref):
    rows = lax.broadcasted_iota(jnp.int32, (tile, tile), 0)
    cols = lax.broadcasted_iota(jnp.int32, (tile, tile), 1)
    eye = jnp.where(rows == cols, 1.0, 0.0).astype(jnp.float32)
    width = gram_ref.shape[0]
    own = panel_ref.shape[0]
    picked = mixed_ref.shape[0] - own
    levels = width // tile
    a_ref[...] = gram_ref[...]
    upper_ref[...] = jnp.zeros_like(upper_ref)
    rows_ref[0:own, :] = panel_ref[...]
    unit_row = lax.broadcasted_iota(jnp.int32, (picked, width), 0) + start_ref[0]
    unit_col = lax.broadcasted_iota(jnp.int32, (picked, width), 1)
    rows_ref[own:, :] = jnp.where(unit_row == unit_col, 1.0, 0.0).astype(jnp.float32)

    def load(b):
        work[:, 0:tile] = a_ref[b : b + tile, b : b + tile] + ridge_shift * eye
        work[:, tile:] = eye

    def spread(b):
        e = b + tile
        inverse = work[:, tile:]
        tinv[b:e, :] = inverse
        upper_ref[b:e, b:e] = jnp.where(cols >= rows, work[:, 0:tile], 0.0)
        y = product(rows_ref[0:own, b:e], inverse, 1, 1)
        rows_ref[0:own, b:e] = y
        if e < width:
            u = product(inverse, a_ref[b:e, e:])
            upper_ref[b:e, e:] = u
            for c in range(e, width, tile):
                a_ref[c : c + tile, c:] = a_ref[c : c + tile, c:] - product(
                    u[:, c - e : c - e + tile], u[:, c - e :], 0, 0
                )
            rows_ref[0:own, e:] = rows_ref[0:own, e:] - product(y, u)

    def level(step, carry):
        for i in range(levels):
            pl.when(step == i)(lambda i=i: load(i * tile))
        factor_diagonal(work)
        for i in range(levels):
            pl.when(step == i)(lambda i=i: spread(i * tile))
        return carry

    lax.fori_loop(0, levels, level, 0)
    for b in range(width - tile, -1, -tile):
        e = b + tile
        right = rows_ref[:, b:e]
        if e < width:
            right = right - product(mixed_ref[:, e:], upper_ref[b:e, e:], 1, 1)
        mixed_ref[:, b:e] = product(right, tinv[b:e, :])


def factor(start, gram, panel, picked):
    width = gram.shape[0]
    own = panel.shape[0]
    vmem = pl.BlockSpec(memory_space=pltpu.VMEM)
    return pl.pallas_call(
        factor_kernel,
        out_shape=(
            jax.ShapeDtypeStruct((width, width), jnp.float32),
            jax.ShapeDtypeStruct((own + picked, width), jnp.float32),
        ),
        in_specs=[pl.BlockSpec(memory_space=pltpu.SMEM), vmem, vmem],
        out_specs=(vmem, vmem),
        scratch_shapes=[
            pltpu.VMEM((width, width), jnp.float32),
            pltpu.VMEM((tile, 2 * tile), jnp.float32),
            pltpu.VMEM((width, tile), jnp.float32),
            pltpu.VMEM((own + picked, width), jnp.float32),
        ],
        compiler_params=pltpu.CompilerParams(vmem_limit_bytes=24 * 1024 * 1024),
        cost_estimate=pl.CostEstimate(flops=10**9, bytes_accessed=4 * 10**6, transcendentals=0),
    )(start, gram, panel)


def products_kernel(core_ref, panel_ref, other_ref, trail_ref, far_ref, w_ref, wo_ref, out_ref):
    core = core_ref[0]
    half = panel_ref.shape[1] // 2
    trail_half = trail_ref.shape[1]

    def add(panel, weight, trail):
        near = jnp.where(core == 0, panel[:, :half], panel[:, half:])
        a = product(panel, trail * weight, 0, 0)
        b = product(panel, near * weight, 0, 0)
        return a, b

    a0, b0 = add(panel_ref[...], w_ref[...], trail_ref[...])
    a1, b1 = add(other_ref[...], wo_ref[...], far_ref[...])
    out_ref[:, :trail_half] = a0 + a1
    out_ref[:, trail_half:] = b0 + b1


def products(core, panel, other, trail, far, weights, other_weights):
    vmem = pl.BlockSpec(memory_space=pltpu.VMEM)
    width = panel.shape[1]
    return pl.pallas_call(
        products_kernel,
        out_shape=jax.ShapeDtypeStruct((width, trail.shape[1] + width // 2), jnp.float32),
        in_specs=[pl.BlockSpec(memory_space=pltpu.SMEM)] + [vmem] * 6,
        out_specs=vmem,
        compiler_params=pltpu.CompilerParams(vmem_limit_bytes=32 * 1024 * 1024),
    )(core, panel, other, trail, far, weights, other_weights)


def finish_kernel(core_ref, mixed_ref, near_ref, far_ref, trail_ref, updated_ref, coupling_ref):
    own = trail_ref.shape[0]
    half = near_ref.shape[1]

    def side(place, cross_ref):
        for c in range(0, half, tile):
            out = product(mixed_ref[...], cross_ref[:, c : c + tile])
            at = pl.ds(place * half + c, tile)
            updated_ref[:, at] = trail_ref[:, at] - out[:own]
            coupling_ref[:, at] = out[own:]

    for place in range(2):
        for ref, match in ((near_ref, core_ref[0] == place), (far_ref, core_ref[0] != place)):
            pl.when(match)(lambda place=place, ref=ref: side(place, ref))


def finish(core, mixed, near, far, trailing):
    vmem = pl.BlockSpec(memory_space=pltpu.VMEM)
    own, trail = trailing.shape
    return pl.pallas_call(
        finish_kernel,
        out_shape=(
            jax.ShapeDtypeStruct((own, trail), jnp.float32),
            jax.ShapeDtypeStruct((mixed.shape[0] - own, trail), jnp.float32),
        ),
        in_specs=[pl.BlockSpec(memory_space=pltpu.SMEM)] + [vmem] * 4,
        out_specs=(vmem, vmem),
        compiler_params=pltpu.CompilerParams(vmem_limit_bytes=32 * 1024 * 1024),
    )(core, mixed, near, far, trailing)


def local(panel, trailing, counts):
    width = panel.shape[1]
    half = trailing.shape[1] // 2
    members = lax.axis_size("z") * lax.axis_size("core")
    groups = lax.axis_size("grp")
    chip_count = groups * lax.axis_size("z")
    core = lax.axis_index("core")
    core_one = core.astype(jnp.int32)[None]
    swap = [(0, 1), (1, 0)]
    weights = (counts.astype(jnp.float32) / (panel.shape[0] * groups * members))[:, None]
    near_trail = lax.dynamic_slice_in_dim(trailing, core * half, half, 1)
    sent_trail = lax.dynamic_slice_in_dim(trailing, (1 - core) * half, half, 1)
    with jax.named_scope("swap_inputs"):
        other_panel = lax.ppermute(panel, "core", swap)
        far_trail = lax.ppermute(sent_trail, "core", swap)
        other_weights = lax.ppermute(weights, "core", swap)
    with jax.named_scope("local_products"):
        terms = products(core_one, panel, other_panel, near_trail, far_trail, weights, other_weights)
    piece = width // chip_count
    with jax.named_scope("scatter_sum"):
        pieces = lax.all_to_all(terms.reshape(chip_count, piece, -1), chips, 0, 0, tiled=True)
        mine = jnp.sum(pieces, 0, keepdims=True)
    with jax.named_scope("gather_sums"):
        copies = jnp.broadcast_to(mine, (chip_count,) + mine.shape[1:])
        sums = lax.all_to_all(copies, chips, 0, 0, tiled=True).reshape(width, -1)
    near_cross = sums[:, :half]
    near_gram = sums[:, half:]
    with jax.named_scope("swap_gram"):
        far_gram = lax.ppermute(near_gram, "core", swap)
    with jax.named_scope("swap_cross"):
        far_cross = lax.ppermute(near_cross, "core", swap)
    first = core == 0
    gram = jnp.concatenate(
        [jnp.where(first, near_gram, far_gram), jnp.where(first, far_gram, near_gram)], 1
    )
    picked = width // members
    start = (lax.axis_index("z") * lax.axis_size("core") + core) * picked
    with jax.named_scope("factor_gram"):
        upper, mixed = factor(start.astype(jnp.int32)[None], gram, panel, picked)
    with jax.named_scope("apply_factor"):
        updated, coupling = finish(core_one, mixed, near_cross, far_cross, trailing)
    r_rows = lax.dynamic_slice_in_dim(upper, start, picked, 0)
    return (r_rows, coupling, updated)


def solution(mesh):
    groups, members = mesh.devices.shape
    split = Mesh(mesh.devices.reshape(groups, members // 2, 2), ("grp", "z", "core"))
    rows = P(("grp", "z", "core"))
    return jax.shard_map(
        local,
        mesh=split,
        in_specs=(P(("grp", "z", "core"), None), P(("grp", "z", "core"), None), rows),
        out_specs=(P(("z", "core"), None), P(("z", "core"), None), P(("grp", "z", "core"), None)),
        check_vma=False,
    )
```

```python
import jax
import jax.numpy as jnp
from jax import lax
from jax.experimental import pallas as pl
from jax.experimental.pallas import tpu as pltpu
from jax.sharding import Mesh, PartitionSpec as P

ridge_shift = 0.05
HIGHEST = lax.Precision.HIGHEST
tile = 128
strip = 32
chips = ("grp", "z")


def product(left, right, left_dim=1, right_dim=0):
    return lax.dot_general(
        left,
        right,
        (((left_dim,), (right_dim,)), ((), ())),
        precision=HIGHEST,
        preferred_element_type=jnp.float32,
    )


def factor_diagonal(work):
    sub = lax.broadcasted_iota(jnp.int32, (8, tile), 0)
    groups = strip // 8

    def spread_row(array, row):
        return jnp.broadcast_to(array[row : row + 1, :], (8, tile))

    for r in range(0, tile, strip):
        left = [work[r + 8 * g : r + 8 * g + 8, 0:tile] for g in range(groups)]
        right = [work[r + 8 * g : r + 8 * g + 8, tile : 2 * tile] for g in range(groups)]
        col = {}
        for c in range(strip):
            for g in range(c // 8, groups):
                col[c, g] = jnp.broadcast_to(left[g][:, r + c : r + c + 1], (8, tile))
        for k in range(strip):
            at, row = k // 8, k % 8
            inv = lax.rsqrt(spread_row(col[k, at], row))
            low = {g: col[k, g] * inv for g in range(at, groups)}
            for c in range(k + 1, strip):
                factor_c = spread_row(low[c // 8], c % 8)
                for g in range(c // 8, groups):
                    col[c, g] = col[c, g] - low[g] * factor_c
            below = jnp.where(sub > row, low[at], 0.0)
            for side in (left, right):
                pivot = spread_row(side[at], row) * inv
                side[at] = jnp.where(sub == row, pivot, side[at] - below * pivot)
                for g in range(at + 1, groups):
                    side[g] = side[g] - low[g] * pivot
        new_left = jnp.concatenate(left, 0)
        new_right = jnp.concatenate(right, 0)
        work[r : r + strip, 0:tile] = new_left
        work[r : r + strip, tile : 2 * tile] = new_right
        if r + strip < tile:
            update = product(new_left, jnp.concatenate([new_left, new_right], 1), 0, 0)
            work[r + strip : tile, :] = work[r + strip : tile, :] - update[r + strip : tile, :]


def factor_kernel(start_ref, gram_ref, panel_ref, upper_ref, mixed_ref, a_ref, work, tinv, rows_ref):
    rows = lax.broadcasted_iota(jnp.int32, (tile, tile), 0)
    cols = lax.broadcasted_iota(jnp.int32, (tile, tile), 1)
    eye = jnp.where(rows == cols, 1.0, 0.0).astype(jnp.float32)
    width = gram_ref.shape[0]
    own = panel_ref.shape[0]
    picked = mixed_ref.shape[0] - own
    levels = width // tile
    a_ref[...] = gram_ref[...]
    upper_ref[...] = jnp.zeros_like(upper_ref)
    rows_ref[0:own, :] = panel_ref[...]
    unit_row = lax.broadcasted_iota(jnp.int32, (picked, width), 0) + start_ref[0]
    unit_col = lax.broadcasted_iota(jnp.int32, (picked, width), 1)
    rows_ref[own:, :] = jnp.where(unit_row == unit_col, 1.0, 0.0).astype(jnp.float32)

    def load(b):
        work[:, 0:tile] = a_ref[b : b + tile, b : b + tile] + ridge_shift * eye
        work[:, tile:] = eye

    def spread(b):
        e = b + tile
        inverse = work[:, tile:]
        tinv[b:e, :] = inverse
        upper_ref[b:e, b:e] = jnp.where(cols >= rows, work[:, 0:tile], 0.0)
        y = product(rows_ref[0:own, b:e], inverse, 1, 1)
        rows_ref[0:own, b:e] = y
        if e < width:
            u = product(inverse, a_ref[b:e, e:])
            upper_ref[b:e, e:] = u
            for c in range(e, width, tile):
                a_ref[c : c + tile, c:] = a_ref[c : c + tile, c:] - product(
                    u[:, c - e : c - e + tile], u[:, c - e :], 0, 0
                )
            rows_ref[0:own, e:] = rows_ref[0:own, e:] - product(y, u)

    def level(step, carry):
        for i in range(levels):
            pl.when(step == i)(lambda i=i: load(i * tile))
        factor_diagonal(work)
        for i in range(levels):
            pl.when(step == i)(lambda i=i: spread(i * tile))
        return carry

    lax.fori_loop(0, levels, level, 0)
    for b in range(width - tile, -1, -tile):
        e = b + tile
        right = rows_ref[:, b:e]
        if e < width:
            right = right - product(mixed_ref[:, e:], upper_ref[b:e, e:], 1, 1)
        mixed_ref[:, b:e] = product(right, tinv[b:e, :])


def factor(start, gram, panel, picked):
    width = gram.shape[0]
    own = panel.shape[0]
    vmem = pl.BlockSpec(memory_space=pltpu.VMEM)
    return pl.pallas_call(
        factor_kernel,
        out_shape=(
            jax.ShapeDtypeStruct((width, width), jnp.float32),
            jax.ShapeDtypeStruct((own + picked, width), jnp.float32),
        ),
        in_specs=[pl.BlockSpec(memory_space=pltpu.SMEM), vmem, vmem],
        out_specs=(vmem, vmem),
        scratch_shapes=[
            pltpu.VMEM((width, width), jnp.float32),
            pltpu.VMEM((tile, 2 * tile), jnp.float32),
            pltpu.VMEM((width, tile), jnp.float32),
            pltpu.VMEM((own + picked, width), jnp.float32),
        ],
        compiler_params=pltpu.CompilerParams(vmem_limit_bytes=24 * 1024 * 1024),
        cost_estimate=pl.CostEstimate(flops=10**9, bytes_accessed=4 * 10**6, transcendentals=0),
    )(start, gram, panel)


def products_kernel(core_ref, panel_ref, other_ref, trail_ref, far_ref, w_ref, wo_ref, out_ref):
    core = core_ref[0]
    half = panel_ref.shape[1] // 2
    trail_half = trail_ref.shape[1]

    def add(panel, weight, trail):
        near = jnp.where(core == 0, panel[:, :half], panel[:, half:])
        a = product(panel, trail * weight, 0, 0)
        b = product(panel, near * weight, 0, 0)
        return a, b

    a0, b0 = add(panel_ref[...], w_ref[...], trail_ref[...])
    a1, b1 = add(other_ref[...], wo_ref[...], far_ref[...])
    out_ref[:, :trail_half] = a0 + a1
    out_ref[:, trail_half:] = b0 + b1


def products(core, panel, other, trail, far, weights, other_weights):
    vmem = pl.BlockSpec(memory_space=pltpu.VMEM)
    width = panel.shape[1]
    return pl.pallas_call(
        products_kernel,
        out_shape=jax.ShapeDtypeStruct((width, trail.shape[1] + width // 2), jnp.float32),
        in_specs=[pl.BlockSpec(memory_space=pltpu.SMEM)] + [vmem] * 6,
        out_specs=vmem,
        compiler_params=pltpu.CompilerParams(vmem_limit_bytes=32 * 1024 * 1024),
    )(core, panel, other, trail, far, weights, other_weights)


def finish_kernel(core_ref, mixed_ref, near_ref, far_ref, trail_ref, updated_ref, coupling_ref):
    own = trail_ref.shape[0]
    half = near_ref.shape[1]

    def side(place, cross_ref):
        for c in range(0, half, tile):
            out = product(mixed_ref[...], cross_ref[:, c : c + tile])
            at = pl.ds(place * half + c, tile)
            updated_ref[:, at] = trail_ref[:, at] - out[:own]
            coupling_ref[:, at] = out[own:]

    for place in range(2):
        for ref, match in ((near_ref, core_ref[0] == place), (far_ref, core_ref[0] != place)):
            pl.when(match)(lambda place=place, ref=ref: side(place, ref))


def finish(core, mixed, near, far, trailing):
    vmem = pl.BlockSpec(memory_space=pltpu.VMEM)
    own, trail = trailing.shape
    return pl.pallas_call(
        finish_kernel,
        out_shape=(
            jax.ShapeDtypeStruct((own, trail), jnp.float32),
            jax.ShapeDtypeStruct((mixed.shape[0] - own, trail), jnp.float32),
        ),
        in_specs=[pl.BlockSpec(memory_space=pltpu.SMEM)] + [vmem] * 4,
        out_specs=(vmem, vmem),
        compiler_params=pltpu.CompilerParams(vmem_limit_bytes=32 * 1024 * 1024),
    )(core, mixed, near, far, trailing)


def local(panel, trailing, counts):
    width = panel.shape[1]
    half = trailing.shape[1] // 2
    members = lax.axis_size("z") * lax.axis_size("core")
    groups = lax.axis_size("grp")
    chip_count = groups * lax.axis_size("z")
    core = lax.axis_index("core")
    core_one = core.astype(jnp.int32)[None]
    swap = [(0, 1), (1, 0)]
    weights = (counts.astype(jnp.float32) / (panel.shape[0] * groups * members))[:, None]
    near_trail = lax.dynamic_slice_in_dim(trailing, core * half, half, 1)
    sent_trail = lax.dynamic_slice_in_dim(trailing, (1 - core) * half, half, 1)
    with jax.named_scope("swap_inputs"):
        other_panel = lax.ppermute(panel, "core", swap)
        far_trail = lax.ppermute(sent_trail, "core", swap)
        other_weights = lax.ppermute(weights, "core", swap)
    with jax.named_scope("local_products"):
        terms = products(core_one, panel, other_panel, near_trail, far_trail, weights, other_weights)
    piece = width // chip_count
    with jax.named_scope("scatter_sum"):
        pieces = lax.all_to_all(terms.reshape(chip_count, piece, -1), chips, 0, 0, tiled=True)
        mine = jnp.sum(pieces, 0, keepdims=True)
    with jax.named_scope("gather_sums"):
        copies = jnp.broadcast_to(mine, (chip_count,) + mine.shape[1:])
        sums = lax.all_to_all(copies, chips, 0, 0, tiled=True).reshape(width, -1)
    near_cross = sums[:, :half]
    near_gram = sums[:, half:]
    with jax.named_scope("swap_gram"):
        far_gram = lax.ppermute(near_gram, "core", swap)
    with jax.named_scope("swap_cross"):
        far_cross = lax.ppermute(near_cross, "core", swap)
    first = core == 0
    gram = jnp.concatenate(
        [jnp.where(first, near_gram, far_gram), jnp.where(first, far_gram, near_gram)], 1
    )
    picked = width // members
    start = (lax.axis_index("z") * lax.axis_size("core") + core) * picked
    with jax.named_scope("factor_gram"):
        upper, mixed = factor(start.astype(jnp.int32)[None], gram, panel, picked)
    with jax.named_scope("apply_factor"):
        updated, coupling = finish(core_one, mixed, near_cross, far_cross, trailing)
    r_rows = lax.dynamic_slice_in_dim(upper, start, picked, 0)
    return (r_rows, coupling, updated)


def solution(mesh):
    groups, members = mesh.devices.shape
    split = Mesh(mesh.devices.reshape(groups, members // 2, 2), ("grp", "z", "core"))
    rows = P(("grp", "z", "core"))
    return jax.shard_map(
        local,
        mesh=split,
        in_specs=(P(("grp", "z", "core"), None), P(("grp", "z", "core"), None), rows),
        out_specs=(P(("z", "core"), None), P(("z", "core"), None), P(("grp", "z", "core"), None)),
        check_vma=False,
    )
```

```python
import functools

import jax
import jax.numpy as jnp
from jax import lax
from jax.experimental import pallas as pl
from jax.experimental.pallas import tpu as pltpu
from jax.sharding import Mesh, PartitionSpec as P

ridge_shift = 0.05
HIGHEST = lax.Precision.HIGHEST
tile = 128
strip = 32
chips = ("grp", "z")
classes = 4


def product(left, right, left_dim=1, right_dim=0):
    return lax.dot_general(
        left,
        right,
        (((left_dim,), (right_dim,)), ((), ())),
        precision=HIGHEST,
        preferred_element_type=jnp.float32,
    )


def factor_diagonal(work):
    sub = lax.broadcasted_iota(jnp.int32, (8, tile), 0)
    groups = strip // 8

    def spread_row(array, row):
        return jnp.broadcast_to(array[row : row + 1, :], (8, tile))

    for r in range(0, tile, strip):
        left = [work[r + 8 * g : r + 8 * g + 8, 0:tile] for g in range(groups)]
        right = [work[r + 8 * g : r + 8 * g + 8, tile : 2 * tile] for g in range(groups)]
        col = {}
        for c in range(strip):
            for g in range(c // 8, groups):
                col[c, g] = jnp.broadcast_to(left[g][:, r + c : r + c + 1], (8, tile))
        for k in range(strip):
            at, row = k // 8, k % 8
            inv = lax.rsqrt(spread_row(col[k, at], row))
            low = {g: col[k, g] * inv for g in range(at, groups)}
            for c in range(k + 1, strip):
                factor_c = spread_row(low[c // 8], c % 8)
                for g in range(c // 8, groups):
                    col[c, g] = col[c, g] - low[g] * factor_c
            below = jnp.where(sub > row, low[at], 0.0)
            for side in (left, right):
                pivot = spread_row(side[at], row) * inv
                side[at] = jnp.where(sub == row, pivot, side[at] - below * pivot)
                for g in range(at + 1, groups):
                    side[g] = side[g] - low[g] * pivot
        new_left = jnp.concatenate(left, 0)
        new_right = jnp.concatenate(right, 0)
        work[r : r + strip, 0:tile] = new_left
        work[r : r + strip, tile : 2 * tile] = new_right
        if r + strip < tile:
            update = product(new_left, jnp.concatenate([new_left, new_right], 1), 0, 0)
            work[r + strip : tile, :] = work[r + strip : tile, :] - update[r + strip : tile, :]


gram_blocks = (((0, 0), (1, 1), (0, 1), (0, 2), (0, 3)), ((2, 2), (3, 3), (2, 3), (1, 2), (1, 3)))


def products_kernel(core_ref, panel_ref, other_ref, trail_ref, far_ref, counts_ref, far_counts_ref, out_ref, pt, wp, wt, quarters, gram, *, chip_count, total_rows):
    core = core_ref[0]
    own, width = panel_ref.shape
    half = trail_ref.shape[1]
    for at, rows, trail, count in ((0, panel_ref, trail_ref, counts_ref), (own, other_ref, far_ref, far_counts_ref)):
        weight = jnp.transpose(jnp.broadcast_to(count[...].astype(jnp.float32) / total_rows, (own, own)))
        for c in range(0, width, tile):
            block = rows[:, c : c + tile]
            pt[c : c + tile, at : at + own] = jnp.transpose(block)
            wp[at : at + own, c : c + tile] = block * weight
        for c in range(0, half, tile):
            wt[at : at + own, c : c + tile] = trail[:, c : c + tile] * weight
    step = 2 * tile
    for c in range(0, half, step):
        n = min(step, half - c)
        part = product(pt[...], wt[:, c : c + n])
        for k in range(classes):
            for j in range(0, n, tile):
                quarters[k, c + j : c + j + tile, :] = part[k * tile : (k + 1) * tile, j : j + tile]
    near = pl.multiple_of(core * step, tile)
    first = product(pt[pl.ds(near, tile), :], wp[:, pl.ds(near, step)])
    gram[0:tile, :] = first[:, :tile]
    gram[2 * tile : 3 * tile, :] = first[:, tile:]
    near = pl.multiple_of(core * step + tile, tile)
    gram[tile : 2 * tile, :] = product(pt[pl.ds(near, tile), :], wp[:, pl.ds(near, tile)])
    near = pl.multiple_of(core * tile, tile)
    last = product(pt[pl.ds(near, tile), :], wp[:, step:])
    gram[3 * tile : 4 * tile, :] = last[:, :tile]
    gram[4 * tile :, :] = last[:, tile:]
    chunk = half // chip_count
    gram_chunk = gram.shape[0] // chip_count
    piece = classes * chunk + gram_chunk
    for q in range(chip_count):
        for k in range(classes):
            at = q * piece + k * chunk
            out_ref[at : at + chunk, :] = quarters[k, q * chunk : (q + 1) * chunk, :]
        at = q * piece + classes * chunk
        out_ref[at : at + gram_chunk, :] = gram[q * gram_chunk : (q + 1) * gram_chunk, :]


def products(core, panel, other, trailing, far, counts, far_counts, chip_count, total_rows):
    own, width = panel.shape
    half = far.shape[1]
    gram_rows = len(gram_blocks[0]) * tile
    whole = lambda shape: pl.BlockSpec(shape, lambda i, core: (0, 0))
    return pl.pallas_call(
        functools.partial(products_kernel, chip_count=chip_count, total_rows=total_rows),
        out_shape=jax.ShapeDtypeStruct((classes * half + gram_rows, tile), jnp.float32),
        grid_spec=pltpu.PrefetchScalarGridSpec(
            num_scalar_prefetch=1,
            grid=(1,),
            in_specs=[
                whole((own, width)),
                whole((own, width)),
                pl.BlockSpec((own, half), lambda i, core: (0, core[0])),
                whole((own, half)),
                whole((1, own)),
                whole((1, own)),
            ],
            out_specs=whole((classes * half + gram_rows, tile)),
            scratch_shapes=[
                pltpu.VMEM((width, 2 * own), jnp.float32),
                pltpu.VMEM((2 * own, width), jnp.float32),
                pltpu.VMEM((2 * own, half), jnp.float32),
                pltpu.VMEM((classes, half, tile), jnp.float32),
                pltpu.VMEM((gram_rows, tile), jnp.float32),
            ],
        ),
        compiler_params=pltpu.CompilerParams(vmem_limit_bytes=32 * 1024 * 1024),
    )(core, panel, other, trailing, far, counts, far_counts)


def sum_kernel(pieces_ref, copies_ref, four, *, chip_count, chunk, gram_chunk, kinds):
    piece = classes * chunk + gram_chunk
    size = 4 * piece
    total = pieces_ref[0:size, :]
    for at in range(size, chip_count * piece, size):
        total = total + pieces_ref[at : at + size, :]
    four[...] = total
    mine = four[0:piece, :]
    for at in range(piece, size, piece):
        mine = mine + four[at : at + piece, :]
    for k in range(classes):
        four[0:piece, :] = mine
        copy = jnp.concatenate(
            [four[k * chunk : (k + 1) * chunk, :], four[classes * chunk : piece, :]], 0
        )
        for chip, kind in enumerate(kinds):
            if kind == k:
                copies_ref[chip * (chunk + gram_chunk) : (chip + 1) * (chunk + gram_chunk), :] = copy


def sum_pieces(pieces, chip_count, chunk, gram_chunk, kinds):
    vmem = pl.BlockSpec(memory_space=pltpu.VMEM)
    return pl.pallas_call(
        functools.partial(
            sum_kernel, chip_count=chip_count, chunk=chunk, gram_chunk=gram_chunk, kinds=kinds
        ),
        out_shape=jax.ShapeDtypeStruct((chip_count * (chunk + gram_chunk), tile), jnp.float32),
        in_specs=[vmem],
        out_specs=vmem,
        scratch_shapes=[pltpu.VMEM((4 * (classes * chunk + gram_chunk), tile), jnp.float32)],
        compiler_params=pltpu.CompilerParams(vmem_limit_bytes=16 * 1024 * 1024),
    )(pieces)


def unpack_kernel(copies_ref, quarter_ref, gram_ref, *, chip_count, chunk, gram_chunk):
    both = chunk + gram_chunk
    for q in range(chip_count):
        quarter_ref[q * chunk : (q + 1) * chunk, :] = copies_ref[q * both : q * both + chunk, :]
        gram_ref[q * gram_chunk : (q + 1) * gram_chunk, :] = copies_ref[q * both + chunk : (q + 1) * both, :]


def unpack(copies, chip_count, chunk, gram_chunk):
    vmem = pl.BlockSpec(memory_space=pltpu.VMEM)
    return pl.pallas_call(
        functools.partial(unpack_kernel, chip_count=chip_count, chunk=chunk, gram_chunk=gram_chunk),
        out_shape=(
            jax.ShapeDtypeStruct((chip_count * chunk, tile), jnp.float32),
            jax.ShapeDtypeStruct((chip_count * gram_chunk, tile), jnp.float32),
        ),
        in_specs=[vmem],
        out_specs=(vmem, vmem),
        compiler_params=pltpu.CompilerParams(vmem_limit_bytes=16 * 1024 * 1024),
    )(copies)


def factor_kernel(core_ref, near_ref, far_ref, panel_ref, upper_ref, tinv, y_ref, a_ref, rows_ref, work):
    rows = lax.broadcasted_iota(jnp.int32, (tile, tile), 0)
    cols = lax.broadcasted_iota(jnp.int32, (tile, tile), 1)
    eye = jnp.where(rows == cols, 1.0, 0.0).astype(jnp.float32)
    width = upper_ref.shape[0]
    levels = width // tile
    for core, blocks in enumerate(gram_blocks):
        for at, (i, j) in enumerate(blocks):
            side = slice(at * tile, (at + 1) * tile)
            block = jnp.where(core_ref[0] == core, near_ref[side, :], far_ref[side, :])
            if i == j:
                block = block + ridge_shift * eye
            a_ref[i * tile : (i + 1) * tile, j * tile : (j + 1) * tile] = block
    upper_ref[...] = jnp.zeros_like(upper_ref)
    rows_ref[...] = panel_ref[...]

    def load(b):
        work[:, 0:tile] = a_ref[b : b + tile, b : b + tile]
        work[:, tile:] = eye

    def spread(b):
        e = b + tile
        inverse = work[:, tile:]
        tinv[b:e, :] = inverse
        upper_ref[b:e, b:e] = jnp.where(cols >= rows, work[:, 0:tile], 0.0)
        y = product(rows_ref[:, b:e], inverse, 1, 1)
        y_ref[:, b:e] = y
        if e < width:
            u = product(inverse, a_ref[b:e, e:])
            upper_ref[b:e, e:] = u
            for c in range(e, width, tile):
                a_ref[c : c + tile, c:] = a_ref[c : c + tile, c:] - product(
                    u[:, c - e : c - e + tile], u[:, c - e :], 0, 0
                )
            rows_ref[:, e:] = rows_ref[:, e:] - product(y, u)

    def level(step, carry):
        for i in range(levels):
            pl.when(step == i)(lambda i=i: load(i * tile))
        factor_diagonal(work)
        for i in range(levels):
            pl.when(step == i)(lambda i=i: spread(i * tile))
        return carry

    lax.fori_loop(0, levels, level, 0)


def factor(core, near, far, panel):
    own, width = panel.shape
    vmem = pl.BlockSpec(memory_space=pltpu.VMEM)
    return pl.pallas_call(
        factor_kernel,
        out_shape=(
            jax.ShapeDtypeStruct((width, width), jnp.float32),
            jax.ShapeDtypeStruct((width, tile), jnp.float32),
            jax.ShapeDtypeStruct((own, width), jnp.float32),
        ),
        in_specs=[pl.BlockSpec(memory_space=pltpu.SMEM), vmem, vmem, vmem],
        out_specs=(vmem, vmem, vmem),
        scratch_shapes=[
            pltpu.VMEM((width, width), jnp.float32),
            pltpu.VMEM((own, width), jnp.float32),
            pltpu.VMEM((tile, 2 * tile), jnp.float32),
        ],
        compiler_params=pltpu.CompilerParams(vmem_limit_bytes=16 * 1024 * 1024),
        cost_estimate=pl.CostEstimate(flops=16 * 10**9, bytes_accessed=4 * 10**6, transcendentals=0),
    )(core, near, far, panel)


def back_kernel(start_ref, upper_ref, tinv, y_ref, mixed_ref, r_ref, right):
    own, width = y_ref.shape
    picked = r_ref.shape[0]
    right[0:own, :] = y_ref[...]
    unit_row = lax.broadcasted_iota(jnp.int32, (picked, width), 0) + start_ref[0]
    unit_col = lax.broadcasted_iota(jnp.int32, (picked, width), 1)
    right[own:, :] = jnp.where(unit_row == unit_col, 1.0, 0.0).astype(jnp.float32)
    r_ref[...] = upper_ref[pl.ds(pl.multiple_of(start_ref[0], picked), picked), :]
    done = None
    for b in range(width - tile, -1, -tile):
        e = b + tile
        side = right[:, b:e]
        if done is not None:
            side = side - product(done, upper_ref[b:e, e:], 1, 1)
        part = product(side, tinv[b:e, :])
        mixed_ref[b // tile] = part
        done = part if done is None else jnp.concatenate([part, done], 1)


def back(start, upper, tinv, y, picked):
    own, width = y.shape
    vmem = pl.BlockSpec(memory_space=pltpu.VMEM)
    return pl.pallas_call(
        back_kernel,
        out_shape=(
            jax.ShapeDtypeStruct((width // tile, own + picked, tile), jnp.float32),
            jax.ShapeDtypeStruct((picked, width), jnp.float32),
        ),
        in_specs=[pl.BlockSpec(memory_space=pltpu.SMEM), vmem, vmem, vmem],
        out_specs=(vmem, vmem),
        scratch_shapes=[pltpu.VMEM((own + picked, width), jnp.float32)],
        compiler_params=pltpu.CompilerParams(vmem_limit_bytes=16 * 1024 * 1024),
        cost_estimate=pl.CostEstimate(flops=4 * 10**9, bytes_accessed=2 * 10**6, transcendentals=0),
    )(start, upper, tinv, y)


def finish_kernel(place_ref, mixed_ref, *refs):
    near, far = refs[:classes], refs[classes : 2 * classes]
    trail_ref, updated_ref, coupling_ref = refs[2 * classes :]
    own = trail_ref.shape[0]
    half = near[0].shape[0]
    core = place_ref[0]
    left = [mixed_ref[place_ref[1 + m]] for m in range(classes)]
    left = [jnp.concatenate(left[m : m + 2], 1) for m in range(0, classes, 2)]
    for c in range(0, half, tile):
        out = None
        for m in range(0, classes, 2):
            right = jnp.concatenate(
                [
                    jnp.concatenate([side[m][c : c + tile, :], side[m + 1][c : c + tile, :]], 0)
                    for side in (near, far)
                ],
                1,
            )
            term = product(left[m // 2], right)
            out = term if out is None else out + term
        for part, where in ((out[:, :tile], core), (out[:, tile:], 1 - core)):
            at = pl.ds(pl.multiple_of(where * half + c, tile), tile)
            updated_ref[:, at] = trail_ref[:, at] - part[:own]
            coupling_ref[:, at] = part[own:]


def finish(place, mixed, near, far, trailing):
    vmem = pl.BlockSpec(memory_space=pltpu.VMEM)
    own, trail = trailing.shape
    return pl.pallas_call(
        finish_kernel,
        out_shape=(
            jax.ShapeDtypeStruct((own, trail), jnp.float32),
            jax.ShapeDtypeStruct((mixed.shape[1] - own, trail), jnp.float32),
        ),
        in_specs=[pl.BlockSpec(memory_space=pltpu.SMEM)] + [vmem] * (2 + 2 * classes),
        out_specs=(vmem, vmem),
        compiler_params=pltpu.CompilerParams(vmem_limit_bytes=32 * 1024 * 1024),
    )(place, mixed, *near, *far, trailing)


def kind_of(x, y, z):
    return (x % 2) ^ (2 * (y % 2)) ^ (3 * (z % 2))


def local(panel, trailing, counts):
    own, width = panel.shape
    half = trailing.shape[1] // 2
    depth = lax.axis_size("z")
    groups = lax.axis_size("grp")
    side = 4
    members = 2 * depth
    chip_count = groups * depth
    chunk = half // chip_count
    gram_chunk = len(gram_blocks[0]) * tile // chip_count
    kinds = [kind_of(g % side, g // side, z) for g in range(groups) for z in range(depth)]
    group, z, core = lax.axis_index("grp"), lax.axis_index("z"), lax.axis_index("core")
    kind = kind_of(group % side, group // side, z)
    core_one = core.astype(jnp.int32)[None]
    place = jnp.stack([core] + [kind ^ m for m in range(classes)]).astype(jnp.int32)
    swap = [(0, 1), (1, 0)]
    count_row = counts[None, :]
    sent_trail = lax.dynamic_slice_in_dim(trailing, (1 - core) * half, half, 1)
    with jax.named_scope("swap_inputs"):
        far_counts = lax.ppermute(count_row, "core", swap)
        other_panel = lax.ppermute(panel, "core", swap)
        far_trail = lax.ppermute(sent_trail, "core", swap)
    with jax.named_scope("local_products"):
        terms = products(
            core_one, panel, other_panel, trailing, far_trail, count_row, far_counts, chip_count, own * groups * members
        )
    with jax.named_scope("scatter_sums"):
        pieces = lax.all_to_all(terms.reshape(chip_count, 1, -1), chips, 0, 0, tiled=True)
    with jax.named_scope("sum_pieces"):
        copies = sum_pieces(pieces.reshape(-1, tile), chip_count, chunk, gram_chunk, kinds)
    with jax.named_scope("gather_sums"):
        copies = lax.all_to_all(copies.reshape(chip_count, 1, -1), chips, 0, 0, tiled=True)
    with jax.named_scope("unpack_sums"):
        quarter, near_gram = unpack(copies.reshape(-1, tile), chip_count, chunk, gram_chunk)
    with jax.named_scope("swap_gram"):
        far_gram = lax.ppermute(near_gram, "core", swap)
    near = [quarter]
    with jax.named_scope("quarters_along_x"):
        near.append(lax.ppermute(quarter, "grp", [(i, i ^ 1) for i in range(groups)]))
    with jax.named_scope("quarters_along_y"):
        near.append(lax.ppermute(quarter, "grp", [(i, i ^ side) for i in range(groups)]))
    with jax.named_scope("quarters_along_z"):
        near.append(lax.ppermute(quarter, "z", [(i, i ^ 1) for i in range(depth)]))
    with jax.named_scope("factor_gram"):
        upper, tinv, y = factor(core_one, near_gram, far_gram, panel)
    upper, tinv, y, *near = lax.optimization_barrier((upper, tinv, y, *near))
    with jax.named_scope("swap_quarters"):
        far = [lax.ppermute(part, "core", swap) for part in near]
    picked = width // members
    start = (z * 2 + core) * picked
    with jax.named_scope("back_substitute"):
        mixed, r_rows = back(start.astype(jnp.int32)[None], upper, tinv, y, picked)
    with jax.named_scope("apply_factor"):
        updated, coupling = finish(place, mixed, near, far, trailing)
    return (r_rows, coupling, updated)


def solution(mesh):
    groups, members = mesh.devices.shape
    split = Mesh(mesh.devices.reshape(groups, members // 2, 2), ("grp", "z", "core"))
    rows = P(("grp", "z", "core"))
    return jax.shard_map(
        local,
        mesh=split,
        in_specs=(P(("grp", "z", "core"), None), P(("grp", "z", "core"), None), rows),
        out_specs=(P(("z", "core"), None), P(("z", "core"), None), P(("grp", "z", "core"), None)),
        check_vma=False,
    )
```

```python
import functools

import jax
import jax.numpy as jnp
from jax import lax
from jax.experimental import pallas as pl
from jax.experimental.pallas import tpu as pltpu
from jax.sharding import Mesh, PartitionSpec as P

ridge_shift = 0.05
HIGHEST = lax.Precision.HIGHEST
tile = 128
strip = 32
chips = ("grp", "z")
classes = 4


def product(left, right, left_dim=1, right_dim=0):
    return lax.dot_general(
        left,
        right,
        (((left_dim,), (right_dim,)), ((), ())),
        precision=HIGHEST,
        preferred_element_type=jnp.float32,
    )


def factor_diagonal(work):
    sub = lax.broadcasted_iota(jnp.int32, (8, tile), 0)
    groups = strip // 8

    def spread_row(array, row):
        return jnp.broadcast_to(array[row : row + 1, :], (8, tile))

    for r in range(0, tile, strip):
        left = [work[r + 8 * g : r + 8 * g + 8, 0:tile] for g in range(groups)]
        right = [work[r + 8 * g : r + 8 * g + 8, tile : 2 * tile] for g in range(groups)]
        col = {}
        for c in range(strip):
            for g in range(c // 8, groups):
                col[c, g] = jnp.broadcast_to(left[g][:, r + c : r + c + 1], (8, tile))
        for k in range(strip):
            at, row = k // 8, k % 8
            inv = lax.rsqrt(spread_row(col[k, at], row))
            low = {g: col[k, g] * inv for g in range(at, groups)}
            for c in range(k + 1, strip):
                factor_c = spread_row(low[c // 8], c % 8)
                for g in range(c // 8, groups):
                    col[c, g] = col[c, g] - low[g] * factor_c
            below = jnp.where(sub > row, low[at], 0.0)
            for side in (left, right):
                pivot = spread_row(side[at], row) * inv
                side[at] = jnp.where(sub == row, pivot, side[at] - below * pivot)
                for g in range(at + 1, groups):
                    side[g] = side[g] - low[g] * pivot
        new_left = jnp.concatenate(left, 0)
        new_right = jnp.concatenate(right, 0)
        work[r : r + strip, 0:tile] = new_left
        work[r : r + strip, tile : 2 * tile] = new_right
        if r + strip < tile:
            update = product(new_left, jnp.concatenate([new_left, new_right], 1), 0, 0)
            work[r + strip : tile, :] = work[r + strip : tile, :] - update[r + strip : tile, :]


gram_blocks = (((0, 0), (1, 1), (0, 1), (0, 2), (0, 3)), ((2, 2), (3, 3), (2, 3), (1, 2), (1, 3)))


def products_kernel(place_ref, panel_ref, other_ref, trail_ref, far_ref, counts_ref, far_counts_ref, *refs, total_rows):
    outs, gram, (pt, wp, wt, quarters) = refs[:classes], refs[classes], refs[classes + 1 :]
    core = place_ref[0]
    own, width = panel_ref.shape
    half = trail_ref.shape[1]
    for at, rows, trail, count in ((0, panel_ref, trail_ref, counts_ref), (own, other_ref, far_ref, far_counts_ref)):
        weight = jnp.transpose(jnp.broadcast_to(count[...].astype(jnp.float32) / total_rows, (own, own)))
        for c in range(0, width, tile):
            block = rows[:, c : c + tile]
            pt[c : c + tile, at : at + own] = jnp.transpose(block)
            wp[at : at + own, c : c + tile] = block * weight
        for c in range(0, half, tile):
            wt[at : at + own, c : c + tile] = trail[:, c : c + tile] * weight
    step = 2 * tile
    for c in range(0, half, step):
        n = min(step, half - c)
        part = product(pt[...], wt[:, c : c + n])
        for k in range(classes):
            for j in range(0, n, tile):
                quarters[k, c + j : c + j + tile, :] = part[k * tile : (k + 1) * tile, j : j + tile]
    for m in range(classes):
        outs[m][...] = quarters[place_ref[1 + m]]
    near = pl.multiple_of(core * step, tile)
    first = product(pt[pl.ds(near, tile), :], wp[:, pl.ds(near, step)])
    gram[0:tile, :] = first[:, :tile]
    gram[2 * tile : 3 * tile, :] = first[:, tile:]
    near = pl.multiple_of(core * step + tile, tile)
    gram[tile : 2 * tile, :] = product(pt[pl.ds(near, tile), :], wp[:, pl.ds(near, tile)])
    near = pl.multiple_of(core * tile, tile)
    last = product(pt[pl.ds(near, tile), :], wp[:, step:])
    gram[3 * tile : 4 * tile, :] = last[:, :tile]
    gram[4 * tile :, :] = last[:, tile:]


def products(place, panel, other, trailing, far, counts, far_counts, total_rows):
    own, width = panel.shape
    half = far.shape[1]
    gram_rows = len(gram_blocks[0]) * tile
    whole = lambda shape: pl.BlockSpec(shape, lambda i, place: (0, 0))
    return pl.pallas_call(
        functools.partial(products_kernel, total_rows=total_rows),
        out_shape=[jax.ShapeDtypeStruct((half, tile), jnp.float32)] * classes
        + [jax.ShapeDtypeStruct((gram_rows, tile), jnp.float32)],
        grid_spec=pltpu.PrefetchScalarGridSpec(
            num_scalar_prefetch=1,
            grid=(1,),
            in_specs=[
                whole((own, width)),
                whole((own, width)),
                pl.BlockSpec((own, half), lambda i, place: (0, place[0])),
                whole((own, half)),
                whole((1, own)),
                whole((1, own)),
            ],
            out_specs=[whole((half, tile))] * classes + [whole((gram_rows, tile))],
            scratch_shapes=[
                pltpu.VMEM((width, 2 * own), jnp.float32),
                pltpu.VMEM((2 * own, width), jnp.float32),
                pltpu.VMEM((2 * own, half), jnp.float32),
                pltpu.VMEM((classes, half, tile), jnp.float32),
            ],
        ),
        compiler_params=pltpu.CompilerParams(vmem_limit_bytes=32 * 1024 * 1024),
    )(place, panel, other, trailing, far, counts, far_counts)


def combine_kernel(gram_ref, *refs, chip_count):
    parts, out_ref, four = refs[:classes], refs[classes], refs[classes + 1]
    size = gram_ref.shape[0] // chip_count
    chunk = parts[0].shape[0] // chip_count
    total = gram_ref[0 : 4 * size, :]
    for at in range(4 * size, chip_count * size, 4 * size):
        total = total + gram_ref[at : at + 4 * size, :]
    four[...] = total
    gram = four[0:size, :]
    for at in range(size, 4 * size, size):
        gram = gram + four[at : at + size, :]
    for q in range(chip_count):
        side = slice(q * chunk, (q + 1) * chunk)
        cross = (parts[0][side, :] + parts[1][side, :]) + (parts[2][side, :] + parts[3][side, :])
        out_ref[q * (size + chunk) : (q + 1) * (size + chunk), :] = jnp.concatenate([gram, cross], 0)


def combine(gram_pieces, parts, chip_count):
    vmem = pl.BlockSpec(memory_space=pltpu.VMEM)
    gram_rows, rows = gram_pieces.shape[0], parts[0].shape[0]
    return pl.pallas_call(
        functools.partial(combine_kernel, chip_count=chip_count),
        out_shape=jax.ShapeDtypeStruct((gram_rows + rows, tile), jnp.float32),
        in_specs=[vmem] * (1 + classes),
        out_specs=vmem,
        scratch_shapes=[pltpu.VMEM((4 * gram_rows // chip_count, tile), jnp.float32)],
        compiler_params=pltpu.CompilerParams(vmem_limit_bytes=16 * 1024 * 1024),
    )(gram_pieces, *parts)


def unpack_kernel(mixed_ref, gram_ref, copies_ref, sums, *, size, chunk, kinds):
    both = size + chunk
    for k in range(classes):
        total = None
        for q, kind in enumerate(kinds):
            if kind == k:
                piece = mixed_ref[q * both : (q + 1) * both, :]
                total = piece if total is None else total + piece
        sums[...] = total
        cross = sums[size:, :]
        for q, kind in enumerate(kinds):
            if kind == k:
                copies_ref[q * chunk : (q + 1) * chunk, :] = cross
    for q in range(len(kinds)):
        gram_ref[q * size : (q + 1) * size, :] = mixed_ref[q * both : q * both + size, :]


def unpack(mixed, size, chunk, kinds):
    vmem = pl.BlockSpec(memory_space=pltpu.VMEM)
    return pl.pallas_call(
        functools.partial(unpack_kernel, size=size, chunk=chunk, kinds=kinds),
        out_shape=(
            jax.ShapeDtypeStruct((len(kinds) * size, tile), jnp.float32),
            jax.ShapeDtypeStruct((len(kinds) * chunk, tile), jnp.float32),
        ),
        in_specs=[vmem],
        out_specs=(vmem, vmem),
        scratch_shapes=[pltpu.VMEM((size + chunk, tile), jnp.float32)],
        compiler_params=pltpu.CompilerParams(vmem_limit_bytes=16 * 1024 * 1024),
    )(mixed)


def factor_levels(a_ref, rows_ref, work, upper_ref, tinv, y_ref):
    rows = lax.broadcasted_iota(jnp.int32, (tile, tile), 0)
    cols = lax.broadcasted_iota(jnp.int32, (tile, tile), 1)
    eye = jnp.where(rows == cols, 1.0, 0.0).astype(jnp.float32)
    width = a_ref.shape[0]
    levels = tinv.shape[0] // tile
    upper_ref[...] = jnp.zeros_like(upper_ref)

    def load(b):
        work[:, 0:tile] = a_ref[b : b + tile, b : b + tile]
        work[:, tile:] = eye

    def spread(b):
        e = b + tile
        inverse = work[:, tile:]
        tinv[b:e, :] = inverse
        upper_ref[b:e, b:e] = jnp.where(cols >= rows, work[:, 0:tile], 0.0)
        y = product(rows_ref[:, b:e], inverse, 1, 1)
        y_ref[:, b:e] = y
        if e < width:
            u = product(inverse, a_ref[b:e, e:])
            upper_ref[b:e, e:] = u
            for c in range(e, width, tile):
                a_ref[c : c + tile, c:] = a_ref[c : c + tile, c:] - product(
                    u[:, c - e : c - e + tile], u[:, c - e :], 0, 0
                )
            rows_ref[:, e:] = rows_ref[:, e:] - product(y, u)

    def level(step, carry):
        for i in range(levels):
            pl.when(step == i)(lambda i=i: load(i * tile))
        factor_diagonal(work)
        for i in range(levels):
            pl.when(step == i)(lambda i=i: spread(i * tile))
        return carry

    lax.fori_loop(0, levels, level, 0)


def factor_first_kernel(place_ref, near_ref, far_ref, panel_ref, upper_ref, tinv, y_ref, rest_a, rest_rows, a_ref, rows_ref, work):
    rows = lax.broadcasted_iota(jnp.int32, (tile, tile), 0)
    cols = lax.broadcasted_iota(jnp.int32, (tile, tile), 1)
    shift = jnp.where(rows == cols, ridge_shift, 0.0).astype(jnp.float32)
    for core, blocks in enumerate(gram_blocks):
        for at, (i, j) in enumerate(blocks):
            side = slice(at * tile, (at + 1) * tile)
            block = jnp.where(place_ref[0] == core, near_ref[side, :], far_ref[side, :])
            if i == j:
                block = block + shift
            a_ref[i * tile : (i + 1) * tile, j * tile : (j + 1) * tile] = block
    rows_ref[...] = panel_ref[...]
    factor_levels(a_ref, rows_ref, work, upper_ref, tinv, y_ref)
    done = tinv.shape[0]
    for c in range(done, a_ref.shape[0], tile):
        rest_a[c - done : c - done + tile, c - done :] = a_ref[c : c + tile, c:]
        if c > done:
            rest_a[c - done : c - done + tile, : c - done] = jnp.zeros((tile, c - done), jnp.float32)
    rest_rows[...] = rows_ref[:, done:]


def factor_rest_kernel(a_in, rows_in, upper_ref, tinv, y_ref, a_ref, rows_ref, work):
    a_ref[...] = a_in[...]
    rows_ref[...] = rows_in[...]
    factor_levels(a_ref, rows_ref, work, upper_ref, tinv, y_ref)


def factor_shapes(width, done, own):
    return [
        jax.ShapeDtypeStruct((done, width), jnp.float32),
        jax.ShapeDtypeStruct((done, tile), jnp.float32),
        jax.ShapeDtypeStruct((own, done), jnp.float32),
    ]


def factor_scratch(width, own):
    return [
        pltpu.VMEM((width, width), jnp.float32),
        pltpu.VMEM((own, width), jnp.float32),
        pltpu.VMEM((tile, 2 * tile), jnp.float32),
    ]


def factor_first(place, near, far, panel, done):
    own, width = panel.shape
    vmem = pl.BlockSpec(memory_space=pltpu.VMEM)
    return pl.pallas_call(
        factor_first_kernel,
        out_shape=factor_shapes(width, done, own)
        + [
            jax.ShapeDtypeStruct((width - done, width - done), jnp.float32),
            jax.ShapeDtypeStruct((own, width - done), jnp.float32),
        ],
        in_specs=[pl.BlockSpec(memory_space=pltpu.SMEM), vmem, vmem, vmem],
        out_specs=[vmem] * 5,
        scratch_shapes=factor_scratch(width, own),
        compiler_params=pltpu.CompilerParams(vmem_limit_bytes=16 * 1024 * 1024),
        cost_estimate=pl.CostEstimate(flops=10 * 10**9, bytes_accessed=4 * 10**6, transcendentals=0),
    )(place, near, far, panel)


def factor_rest(rest_a, rest_rows):
    own, width = rest_rows.shape
    vmem = pl.BlockSpec(memory_space=pltpu.VMEM)
    return pl.pallas_call(
        factor_rest_kernel,
        out_shape=factor_shapes(width, width, own),
        in_specs=[vmem, vmem],
        out_specs=[vmem] * 3,
        scratch_shapes=factor_scratch(width, own),
        compiler_params=pltpu.CompilerParams(vmem_limit_bytes=16 * 1024 * 1024),
        cost_estimate=pl.CostEstimate(flops=10 * 10**9, bytes_accessed=2 * 10**6, transcendentals=0),
    )(rest_a, rest_rows)


def back_kernel(place_ref, upper_a, tinv_a, y_a, upper_b, tinv_b, y_b, mixed_ref, r_ref, right):
    own, done = y_a.shape
    width = upper_a.shape[1]
    picked = r_ref.shape[0]
    start = pl.multiple_of(place_ref[1 + classes], picked)
    right[0:own, 0:done] = y_a[...]
    right[0:own, done:] = y_b[...]
    unit_row = lax.broadcasted_iota(jnp.int32, (picked, width), 0) + start
    unit_col = lax.broadcasted_iota(jnp.int32, (picked, width), 1)
    right[own:, :] = jnp.where(unit_row == unit_col, 1.0, 0.0).astype(jnp.float32)

    @pl.when(start < done)
    def _():
        r_ref[...] = upper_a[pl.ds(start, picked), :]

    @pl.when(start >= done)
    def _():
        r_ref[:, 0:done] = jnp.zeros((picked, done), jnp.float32)
        r_ref[:, done:] = upper_b[pl.ds(pl.multiple_of(start - done, picked), picked), :]

    solved = None
    for b in range(width - tile, -1, -tile):
        side = right[:, b : b + tile]
        low = b >= done
        if solved is not None:
            rest = upper_b[b - done : b - done + tile, b - done + tile :] if low else upper_a[b : b + tile, b + tile :]
            side = side - product(solved, rest, 1, 1)
        part = product(side, tinv_b[b - done : b - done + tile, :] if low else tinv_a[b : b + tile, :])
        mixed_ref[b // tile] = part
        solved = part if solved is None else jnp.concatenate([part, solved], 1)


def back(place, first, rest, picked):
    own, done = first[2].shape
    width = done + rest[2].shape[1]
    vmem = pl.BlockSpec(memory_space=pltpu.VMEM)
    return pl.pallas_call(
        back_kernel,
        out_shape=(
            jax.ShapeDtypeStruct((width // tile, own + picked, tile), jnp.float32),
            jax.ShapeDtypeStruct((picked, width), jnp.float32),
        ),
        in_specs=[pl.BlockSpec(memory_space=pltpu.SMEM)] + [vmem] * 6,
        out_specs=(vmem, vmem),
        scratch_shapes=[pltpu.VMEM((own + picked, width), jnp.float32)],
        compiler_params=pltpu.CompilerParams(vmem_limit_bytes=16 * 1024 * 1024),
        cost_estimate=pl.CostEstimate(flops=4 * 10**9, bytes_accessed=2 * 10**6, transcendentals=0),
    )(place, *first, *rest)


def finish_kernel(place_ref, mixed_ref, *refs):
    near, far = refs[:classes], refs[classes : 2 * classes]
    trail_ref, updated_ref, coupling_ref = refs[2 * classes :]
    own = trail_ref.shape[0]
    half = near[0].shape[0]
    core = place_ref[0]
    left = [mixed_ref[place_ref[1 + m]] for m in range(classes)]
    left = [jnp.concatenate(left[m : m + 2], 1) for m in range(0, classes, 2)]
    for c in range(0, half, tile):
        out = None
        for m in range(0, classes, 2):
            right = jnp.concatenate(
                [
                    jnp.concatenate([side[m][c : c + tile, :], side[m + 1][c : c + tile, :]], 0)
                    for side in (near, far)
                ],
                1,
            )
            term = product(left[m // 2], right)
            out = term if out is None else out + term
        for part, where in ((out[:, :tile], core), (out[:, tile:], 1 - core)):
            at = pl.ds(pl.multiple_of(where * half + c, tile), tile)
            updated_ref[:, at] = trail_ref[:, at] - part[:own]
            coupling_ref[:, at] = part[own:]


def finish(place, mixed, near, far, trailing):
    vmem = pl.BlockSpec(memory_space=pltpu.VMEM)
    own, trail = trailing.shape
    return pl.pallas_call(
        finish_kernel,
        out_shape=(
            jax.ShapeDtypeStruct((own, trail), jnp.float32),
            jax.ShapeDtypeStruct((mixed.shape[1] - own, trail), jnp.float32),
        ),
        in_specs=[pl.BlockSpec(memory_space=pltpu.SMEM)] + [vmem] * (2 + 2 * classes),
        out_specs=(vmem, vmem),
        compiler_params=pltpu.CompilerParams(vmem_limit_bytes=32 * 1024 * 1024),
    )(place, mixed, *near, *far, trailing)


def kind_of(x, y, z):
    return (x % 2) ^ (2 * (y % 2)) ^ (3 * (z % 2))


def local(panel, trailing, counts):
    own, width = panel.shape
    half = trailing.shape[1] // 2
    depth = lax.axis_size("z")
    groups = lax.axis_size("grp")
    side = 4
    members = 2 * depth
    chip_count = groups * depth
    chunk = half // chip_count
    gram_chunk = len(gram_blocks[0]) * tile // chip_count
    kinds = [kind_of(g % side, g // side, z) for g in range(groups) for z in range(depth)]
    group, z, core = lax.axis_index("grp"), lax.axis_index("z"), lax.axis_index("core")
    kind = kind_of(group % side, group // side, z)
    picked = width // members
    start = (z * 2 + core) * picked
    place = jnp.stack([core] + [kind ^ m for m in range(classes)] + [start]).astype(jnp.int32)
    swap = [(0, 1), (1, 0)]
    count_row = counts[None, :]
    sent_trail = lax.dynamic_slice_in_dim(trailing, (1 - core) * half, half, 1)
    with jax.named_scope("swap_inputs"):
        far_counts = lax.ppermute(count_row, "core", swap)
        other_panel = lax.ppermute(panel, "core", swap)
        far_trail = lax.ppermute(sent_trail, "core", swap)
    with jax.named_scope("local_products"):
        *terms, gram_terms = products(
            place, panel, other_panel, trailing, far_trail, count_row, far_counts, own * groups * members
        )
    along = (
        ("along_x", "grp", [(i, i ^ 1) for i in range(groups)]),
        ("along_y", "grp", [(i, i ^ side) for i in range(groups)]),
        ("along_z", "z", [(i, i ^ 1) for i in range(depth)]),
    )

    def exchange(rows):
        with jax.named_scope("exchange"):
            rows = lax.all_to_all(rows.reshape(chip_count, 1, -1), chips, 0, 0, tiled=True)
        return rows.reshape(-1, tile)

    parts = [terms[0]]
    for m, (name, axis, pairs) in enumerate(along):
        with jax.named_scope("terms_" + name):
            parts.append(lax.ppermute(terms[1 + m], axis, pairs))
    gram_pieces = exchange(gram_terms)
    with jax.named_scope("combine_terms"):
        both = combine(gram_pieces, parts, chip_count)
    both = exchange(both)
    with jax.named_scope("unpack_sums"):
        near_gram, copies = unpack(both, gram_chunk, chunk, kinds)
    with jax.named_scope("swap_gram"):
        far_gram = lax.ppermute(near_gram, "core", swap)
    quarter = exchange(copies)
    with jax.named_scope("factor_first"):
        *first, rest_a, rest_rows = factor_first(place, near_gram, far_gram, panel, width // 2)
    quarter, rest_a, rest_rows = lax.optimization_barrier((quarter, rest_a, rest_rows))
    near = []
    for name, axis, pairs in along:
        with jax.named_scope("quarters_" + name):
            near.append(lax.ppermute(quarter, axis, pairs))
    with jax.named_scope("swap_quarter"):
        far = [lax.ppermute(quarter, "core", swap)]
    with jax.named_scope("factor_rest"):
        rest = list(factor_rest(rest_a, rest_rows))
    *near, rest[1] = lax.optimization_barrier((*near, rest[1]))
    with jax.named_scope("swap_quarters"):
        far += [lax.ppermute(part, "core", swap) for part in near]
    near = [quarter, *near]
    with jax.named_scope("back_substitute"):
        mixed, r_rows = back(place, first, rest, picked)
    with jax.named_scope("apply_factor"):
        updated, coupling = finish(place, mixed, near, far, trailing)
    return (r_rows, coupling, updated)


def solution(mesh):
    groups, members = mesh.devices.shape
    split = Mesh(mesh.devices.reshape(groups, members // 2, 2), ("grp", "z", "core"))
    rows = P(("grp", "z", "core"))
    return jax.shard_map(
        local,
        mesh=split,
        in_specs=(P(("grp", "z", "core"), None), P(("grp", "z", "core"), None), rows),
        out_specs=(P(("z", "core"), None), P(("z", "core"), None), P(("grp", "z", "core"), None)),
        check_vma=False,
    )
```

```python
import functools

import jax
import jax.numpy as jnp
from jax import lax
from jax.experimental import pallas as pl
from jax.experimental.pallas import tpu as pltpu
from jax.sharding import Mesh, PartitionSpec as P

ridge_shift = 0.05
HIGHEST = lax.Precision.HIGHEST
tile = 128
strip = 32
chips = ("grp", "z")
classes = 4


def product(left, right, left_dim=1, right_dim=0):
    return lax.dot_general(
        left,
        right,
        (((left_dim,), (right_dim,)), ((), ())),
        precision=HIGHEST,
        preferred_element_type=jnp.float32,
    )


def factor_diagonal(work):
    sub = lax.broadcasted_iota(jnp.int32, (8, tile), 0)
    groups = strip // 8

    def spread_row(array, row):
        return jnp.broadcast_to(array[row : row + 1, :], (8, tile))

    for r in range(0, tile, strip):
        left = [work[r + 8 * g : r + 8 * g + 8, 0:tile] for g in range(groups)]
        right = [work[r + 8 * g : r + 8 * g + 8, tile : 2 * tile] for g in range(groups)]
        col = {}
        for c in range(strip):
            for g in range(c // 8, groups):
                col[c, g] = jnp.broadcast_to(left[g][:, r + c : r + c + 1], (8, tile))
        for k in range(strip):
            at, row = k // 8, k % 8
            inv = lax.rsqrt(spread_row(col[k, at], row))
            low = {g: col[k, g] * inv for g in range(at, groups)}
            for c in range(k + 1, strip):
                factor_c = spread_row(low[c // 8], c % 8)
                for g in range(c // 8, groups):
                    col[c, g] = col[c, g] - low[g] * factor_c
            below = jnp.where(sub > row, low[at], 0.0)
            for side in (left, right):
                pivot = spread_row(side[at], row) * inv
                side[at] = jnp.where(sub == row, pivot, side[at] - below * pivot)
                for g in range(at + 1, groups):
                    side[g] = side[g] - low[g] * pivot
        new_left = jnp.concatenate(left, 0)
        new_right = jnp.concatenate(right, 0)
        work[r : r + strip, 0:tile] = new_left
        work[r : r + strip, tile : 2 * tile] = new_right
        if r + strip < tile:
            update = product(new_left, jnp.concatenate([new_left, new_right], 1), 0, 0)
            work[r + strip : tile, :] = work[r + strip : tile, :] - update[r + strip : tile, :]


gram_blocks = (((0, 0), (1, 1), (0, 1), (0, 2), (0, 3)), ((2, 2), (3, 3), (2, 3), (1, 2), (1, 3)))


def products_kernel(place_ref, panel_ref, other_ref, trail_ref, far_ref, counts_ref, far_counts_ref, *refs, total_rows):
    outs, gram, (pt, wp, wt, quarters) = refs[:classes], refs[classes], refs[classes + 1 :]
    core = place_ref[0]
    own, width = panel_ref.shape
    half = trail_ref.shape[1]
    for at, rows, trail, count in ((0, panel_ref, trail_ref, counts_ref), (own, other_ref, far_ref, far_counts_ref)):
        weight = jnp.transpose(jnp.broadcast_to(count[...].astype(jnp.float32) / total_rows, (own, own)))
        for c in range(0, width, tile):
            block = rows[:, c : c + tile]
            pt[c : c + tile, at : at + own] = jnp.transpose(block)
            wp[at : at + own, c : c + tile] = block * weight
        for c in range(0, half, tile):
            wt[at : at + own, c : c + tile] = trail[:, c : c + tile] * weight
    step = 2 * tile
    for c in range(0, half, step):
        n = min(step, half - c)
        part = product(pt[...], wt[:, c : c + n])
        for k in range(classes):
            for j in range(0, n, tile):
                quarters[k, c + j : c + j + tile, :] = part[k * tile : (k + 1) * tile, j : j + tile]
    for m in range(classes):
        outs[m][...] = quarters[place_ref[1 + m]]
    near = pl.multiple_of(core * step, tile)
    first = product(pt[pl.ds(near, tile), :], wp[:, pl.ds(near, step)])
    gram[0:tile, :] = first[:, :tile]
    gram[2 * tile : 3 * tile, :] = first[:, tile:]
    near = pl.multiple_of(core * step + tile, tile)
    gram[tile : 2 * tile, :] = product(pt[pl.ds(near, tile), :], wp[:, pl.ds(near, tile)])
    near = pl.multiple_of(core * tile, tile)
    last = product(pt[pl.ds(near, tile), :], wp[:, step:])
    gram[3 * tile : 4 * tile, :] = last[:, :tile]
    gram[4 * tile :, :] = last[:, tile:]


def products(place, panel, other, trailing, far, counts, far_counts, total_rows):
    own, width = panel.shape
    half = far.shape[1]
    gram_rows = len(gram_blocks[0]) * tile
    whole = lambda shape: pl.BlockSpec(shape, lambda i, place: (0, 0))
    return pl.pallas_call(
        functools.partial(products_kernel, total_rows=total_rows),
        out_shape=[jax.ShapeDtypeStruct((half, tile), jnp.float32)] * classes
        + [jax.ShapeDtypeStruct((gram_rows, tile), jnp.float32)],
        grid_spec=pltpu.PrefetchScalarGridSpec(
            num_scalar_prefetch=1,
            grid=(1,),
            in_specs=[
                whole((own, width)),
                whole((own, width)),
                pl.BlockSpec((own, half), lambda i, place: (0, place[0])),
                whole((own, half)),
                whole((1, own)),
                whole((1, own)),
            ],
            out_specs=[whole((half, tile))] * classes + [whole((gram_rows, tile))],
            scratch_shapes=[
                pltpu.VMEM((width, 2 * own), jnp.float32),
                pltpu.VMEM((2 * own, width), jnp.float32),
                pltpu.VMEM((2 * own, half), jnp.float32),
                pltpu.VMEM((classes, half, tile), jnp.float32),
            ],
        ),
        compiler_params=pltpu.CompilerParams(vmem_limit_bytes=32 * 1024 * 1024),
    )(place, panel, other, trailing, far, counts, far_counts)


def combine_kernel(gram_ref, *refs, chip_count):
    parts, out_ref = refs[:classes], refs[classes]
    size = gram_ref.shape[0] // chip_count
    chunk = parts[0].shape[0] // chip_count
    for q in range(chip_count):
        side = slice(q * chunk, (q + 1) * chunk)
        cross = (parts[0][side, :] + parts[1][side, :]) + (parts[2][side, :] + parts[3][side, :])
        gram = gram_ref[q * size : (q + 1) * size, :]
        out_ref[q * (size + chunk) : (q + 1) * (size + chunk), :] = jnp.concatenate([gram, cross], 0)


def combine(gram, parts, chip_count):
    vmem = pl.BlockSpec(memory_space=pltpu.VMEM)
    return pl.pallas_call(
        functools.partial(combine_kernel, chip_count=chip_count),
        out_shape=jax.ShapeDtypeStruct((gram.shape[0] + parts[0].shape[0], tile), jnp.float32),
        in_specs=[vmem] * (1 + classes),
        out_specs=vmem,
        compiler_params=pltpu.CompilerParams(vmem_limit_bytes=16 * 1024 * 1024),
    )(gram, *parts)


def sum_kernel(pieces_ref, copies_ref, *, size, kinds):
    both = pieces_ref.shape[0] // len(kinds)
    totals = []
    for k in range(classes):
        total = None
        for q, kind in enumerate(kinds):
            if kind == k:
                piece = pieces_ref[q * both : (q + 1) * both, :]
                total = piece if total is None else total + piece
        totals.append(total)
    gram = (totals[0] + totals[1]) + (totals[2] + totals[3])
    is_gram = lax.broadcasted_iota(jnp.int32, (both, tile), 0) < size
    for k in range(classes):
        copy = jnp.where(is_gram, gram, totals[k])
        for q, kind in enumerate(kinds):
            if kind == k:
                copies_ref[q * both : (q + 1) * both, :] = copy


def sum_pieces(pieces, size, kinds):
    vmem = pl.BlockSpec(memory_space=pltpu.VMEM)
    return pl.pallas_call(
        functools.partial(sum_kernel, size=size, kinds=kinds),
        out_shape=jax.ShapeDtypeStruct(pieces.shape, jnp.float32),
        in_specs=[vmem],
        out_specs=vmem,
        compiler_params=pltpu.CompilerParams(vmem_limit_bytes=16 * 1024 * 1024),
    )(pieces)


def unpack_kernel(copies_ref, gram_ref, quarter_ref, *, chip_count):
    size = gram_ref.shape[0] // chip_count
    chunk = quarter_ref.shape[0] // chip_count
    both = size + chunk
    for q in range(chip_count):
        gram_ref[q * size : (q + 1) * size, :] = copies_ref[q * both : q * both + size, :]
        quarter_ref[q * chunk : (q + 1) * chunk, :] = copies_ref[q * both + size : (q + 1) * both, :]


def unpack(copies, chip_count, size, chunk):
    vmem = pl.BlockSpec(memory_space=pltpu.VMEM)
    return pl.pallas_call(
        functools.partial(unpack_kernel, chip_count=chip_count),
        out_shape=(
            jax.ShapeDtypeStruct((chip_count * size, tile), jnp.float32),
            jax.ShapeDtypeStruct((chip_count * chunk, tile), jnp.float32),
        ),
        in_specs=[vmem],
        out_specs=(vmem, vmem),
        compiler_params=pltpu.CompilerParams(vmem_limit_bytes=16 * 1024 * 1024),
    )(copies)


def factor_levels(a_ref, rows_ref, work, upper_ref, tinv, y_ref):
    rows = lax.broadcasted_iota(jnp.int32, (tile, tile), 0)
    cols = lax.broadcasted_iota(jnp.int32, (tile, tile), 1)
    eye = jnp.where(rows == cols, 1.0, 0.0).astype(jnp.float32)
    width = a_ref.shape[0]
    levels = tinv.shape[0] // tile
    upper_ref[...] = jnp.zeros_like(upper_ref)

    def load(b):
        work[:, 0:tile] = a_ref[b : b + tile, b : b + tile]
        work[:, tile:] = eye

    def spread(b):
        e = b + tile
        inverse = work[:, tile:]
        tinv[b:e, :] = inverse
        upper_ref[b:e, b:e] = jnp.where(cols >= rows, work[:, 0:tile], 0.0)
        y = product(rows_ref[:, b:e], inverse, 1, 1)
        y_ref[:, b:e] = y
        if e < width:
            u = product(inverse, a_ref[b:e, e:])
            upper_ref[b:e, e:] = u
            for c in range(e, width, tile):
                a_ref[c : c + tile, c:] = a_ref[c : c + tile, c:] - product(
                    u[:, c - e : c - e + tile], u[:, c - e :], 0, 0
                )
            rows_ref[:, e:] = rows_ref[:, e:] - product(y, u)

    def level(step, carry):
        for i in range(levels):
            pl.when(step == i)(lambda i=i: load(i * tile))
        factor_diagonal(work)
        for i in range(levels):
            pl.when(step == i)(lambda i=i: spread(i * tile))
        return carry

    lax.fori_loop(0, levels, level, 0)


def factor_first_kernel(place_ref, near_ref, far_ref, panel_ref, upper_ref, tinv, y_ref, rest_a, rest_rows, a_ref, rows_ref, work):
    rows = lax.broadcasted_iota(jnp.int32, (tile, tile), 0)
    cols = lax.broadcasted_iota(jnp.int32, (tile, tile), 1)
    shift = jnp.where(rows == cols, ridge_shift, 0.0).astype(jnp.float32)
    for core, blocks in enumerate(gram_blocks):
        for at, (i, j) in enumerate(blocks):
            side = slice(at * tile, (at + 1) * tile)
            block = jnp.where(place_ref[0] == core, near_ref[side, :], far_ref[side, :])
            if i == j:
                block = block + shift
            a_ref[i * tile : (i + 1) * tile, j * tile : (j + 1) * tile] = block
    rows_ref[...] = panel_ref[...]
    factor_levels(a_ref, rows_ref, work, upper_ref, tinv, y_ref)
    done = tinv.shape[0]
    for c in range(done, a_ref.shape[0], tile):
        rest_a[c - done : c - done + tile, c - done :] = a_ref[c : c + tile, c:]
        if c > done:
            rest_a[c - done : c - done + tile, : c - done] = jnp.zeros((tile, c - done), jnp.float32)
    rest_rows[...] = rows_ref[:, done:]


def factor_rest_kernel(a_in, rows_in, upper_ref, tinv, y_ref, a_ref, rows_ref, work):
    a_ref[...] = a_in[...]
    rows_ref[...] = rows_in[...]
    factor_levels(a_ref, rows_ref, work, upper_ref, tinv, y_ref)


def factor_shapes(width, done, own):
    return [
        jax.ShapeDtypeStruct((done, width), jnp.float32),
        jax.ShapeDtypeStruct((done, tile), jnp.float32),
        jax.ShapeDtypeStruct((own, done), jnp.float32),
    ]


def factor_scratch(width, own):
    return [
        pltpu.VMEM((width, width), jnp.float32),
        pltpu.VMEM((own, width), jnp.float32),
        pltpu.VMEM((tile, 2 * tile), jnp.float32),
    ]


def factor_first(place, near, far, panel, done):
    own, width = panel.shape
    vmem = pl.BlockSpec(memory_space=pltpu.VMEM)
    return pl.pallas_call(
        factor_first_kernel,
        out_shape=factor_shapes(width, done, own)
        + [
            jax.ShapeDtypeStruct((width - done, width - done), jnp.float32),
            jax.ShapeDtypeStruct((own, width - done), jnp.float32),
        ],
        in_specs=[pl.BlockSpec(memory_space=pltpu.SMEM), vmem, vmem, vmem],
        out_specs=[vmem] * 5,
        scratch_shapes=factor_scratch(width, own),
        compiler_params=pltpu.CompilerParams(vmem_limit_bytes=16 * 1024 * 1024),
        cost_estimate=pl.CostEstimate(flops=10 * 10**9, bytes_accessed=4 * 10**6, transcendentals=0),
    )(place, near, far, panel)


def factor_rest(rest_a, rest_rows):
    own, width = rest_rows.shape
    vmem = pl.BlockSpec(memory_space=pltpu.VMEM)
    return pl.pallas_call(
        factor_rest_kernel,
        out_shape=factor_shapes(width, width, own),
        in_specs=[vmem, vmem],
        out_specs=[vmem] * 3,
        scratch_shapes=factor_scratch(width, own),
        compiler_params=pltpu.CompilerParams(vmem_limit_bytes=16 * 1024 * 1024),
        cost_estimate=pl.CostEstimate(flops=10 * 10**9, bytes_accessed=2 * 10**6, transcendentals=0),
    )(rest_a, rest_rows)


def back_kernel(place_ref, upper_a, tinv_a, y_a, upper_b, tinv_b, y_b, mixed_ref, r_ref, right):
    own, done = y_a.shape
    width = upper_a.shape[1]
    picked = r_ref.shape[0]
    start = pl.multiple_of(place_ref[1 + classes], picked)
    right[0:own, 0:done] = y_a[...]
    right[0:own, done:] = y_b[...]
    unit_row = lax.broadcasted_iota(jnp.int32, (picked, width), 0) + start
    unit_col = lax.broadcasted_iota(jnp.int32, (picked, width), 1)
    right[own:, :] = jnp.where(unit_row == unit_col, 1.0, 0.0).astype(jnp.float32)

    @pl.when(start < done)
    def _():
        r_ref[...] = upper_a[pl.ds(start, picked), :]

    @pl.when(start >= done)
    def _():
        r_ref[:, 0:done] = jnp.zeros((picked, done), jnp.float32)
        r_ref[:, done:] = upper_b[pl.ds(pl.multiple_of(start - done, picked), picked), :]

    solved = None
    for b in range(width - tile, -1, -tile):
        side = right[:, b : b + tile]
        low = b >= done
        if solved is not None:
            rest = upper_b[b - done : b - done + tile, b - done + tile :] if low else upper_a[b : b + tile, b + tile :]
            side = side - product(solved, rest, 1, 1)
        part = product(side, tinv_b[b - done : b - done + tile, :] if low else tinv_a[b : b + tile, :])
        mixed_ref[b // tile] = part
        solved = part if solved is None else jnp.concatenate([part, solved], 1)


def back(place, first, rest, picked):
    own, done = first[2].shape
    width = done + rest[2].shape[1]
    vmem = pl.BlockSpec(memory_space=pltpu.VMEM)
    return pl.pallas_call(
        back_kernel,
        out_shape=(
            jax.ShapeDtypeStruct((width // tile, own + picked, tile), jnp.float32),
            jax.ShapeDtypeStruct((picked, width), jnp.float32),
        ),
        in_specs=[pl.BlockSpec(memory_space=pltpu.SMEM)] + [vmem] * 6,
        out_specs=(vmem, vmem),
        scratch_shapes=[pltpu.VMEM((own + picked, width), jnp.float32)],
        compiler_params=pltpu.CompilerParams(vmem_limit_bytes=16 * 1024 * 1024),
        cost_estimate=pl.CostEstimate(flops=4 * 10**9, bytes_accessed=2 * 10**6, transcendentals=0),
    )(place, *first, *rest)


def finish_kernel(place_ref, mixed_ref, *refs):
    near, far = refs[:classes], refs[classes : 2 * classes]
    trail_ref, updated_ref, coupling_ref = refs[2 * classes :]
    own = trail_ref.shape[0]
    half = near[0].shape[0]
    core = place_ref[0]
    left = [mixed_ref[place_ref[1 + m]] for m in range(classes)]
    left = [jnp.concatenate(left[m : m + 2], 1) for m in range(0, classes, 2)]
    for c in range(0, half, tile):
        out = None
        for m in range(0, classes, 2):
            right = jnp.concatenate(
                [
                    jnp.concatenate([side[m][c : c + tile, :], side[m + 1][c : c + tile, :]], 0)
                    for side in (near, far)
                ],
                1,
            )
            term = product(left[m // 2], right)
            out = term if out is None else out + term
        for part, where in ((out[:, :tile], core), (out[:, tile:], 1 - core)):
            at = pl.ds(pl.multiple_of(where * half + c, tile), tile)
            updated_ref[:, at] = trail_ref[:, at] - part[:own]
            coupling_ref[:, at] = part[own:]


def finish(place, mixed, near, far, trailing):
    vmem = pl.BlockSpec(memory_space=pltpu.VMEM)
    own, trail = trailing.shape
    return pl.pallas_call(
        finish_kernel,
        out_shape=(
            jax.ShapeDtypeStruct((own, trail), jnp.float32),
            jax.ShapeDtypeStruct((mixed.shape[1] - own, trail), jnp.float32),
        ),
        in_specs=[pl.BlockSpec(memory_space=pltpu.SMEM)] + [vmem] * (2 + 2 * classes),
        out_specs=(vmem, vmem),
        compiler_params=pltpu.CompilerParams(vmem_limit_bytes=32 * 1024 * 1024),
    )(place, mixed, *near, *far, trailing)


def kind_of(x, y, z):
    return (x % 2) ^ (2 * (y % 2)) ^ (3 * (z % 2))


def local(panel, trailing, counts):
    own, width = panel.shape
    half = trailing.shape[1] // 2
    depth = lax.axis_size("z")
    groups = lax.axis_size("grp")
    side = 4
    members = 2 * depth
    chip_count = groups * depth
    chunk = half // chip_count
    gram_chunk = len(gram_blocks[0]) * tile // chip_count
    kinds = [kind_of(g % side, g // side, z) for g in range(groups) for z in range(depth)]
    group, z, core = lax.axis_index("grp"), lax.axis_index("z"), lax.axis_index("core")
    kind = kind_of(group % side, group // side, z)
    picked = width // members
    start = (z * 2 + core) * picked
    place = jnp.stack([core] + [kind ^ m for m in range(classes)] + [start]).astype(jnp.int32)
    swap = [(0, 1), (1, 0)]
    count_row = counts[None, :]
    sent_trail = lax.dynamic_slice_in_dim(trailing, (1 - core) * half, half, 1)
    with jax.named_scope("swap_inputs"):
        far_counts = lax.ppermute(count_row, "core", swap)
        other_panel = lax.ppermute(panel, "core", swap)
        far_trail = lax.ppermute(sent_trail, "core", swap)
    with jax.named_scope("local_products"):
        *terms, gram_terms = products(
            place, panel, other_panel, trailing, far_trail, count_row, far_counts, own * groups * members
        )
    line = [(i * 2 + c, (i ^ (3 if c else 1)) * 2 + c) for i in range(side) for c in range(2)]
    across = [
        ((i * side + j) * 2 + c, ((i ^ (3 if c else 1)) * side + j) * 2 + c)
        for i in range(groups // side)
        for j in range(side)
        for c in range(2)
    ]
    inner = [
        ((j * side + i) * 2 + c, (j * side + (i ^ (3 if c else 1))) * 2 + c)
        for i in range(side)
        for j in range(groups // side)
        for c in range(2)
    ]
    along = (
        ("along_x", ("grp", "core"), inner),
        ("along_y", ("grp", "core"), across),
        ("along_z", ("z", "core"), line),
    )

    def exchange(rows):
        with jax.named_scope("exchange"):
            rows = lax.all_to_all(rows.reshape(chip_count, 1, -1), chips, 0, 0, tiled=True)
        return rows.reshape(-1, tile)

    parts = [terms[0]]
    for m, (name, axis, pairs) in enumerate(along):
        with jax.named_scope("terms_" + name):
            parts.append(lax.ppermute(terms[1 + m], axis, pairs))
    with jax.named_scope("combine_terms"):
        pieces = combine(gram_terms, parts, chip_count)
    pieces = exchange(pieces)
    with jax.named_scope("sum_pieces"):
        copies = sum_pieces(pieces, gram_chunk, kinds)
    copies = exchange(copies)
    with jax.named_scope("unpack_sums"):
        near_gram, quarter = unpack(copies, chip_count, gram_chunk, chunk)
    with jax.named_scope("swap_gram"):
        far_gram = lax.ppermute(near_gram, "core", swap)
    near = []
    for name, axis, pairs in along:
        with jax.named_scope("quarters_" + name):
            near.append(lax.ppermute(quarter, axis, pairs))
    with jax.named_scope("swap_quarter"):
        far = [lax.ppermute(quarter, "core", swap)]
    with jax.named_scope("factor_first"):
        *first, rest_a, rest_rows = factor_first(place, near_gram, far_gram, panel, width // 2)
    *near, rest_a, rest_rows = lax.optimization_barrier((*near, rest_a, rest_rows))
    with jax.named_scope("swap_quarters"):
        far += [lax.ppermute(part, "core", swap) for part in near]
    near = [quarter, *near]
    with jax.named_scope("factor_rest"):
        rest = factor_rest(rest_a, rest_rows)
    with jax.named_scope("back_substitute"):
        mixed, r_rows = back(place, first, rest, picked)
    with jax.named_scope("apply_factor"):
        updated, coupling = finish(place, mixed, near, far, trailing)
    return (r_rows, coupling, updated)


def solution(mesh):
    groups, members = mesh.devices.shape
    split = Mesh(mesh.devices.reshape(groups, members // 2, 2), ("grp", "z", "core"))
    rows = P(("grp", "z", "core"))
    return jax.shard_map(
        local,
        mesh=split,
        in_specs=(P(("grp", "z", "core"), None), P(("grp", "z", "core"), None), rows),
        out_specs=(P(("z", "core"), None), P(("z", "core"), None), P(("grp", "z", "core"), None)),
        check_vma=False,
    )
```

```python
import functools

import jax
import jax.numpy as jnp
from jax import lax
from jax.experimental import pallas as pl
from jax.experimental.pallas import tpu as pltpu
from jax.sharding import Mesh, PartitionSpec as P

ridge_shift = 0.05
HIGHEST = lax.Precision.HIGHEST
tile = 128
strip = 32
chips = ("grp", "z")
classes = 4


def product(left, right, left_dim=1, right_dim=0):
    return lax.dot_general(
        left,
        right,
        (((left_dim,), (right_dim,)), ((), ())),
        precision=HIGHEST,
        preferred_element_type=jnp.float32,
    )


def three_parts(x):
    high = x.astype(jnp.bfloat16)
    rest = x - high.astype(jnp.float32)
    middle = rest.astype(jnp.bfloat16)
    return high, middle, (rest - middle.astype(jnp.float32)).astype(jnp.bfloat16)


def stacked(left, right, left_dim=1, right_dim=0):
    lh, lm, ll = three_parts(left)
    rh, rm, rl = three_parts(right)
    return lax.dot_general(
        jnp.concatenate([lh, lh, lm, lh, ll, lm], left_dim),
        jnp.concatenate([rh, rm, rh, rl, rh, rm], right_dim),
        (((left_dim,), (right_dim,)), ((), ())),
        preferred_element_type=jnp.float32,
    )


def factor_diagonal(work, later):
    sub = lax.broadcasted_iota(jnp.int32, (8, tile), 0)
    groups = strip // 8

    def spread_row(array, row):
        return jnp.broadcast_to(array[row : row + 1, :], (8, tile))

    for r in range(0, tile, strip):
        left = [work[r + 8 * g : r + 8 * g + 8, 0:tile] for g in range(groups)]
        right = [work[r + 8 * g : r + 8 * g + 8, tile : 2 * tile] for g in range(groups)]
        if later:
            later.pop(0)()
        col = {}
        for c in range(strip):
            for g in range(c // 8, groups):
                col[c, g] = jnp.broadcast_to(left[g][:, r + c : r + c + 1], (8, tile))
        for k in range(strip):
            at, row = k // 8, k % 8
            inv = lax.rsqrt(spread_row(col[k, at], row))
            low = {g: col[k, g] * inv for g in range(at, groups)}
            for c in range(k + 1, strip):
                factor_c = spread_row(low[c // 8], c % 8)
                for g in range(c // 8, groups):
                    col[c, g] = col[c, g] - low[g] * factor_c
            below = jnp.where(sub > row, low[at], 0.0)
            for side in (left, right):
                pivot = spread_row(side[at], row) * inv
                side[at] = jnp.where(sub == row, pivot, side[at] - below * pivot)
                for g in range(at + 1, groups):
                    side[g] = side[g] - low[g] * pivot
        new_left = jnp.concatenate(left, 0)
        new_right = jnp.concatenate(right, 0)
        work[r : r + strip, 0:tile] = new_left
        work[r : r + strip, tile : 2 * tile] = new_right
        if r + strip < tile:
            update = stacked(new_left, jnp.concatenate([new_left, new_right], 1), 0, 0)
            work[r + strip : tile, :] = work[r + strip : tile, :] - update[r + strip : tile, :]


gram_blocks = (((0, 0), (1, 1), (0, 1), (0, 2), (0, 3)), ((2, 2), (3, 3), (2, 3), (1, 2), (1, 3)))


def products_kernel(place_ref, panel_ref, other_ref, trail_ref, far_ref, counts_ref, far_counts_ref, *refs, total_rows):
    outs, gram, (pt, wp, wt, quarters) = refs[:classes], refs[classes], refs[classes + 1 :]
    core = place_ref[0]
    own, width = panel_ref.shape
    half = trail_ref.shape[1]
    for at, rows, trail, count in ((0, panel_ref, trail_ref, counts_ref), (own, other_ref, far_ref, far_counts_ref)):
        weight = jnp.transpose(jnp.broadcast_to(count[...].astype(jnp.float32) / total_rows, (own, own)))
        for c in range(0, width, tile):
            block = rows[:, c : c + tile]
            pt[c : c + tile, at : at + own] = jnp.transpose(block)
            wp[at : at + own, c : c + tile] = block * weight
        for c in range(0, half, tile):
            wt[at : at + own, c : c + tile] = trail[:, c : c + tile] * weight
    step = 2 * tile
    for c in range(0, half, step):
        n = min(step, half - c)
        part = product(pt[...], wt[:, c : c + n])
        for k in range(classes):
            for j in range(0, n, tile):
                quarters[k, c + j : c + j + tile, :] = part[k * tile : (k + 1) * tile, j : j + tile]
    for m in range(classes):
        outs[m][...] = quarters[place_ref[1 + m]]
    near = pl.multiple_of(core * step, tile)
    first = product(pt[pl.ds(near, tile), :], wp[:, pl.ds(near, step)])
    gram[0:tile, :] = first[:, :tile]
    gram[2 * tile : 3 * tile, :] = first[:, tile:]
    near = pl.multiple_of(core * step + tile, tile)
    gram[tile : 2 * tile, :] = product(pt[pl.ds(near, tile), :], wp[:, pl.ds(near, tile)])
    near = pl.multiple_of(core * tile, tile)
    last = product(pt[pl.ds(near, tile), :], wp[:, step:])
    gram[3 * tile : 4 * tile, :] = last[:, :tile]
    gram[4 * tile :, :] = last[:, tile:]


def products(place, panel, other, trailing, far, counts, far_counts, total_rows):
    own, width = panel.shape
    half = far.shape[1]
    gram_rows = len(gram_blocks[0]) * tile
    whole = lambda shape: pl.BlockSpec(shape, lambda i, place: (0, 0))
    return pl.pallas_call(
        functools.partial(products_kernel, total_rows=total_rows),
        out_shape=[jax.ShapeDtypeStruct((half, tile), jnp.float32)] * classes
        + [jax.ShapeDtypeStruct((gram_rows, tile), jnp.float32)],
        grid_spec=pltpu.PrefetchScalarGridSpec(
            num_scalar_prefetch=1,
            grid=(1,),
            in_specs=[
                whole((own, width)),
                whole((own, width)),
                pl.BlockSpec((own, half), lambda i, place: (0, place[0])),
                whole((own, half)),
                whole((1, own)),
                whole((1, own)),
            ],
            out_specs=[whole((half, tile))] * classes + [whole((gram_rows, tile))],
            scratch_shapes=[
                pltpu.VMEM((width, 2 * own), jnp.float32),
                pltpu.VMEM((2 * own, width), jnp.float32),
                pltpu.VMEM((2 * own, half), jnp.float32),
                pltpu.VMEM((classes, half, tile), jnp.float32),
            ],
        ),
        compiler_params=pltpu.CompilerParams(vmem_limit_bytes=32 * 1024 * 1024),
    )(place, panel, other, trailing, far, counts, far_counts)


def combine_kernel(gram_ref, *refs, chip_count):
    parts, out_ref = refs[:classes], refs[classes]
    size = gram_ref.shape[0] // chip_count
    chunk = parts[0].shape[0] // chip_count
    for q in range(chip_count):
        side = slice(q * chunk, (q + 1) * chunk)
        cross = (parts[0][side, :] + parts[1][side, :]) + (parts[2][side, :] + parts[3][side, :])
        gram = gram_ref[q * size : (q + 1) * size, :]
        out_ref[q * (size + chunk) : (q + 1) * (size + chunk), :] = jnp.concatenate([gram, cross], 0)


def combine(gram, parts, chip_count):
    vmem = pl.BlockSpec(memory_space=pltpu.VMEM)
    return pl.pallas_call(
        functools.partial(combine_kernel, chip_count=chip_count),
        out_shape=jax.ShapeDtypeStruct((gram.shape[0] + parts[0].shape[0], tile), jnp.float32),
        in_specs=[vmem] * (1 + classes),
        out_specs=vmem,
        compiler_params=pltpu.CompilerParams(vmem_limit_bytes=16 * 1024 * 1024),
    )(gram, *parts)


def sum_kernel(pieces_ref, copies_ref, *, size, kinds):
    both = pieces_ref.shape[0] // len(kinds)
    totals = []
    for k in range(classes):
        total = None
        for q, kind in enumerate(kinds):
            if kind == k:
                piece = pieces_ref[q * both : (q + 1) * both, :]
                total = piece if total is None else total + piece
        totals.append(total)
    gram = (totals[0] + totals[1]) + (totals[2] + totals[3])
    is_gram = lax.broadcasted_iota(jnp.int32, (both, tile), 0) < size
    for k in range(classes):
        copy = jnp.where(is_gram, gram, totals[k])
        for q, kind in enumerate(kinds):
            if kind == k:
                copies_ref[q * both : (q + 1) * both, :] = copy


def sum_pieces(pieces, size, kinds):
    vmem = pl.BlockSpec(memory_space=pltpu.VMEM)
    return pl.pallas_call(
        functools.partial(sum_kernel, size=size, kinds=kinds),
        out_shape=jax.ShapeDtypeStruct(pieces.shape, jnp.float32),
        in_specs=[vmem],
        out_specs=vmem,
        compiler_params=pltpu.CompilerParams(vmem_limit_bytes=16 * 1024 * 1024),
    )(pieces)


def unpack_kernel(near_ref, far_ref, near_gram, far_gram, quarters_ref, *, chip_count):
    size = near_gram.shape[0] // chip_count
    chunk = quarters_ref.shape[1] // chip_count
    both = size + chunk
    for at, (copies_ref, gram_ref) in enumerate(((near_ref, near_gram), (far_ref, far_gram))):
        for q in range(chip_count):
            gram_ref[q * size : (q + 1) * size, :] = copies_ref[q * both : q * both + size, :]
            quarters_ref[at, q * chunk : (q + 1) * chunk, :] = copies_ref[q * both + size : (q + 1) * both, :]


def unpack(near, far, chip_count, size, chunk):
    vmem = pl.BlockSpec(memory_space=pltpu.VMEM)
    gram = jax.ShapeDtypeStruct((chip_count * size, tile), jnp.float32)
    return pl.pallas_call(
        functools.partial(unpack_kernel, chip_count=chip_count),
        out_shape=(gram, gram, jax.ShapeDtypeStruct((2, chip_count * chunk, tile), jnp.float32)),
        in_specs=[vmem] * 2,
        out_specs=[vmem] * 3,
        compiler_params=pltpu.CompilerParams(vmem_limit_bytes=16 * 1024 * 1024),
    )(near, far)


def factor_kernel(place_ref, near_ref, far_ref, panel_ref, mixed_ref, r_ref, a_ref, upper, linv, rows_ref, y_ref, w_ref, z_ref, work):
    rows = lax.broadcasted_iota(jnp.int32, (tile, tile), 0)
    cols = lax.broadcasted_iota(jnp.int32, (tile, tile), 1)
    eye = jnp.where(rows == cols, 1.0, 0.0).astype(jnp.float32)
    own, width = panel_ref.shape
    picked = r_ref.shape[0]
    for core, blocks in enumerate(gram_blocks):
        for at, (i, j) in enumerate(blocks):
            side = slice(at * tile, (at + 1) * tile)
            block = jnp.where(place_ref[0] == core, near_ref[side, :], far_ref[side, :])
            if i == j:
                block = block + ridge_shift * eye
            a_ref[i * tile : (i + 1) * tile, j * tile : (j + 1) * tile] = block
    upper[...] = jnp.zeros_like(upper)
    linv[...] = jnp.zeros_like(linv)
    z_ref[...] = jnp.zeros_like(z_ref)
    rows_ref[...] = panel_ref[...]
    work[:, 0:tile] = a_ref[0:tile, 0:tile]
    work[:, tile:] = eye
    later = []
    for b in range(0, width, tile):
        e = b + tile
        n = e + tile
        factor_diagonal(work, later)
        while later:
            later.pop(0)()
        inverse = work[:, tile:]
        diagonal = work[:, 0:tile]
        if e == width:
            upper[b:e, b:e] = jnp.where(cols >= rows, diagonal, 0.0)
            y = stacked(rows_ref[:, b:e], inverse, 1, 1)
            last = jnp.concatenate([-stacked(inverse, w_ref[:, 0:b]), inverse], 1)
            linv[b:e, :] = last
            z_ref[...] = z_ref[...] + stacked(y, last)
            break
        beside = stacked(inverse, a_ref[b:e, e:n])
        work[:, 0:tile] = a_ref[e:n, e:n] - stacked(beside, beside, 0, 0)
        work[:, tile:] = eye

        def rows_of_tiles(b=b, e=e, n=n, inverse=inverse, diagonal=diagonal, beside=beside):
            upper[b:e, b:e] = jnp.where(cols >= rows, diagonal, 0.0)
            upper[b:e, e:n] = beside
            linv[b:e, b:e] = inverse
            if b:
                linv[b:e, 0:b] = -stacked(inverse, w_ref[:, 0:b])
            y_ref[:, b:e] = stacked(rows_ref[:, b:e], inverse, 1, 1)
            if n < width:
                upper[b:e, n:] = stacked(inverse, a_ref[b:e, n:])

        def remainder(b=b, e=e, n=n, beside=beside):
            right = upper[b:e, e:]
            if n < width:
                a_ref[e:n, n:] = a_ref[e:n, n:] - stacked(beside, right[:, tile:], 0, 0)
            for c in range(n, width, tile):
                a_ref[c : c + tile, c:] = a_ref[c : c + tile, c:] - stacked(
                    right[:, c - e : c - e + tile], right[:, c - e :], 0, 0
                )
            rows_ref[:, e:] = rows_ref[:, e:] - stacked(y_ref[:, b:e], right)

        def inverses(b=b, e=e, n=n):
            w_ref[:, 0:e] = stacked(upper[0:e, e:n], linv[0:e, 0:e], 0, 0)
            z_ref[:, 0:e] = z_ref[:, 0:e] + stacked(y_ref[:, b:e], linv[b:e, 0:e])

        later = [rows_of_tiles, remainder, inverses]
    at = pl.ds(pl.multiple_of(place_ref[1 + classes], picked), picked)
    r_ref[...] = upper[at, :]
    for b in range(0, width, tile):
        mixed_ref[b // tile, 0:own, :] = z_ref[:, b : b + tile]
        mixed_ref[b // tile, own:, :] = linv[at, b : b + tile]


def factor(place, near, far, panel, picked):
    own, width = panel.shape
    vmem = pl.BlockSpec(memory_space=pltpu.VMEM)
    square = pltpu.VMEM((width, width), jnp.float32)
    flat = pltpu.VMEM((own, width), jnp.float32)
    return pl.pallas_call(
        factor_kernel,
        out_shape=(
            jax.ShapeDtypeStruct((width // tile, own + picked, tile), jnp.float32),
            jax.ShapeDtypeStruct((picked, width), jnp.float32),
        ),
        in_specs=[pl.BlockSpec(memory_space=pltpu.SMEM), vmem, vmem, vmem],
        out_specs=(vmem, vmem),
        scratch_shapes=[
            square,
            square,
            square,
            flat,
            flat,
            pltpu.VMEM((tile, width - tile), jnp.float32),
            flat,
            pltpu.VMEM((tile, 2 * tile), jnp.float32),
        ],
        compiler_params=pltpu.CompilerParams(vmem_limit_bytes=20 * 1024 * 1024),
        cost_estimate=pl.CostEstimate(flops=20 * 10**9, bytes_accessed=4 * 10**6, transcendentals=0),
    )(place, near, far, panel)


def finish_kernel(place_ref, mixed_ref, *refs):
    quarters = refs[:classes]
    trail_ref, updated_ref, coupling_ref = refs[classes:]
    own = trail_ref.shape[0]
    half = quarters[0].shape[1]
    core = place_ref[0]
    left = [mixed_ref[place_ref[1 + m]] for m in range(classes)]
    left = [jnp.concatenate(left[m : m + 2], 1) for m in range(0, classes, 2)]
    for c in range(0, half, tile):
        out = None
        for m in range(0, classes, 2):
            right = jnp.concatenate(
                [
                    jnp.concatenate([quarters[m][side, c : c + tile, :], quarters[m + 1][side, c : c + tile, :]], 0)
                    for side in range(2)
                ],
                1,
            )
            term = product(left[m // 2], right)
            out = term if out is None else out + term
        for part, where in ((out[:, :tile], core), (out[:, tile:], 1 - core)):
            at = pl.ds(pl.multiple_of(where * half + c, tile), tile)
            updated_ref[:, at] = trail_ref[:, at] - part[:own]
            coupling_ref[:, at] = part[own:]


def finish(place, mixed, quarters, trailing):
    vmem = pl.BlockSpec(memory_space=pltpu.VMEM)
    own, trail = trailing.shape
    return pl.pallas_call(
        finish_kernel,
        out_shape=(
            jax.ShapeDtypeStruct((own, trail), jnp.float32),
            jax.ShapeDtypeStruct((mixed.shape[1] - own, trail), jnp.float32),
        ),
        in_specs=[pl.BlockSpec(memory_space=pltpu.SMEM)] + [vmem] * (2 + classes),
        out_specs=(vmem, vmem),
        compiler_params=pltpu.CompilerParams(vmem_limit_bytes=32 * 1024 * 1024),
    )(place, mixed, *quarters, trailing)


def kind_of(x, y, z):
    return (x % 2) ^ (2 * (y % 2)) ^ (3 * (z % 2))


def local(panel, trailing, counts):
    own, width = panel.shape
    half = trailing.shape[1] // 2
    depth = lax.axis_size("z")
    groups = lax.axis_size("grp")
    side = 4
    members = 2 * depth
    chip_count = groups * depth
    chunk = half // chip_count
    gram_chunk = len(gram_blocks[0]) * tile // chip_count
    kinds = [kind_of(g % side, g // side, z) for g in range(groups) for z in range(depth)]
    group, z, core = lax.axis_index("grp"), lax.axis_index("z"), lax.axis_index("core")
    kind = kind_of(group % side, group // side, z)
    picked = width // members
    start = (z * 2 + core) * picked
    place = jnp.stack([core] + [kind ^ m for m in range(classes)] + [start]).astype(jnp.int32)
    swap = [(0, 1), (1, 0)]
    count_row = counts[None, :]
    sent_trail = lax.dynamic_slice_in_dim(trailing, (1 - core) * half, half, 1)
    with jax.named_scope("swap_inputs"):
        far_counts = lax.ppermute(count_row, "core", swap)
        other_panel = lax.ppermute(panel, "core", swap)
        far_trail = lax.ppermute(sent_trail, "core", swap)
    with jax.named_scope("local_products"):
        *terms, gram_terms = products(
            place, panel, other_panel, trailing, far_trail, count_row, far_counts, own * groups * members
        )
    def pairs(before, after):
        out = []
        for a in range(before):
            for i in range(side):
                for b in range(after):
                    for c in range(2):
                        to = i ^ (3 if c else 1)
                        out.append((((a * side + i) * after + b) * 2 + c, ((a * side + to) * after + b) * 2 + c))
        return out

    along = (
        ("along_x", ("grp", "core"), groups // side, 1),
        ("along_y", ("grp", "core"), 1, side),
        ("along_z", ("z", "core"), 1, 1),
    )

    def exchange(rows):
        with jax.named_scope("exchange"):
            rows = lax.all_to_all(rows.reshape(chip_count, 1, -1), chips, 0, 0, tiled=True)
        return rows.reshape(-1, tile)

    parts = [terms[0]]
    for m, (name, axis, before, after) in enumerate(along):
        with jax.named_scope("terms_" + name):
            parts.append(lax.ppermute(terms[1 + m], axis, pairs(before, after)))
    with jax.named_scope("combine_terms"):
        pieces = combine(gram_terms, parts, chip_count)
    pieces = exchange(pieces)
    with jax.named_scope("sum_pieces"):
        copies = sum_pieces(pieces, gram_chunk, kinds)
    copies = exchange(copies)
    with jax.named_scope("swap_copies"):
        far_copies = lax.ppermute(copies, "core", swap)
    with jax.named_scope("unpack_sums"):
        near_gram, far_gram, quarter = unpack(copies, far_copies, chip_count, gram_chunk, chunk)
    quarters = [quarter]
    for name, axis, before, after in along:
        with jax.named_scope("quarters_" + name):
            quarters.append(lax.ppermute(quarter, axis, pairs(before, after)))
    with jax.named_scope("factor_gram"):
        mixed, r_rows = factor(place, near_gram, far_gram, panel, picked)
    with jax.named_scope("apply_factor"):
        updated, coupling = finish(place, mixed, quarters, trailing)
    return (r_rows, coupling, updated)


def solution(mesh):
    groups, members = mesh.devices.shape
    split = Mesh(mesh.devices.reshape(groups, members // 2, 2), ("grp", "z", "core"))
    rows = P(("grp", "z", "core"))
    return jax.shard_map(
        local,
        mesh=split,
        in_specs=(P(("grp", "z", "core"), None), P(("grp", "z", "core"), None), rows),
        out_specs=(P(("z", "core"), None), P(("z", "core"), None), P(("grp", "z", "core"), None)),
        check_vma=False,
    )
```

```python
import functools

import jax
import jax.numpy as jnp
from jax import lax
from jax.experimental import pallas as pl
from jax.experimental.pallas import tpu as pltpu
from jax.sharding import Mesh, PartitionSpec as P

ridge_shift = 0.05
HIGHEST = lax.Precision.HIGHEST
tile = 128
strip = 32
chips = ("grp", "z")
classes = 4
shares = (3, 3, 2, 2)


def product(left, right, left_dim=1, right_dim=0):
    return lax.dot_general(
        left,
        right,
        (((left_dim,), (right_dim,)), ((), ())),
        precision=HIGHEST,
        preferred_element_type=jnp.float32,
    )


def three_parts(x):
    high = x.astype(jnp.bfloat16)
    rest = x - high.astype(jnp.float32)
    middle = rest.astype(jnp.bfloat16)
    return high, middle, (rest - middle.astype(jnp.float32)).astype(jnp.bfloat16)


def stacked(left, right, left_dim=1, right_dim=0):
    lh, lm, ll = three_parts(left)
    rh, rm, rl = three_parts(right)
    return lax.dot_general(
        jnp.concatenate([lh, lh, lm, lh, ll, lm], left_dim),
        jnp.concatenate([rh, rm, rh, rl, rh, rm], right_dim),
        (((left_dim,), (right_dim,)), ((), ())),
        preferred_element_type=jnp.float32,
    )


def stacked_two(left, right, left_dim=1, right_dim=0):
    lh, ll, _ = three_parts(left)
    rh, rl, _ = three_parts(right)
    return lax.dot_general(
        jnp.concatenate([lh, lh, ll], left_dim),
        jnp.concatenate([rh, rl, rh], right_dim),
        (((left_dim,), (right_dim,)), ((), ())),
        preferred_element_type=jnp.float32,
    )


def factor_diagonal(work, later):
    sub = lax.broadcasted_iota(jnp.int32, (8, tile), 0)
    groups = strip // 8

    def spread_row(array, row):
        return jnp.broadcast_to(array[row : row + 1, :], (8, tile))

    for r in range(0, tile, strip):
        left = [work[r + 8 * g : r + 8 * g + 8, 0:tile] for g in range(groups)]
        right = [work[r + 8 * g : r + 8 * g + 8, tile : 2 * tile] for g in range(groups)]
        if later:
            later.pop(0)()
        col = {}
        for c in range(strip):
            for g in range(c // 8, groups):
                col[c, g] = jnp.broadcast_to(left[g][:, r + c : r + c + 1], (8, tile))
        for k in range(strip):
            at, row = k // 8, k % 8
            inv = lax.rsqrt(spread_row(col[k, at], row))
            low = {g: col[k, g] * inv for g in range(at, groups)}
            for c in range(k + 1, strip):
                factor_c = spread_row(low[c // 8], c % 8)
                for g in range(c // 8, groups):
                    col[c, g] = col[c, g] - low[g] * factor_c
            below = jnp.where(sub > row, low[at], 0.0)
            for side in (left, right):
                pivot = spread_row(side[at], row) * inv
                side[at] = jnp.where(sub == row, pivot, side[at] - below * pivot)
                for g in range(at + 1, groups):
                    side[g] = side[g] - low[g] * pivot
        new_left = jnp.concatenate(left, 0)
        new_right = jnp.concatenate(right, 0)
        work[r : r + strip, 0:tile] = new_left
        work[r : r + strip, tile : 2 * tile] = new_right
        if r + strip < tile:
            update = stacked(new_left, jnp.concatenate([new_left, new_right], 1), 0, 0)
            work[r + strip : tile, :] = work[r + strip : tile, :] - update[r + strip : tile, :]


gram_blocks = (((0, 0), (1, 1), (0, 1), (0, 2), (0, 3)), ((2, 2), (3, 3), (2, 3), (1, 2), (1, 3)))


def products_kernel(place_ref, panel_ref, other_ref, trail_ref, far_ref, counts_ref, far_counts_ref, *refs, total_rows):
    outs, (pt, wp, wt, quarters, gram, shared) = refs[:classes], refs[classes:]
    core = place_ref[0]
    own, width = panel_ref.shape
    half = trail_ref.shape[1]
    for at, rows, trail, count in ((0, panel_ref, trail_ref, counts_ref), (own, other_ref, far_ref, far_counts_ref)):
        weight = jnp.transpose(jnp.broadcast_to(count[...].astype(jnp.float32) / total_rows, (own, own)))
        for c in range(0, width, tile):
            block = rows[:, c : c + tile]
            pt[c : c + tile, at : at + own] = jnp.transpose(block)
            wp[at : at + own, c : c + tile] = block * weight
        for c in range(0, half, tile):
            wt[at : at + own, c : c + tile] = trail[:, c : c + tile] * weight
    step = 2 * tile
    for c in range(0, half, step):
        n = min(step, half - c)
        part = stacked_two(pt[...], wt[:, c : c + n])
        for k in range(classes):
            for j in range(0, n, tile):
                quarters[k, c + j : c + j + tile, :] = part[k * tile : (k + 1) * tile, j : j + tile]
    near = pl.multiple_of(core * step, tile)
    first = product(pt[pl.ds(near, tile), :], wp[:, pl.ds(near, step)])
    gram[0:tile, :] = first[:, :tile]
    gram[2 * tile : 3 * tile, :] = first[:, tile:]
    near = pl.multiple_of(core * step + tile, tile)
    gram[tile : 2 * tile, :] = product(pt[pl.ds(near, tile), :], wp[:, pl.ds(near, tile)])
    near = pl.multiple_of(core * tile, tile)
    last = product(pt[pl.ds(near, tile), :], wp[:, step:])
    gram[3 * tile : 4 * tile, :] = last[:, :tile]
    gram[4 * tile :, :] = last[:, tile:]
    most = max(shares)
    chip_count = shared.shape[1] // most
    first = 0
    for k, share in enumerate(shares):
        if share == most:
            shared[k] = gram[first : first + chip_count * share, :]
        else:
            shared[k] = jnp.zeros_like(shared[k])
            for q in range(chip_count):
                shared[k, q * most : q * most + share, :] = gram[first + q * share : first + (q + 1) * share, :]
        first += chip_count * share
    for m in range(classes):
        outs[m][0:half, :] = quarters[place_ref[1 + m]]
        outs[m][half:, :] = shared[place_ref[1 + m]]


def products(place, panel, other, trailing, far, counts, far_counts, chip_count, total_rows):
    own, width = panel.shape
    half = far.shape[1]
    gram_rows = len(gram_blocks[0]) * tile
    sent_rows = half + max(shares) * chip_count
    whole = lambda shape: pl.BlockSpec(shape, lambda i, place: (0, 0))
    return pl.pallas_call(
        functools.partial(products_kernel, total_rows=total_rows),
        out_shape=[jax.ShapeDtypeStruct((sent_rows, tile), jnp.float32)] * classes,
        grid_spec=pltpu.PrefetchScalarGridSpec(
            num_scalar_prefetch=1,
            grid=(1,),
            in_specs=[
                whole((own, width)),
                whole((own, width)),
                pl.BlockSpec((own, half), lambda i, place: (0, place[0])),
                whole((own, half)),
                whole((1, own)),
                whole((1, own)),
            ],
            out_specs=[whole((sent_rows, tile))] * classes,
            scratch_shapes=[
                pltpu.VMEM((width, 2 * own), jnp.float32),
                pltpu.VMEM((2 * own, width), jnp.float32),
                pltpu.VMEM((2 * own, half), jnp.float32),
                pltpu.VMEM((classes, half, tile), jnp.float32),
                pltpu.VMEM((gram_rows, tile), jnp.float32),
                pltpu.VMEM((classes, max(shares) * chip_count, tile), jnp.float32),
            ],
        ),
        compiler_params=pltpu.CompilerParams(vmem_limit_bytes=32 * 1024 * 1024),
    )(place, panel, other, trailing, far, counts, far_counts)


def combine_kernel(*refs, chip_count, chunk):
    parts, out_ref = refs[:classes], refs[classes]
    most = max(shares)
    piece = chunk + most

    def added(at, rows):
        side = slice(at, at + rows)
        return (parts[0][side, :] + parts[1][side, :]) + (parts[2][side, :] + parts[3][side, :])

    for q in range(chip_count):
        gram = added(chip_count * chunk + q * most, most)
        out_ref[q * piece : (q + 1) * piece, :] = jnp.concatenate([gram, added(q * chunk, chunk)], 0)


def combine(parts, chip_count, chunk):
    vmem = pl.BlockSpec(memory_space=pltpu.VMEM)
    return pl.pallas_call(
        functools.partial(combine_kernel, chip_count=chip_count, chunk=chunk),
        out_shape=jax.ShapeDtypeStruct(parts[0].shape, jnp.float32),
        in_specs=[vmem] * classes,
        out_specs=vmem,
        compiler_params=pltpu.CompilerParams(vmem_limit_bytes=16 * 1024 * 1024),
    )(*parts)


def sum_kernel(pieces_ref, copies_ref, total_ref, *, chunk, kinds):
    most = max(shares)
    piece = chunk + most
    both = chunk + sum(shares)
    for k in range(classes):
        total = None
        for q, kind in enumerate(kinds):
            if kind == k:
                part = pieces_ref[q * piece : (q + 1) * piece, :]
                total = part if total is None else total + part
        total_ref[k, 0:piece, :] = total
    gram = [total_ref[k, 0:share, :] for k, share in enumerate(shares)]
    for k in range(classes):
        copy = jnp.concatenate(gram + [total_ref[k, most:piece, :]], 0)
        for q, kind in enumerate(kinds):
            if kind == k:
                copies_ref[q * both : (q + 1) * both, :] = copy


def sum_pieces(pieces, chunk, kinds):
    vmem = pl.BlockSpec(memory_space=pltpu.VMEM)
    return pl.pallas_call(
        functools.partial(sum_kernel, chunk=chunk, kinds=kinds),
        out_shape=jax.ShapeDtypeStruct((len(kinds) * (chunk + sum(shares)), tile), jnp.float32),
        in_specs=[vmem],
        out_specs=vmem,
        scratch_shapes=[pltpu.VMEM((classes, chunk + max(shares) + 7, tile), jnp.float32)],
        compiler_params=pltpu.CompilerParams(vmem_limit_bytes=16 * 1024 * 1024),
    )(pieces)


def unpack_kernel(near_ref, far_ref, near_gram, far_gram, quarters_ref, *, chip_count):
    size = near_gram.shape[0] // chip_count
    chunk = quarters_ref.shape[1] // chip_count
    both = size + chunk
    for at, (copies_ref, gram_ref) in enumerate(((near_ref, near_gram), (far_ref, far_gram))):
        for q in range(chip_count):
            at_row, first = q * both, 0
            for share in shares:
                gram_ref[first + q * share : first + (q + 1) * share, :] = copies_ref[at_row : at_row + share, :]
                at_row += share
                first += chip_count * share
            quarters_ref[at, q * chunk : (q + 1) * chunk, :] = copies_ref[q * both + size : (q + 1) * both, :]


def unpack(near, far, chip_count, size, chunk):
    vmem = pl.BlockSpec(memory_space=pltpu.VMEM)
    gram = jax.ShapeDtypeStruct((chip_count * size, tile), jnp.float32)
    return pl.pallas_call(
        functools.partial(unpack_kernel, chip_count=chip_count),
        out_shape=(gram, gram, jax.ShapeDtypeStruct((2, chip_count * chunk, tile), jnp.float32)),
        in_specs=[vmem] * 2,
        out_specs=[vmem] * 3,
        compiler_params=pltpu.CompilerParams(vmem_limit_bytes=16 * 1024 * 1024),
    )(near, far)


def factor_kernel(place_ref, near_ref, far_ref, panel_ref, mixed_ref, r_ref, a_ref, upper, linv, rows_ref, y_ref, w_ref, z_ref, work):
    rows = lax.broadcasted_iota(jnp.int32, (tile, tile), 0)
    cols = lax.broadcasted_iota(jnp.int32, (tile, tile), 1)
    eye = jnp.where(rows == cols, 1.0, 0.0).astype(jnp.float32)
    own, width = panel_ref.shape
    picked = r_ref.shape[0]
    for core, blocks in enumerate(gram_blocks):
        for at, (i, j) in enumerate(blocks):
            side = slice(at * tile, (at + 1) * tile)
            block = jnp.where(place_ref[0] == core, near_ref[side, :], far_ref[side, :])
            if i == j:
                block = block + ridge_shift * eye
            a_ref[i * tile : (i + 1) * tile, j * tile : (j + 1) * tile] = block
    upper[...] = jnp.zeros_like(upper)
    linv[...] = jnp.zeros_like(linv)
    z_ref[...] = jnp.zeros_like(z_ref)
    rows_ref[...] = panel_ref[...]
    work[:, 0:tile] = a_ref[0:tile, 0:tile]
    work[:, tile:] = eye
    later = []
    for b in range(0, width, tile):
        e = b + tile
        n = e + tile
        factor_diagonal(work, later)
        while later:
            later.pop(0)()
        inverse = work[:, tile:]
        diagonal = work[:, 0:tile]
        if e == width:
            upper[b:e, b:e] = jnp.where(cols >= rows, diagonal, 0.0)
            y = stacked(rows_ref[:, b:e], inverse, 1, 1)
            last = jnp.concatenate([-stacked(inverse, w_ref[:, 0:b]), inverse], 1)
            linv[b:e, :] = last
            z_ref[...] = z_ref[...] + stacked(y, last)
            break
        beside = stacked(inverse, a_ref[b:e, e:n])
        work[:, 0:tile] = a_ref[e:n, e:n] - stacked(beside, beside, 0, 0)
        work[:, tile:] = eye

        def rows_of_tiles(b=b, e=e, n=n, inverse=inverse, diagonal=diagonal, beside=beside):
            upper[b:e, b:e] = jnp.where(cols >= rows, diagonal, 0.0)
            upper[b:e, e:n] = beside
            linv[b:e, b:e] = inverse
            if b:
                linv[b:e, 0:b] = -stacked(inverse, w_ref[:, 0:b])
            y_ref[:, b:e] = stacked(rows_ref[:, b:e], inverse, 1, 1)
            if n < width:
                upper[b:e, n:] = stacked(inverse, a_ref[b:e, n:])

        def remainder(b=b, e=e, n=n, beside=beside):
            right = upper[b:e, e:]
            if n < width:
                a_ref[e:n, n:] = a_ref[e:n, n:] - stacked(beside, right[:, tile:], 0, 0)
            for c in range(n, width, tile):
                a_ref[c : c + tile, c:] = a_ref[c : c + tile, c:] - stacked(
                    right[:, c - e : c - e + tile], right[:, c - e :], 0, 0
                )
            rows_ref[:, e:] = rows_ref[:, e:] - stacked(y_ref[:, b:e], right)

        def inverses(b=b, e=e, n=n):
            w_ref[:, 0:e] = stacked(upper[0:e, e:n], linv[0:e, 0:e], 0, 0)
            z_ref[:, 0:e] = z_ref[:, 0:e] + stacked(y_ref[:, b:e], linv[b:e, 0:e])

        later = [rows_of_tiles, remainder, inverses]
    at = pl.ds(pl.multiple_of(place_ref[1 + classes], picked), picked)
    r_ref[...] = upper[at, :]
    for b in range(0, width, tile):
        mixed_ref[b // tile, 0:own, :] = z_ref[:, b : b + tile]
        mixed_ref[b // tile, own:, :] = linv[at, b : b + tile]


def factor(place, near, far, panel, picked):
    own, width = panel.shape
    vmem = pl.BlockSpec(memory_space=pltpu.VMEM)
    square = pltpu.VMEM((width, width), jnp.float32)
    flat = pltpu.VMEM((own, width), jnp.float32)
    return pl.pallas_call(
        factor_kernel,
        out_shape=(
            jax.ShapeDtypeStruct((width // tile, own + picked, tile), jnp.float32),
            jax.ShapeDtypeStruct((picked, width), jnp.float32),
        ),
        in_specs=[pl.BlockSpec(memory_space=pltpu.SMEM), vmem, vmem, vmem],
        out_specs=(vmem, vmem),
        scratch_shapes=[
            square,
            square,
            square,
            flat,
            flat,
            pltpu.VMEM((tile, width - tile), jnp.float32),
            flat,
            pltpu.VMEM((tile, 2 * tile), jnp.float32),
        ],
        compiler_params=pltpu.CompilerParams(vmem_limit_bytes=20 * 1024 * 1024),
        cost_estimate=pl.CostEstimate(flops=20 * 10**9, bytes_accessed=4 * 10**6, transcendentals=0),
    )(place, near, far, panel)


def finish_kernel(place_ref, mixed_ref, *refs):
    quarters = refs[:classes]
    trail_ref, updated_ref, coupling_ref = refs[classes:]
    own = trail_ref.shape[0]
    half = quarters[0].shape[1]
    core = place_ref[0]
    left = [mixed_ref[place_ref[1 + m]] for m in range(classes)]
    left = [jnp.concatenate(left[m : m + 2], 1) for m in range(0, classes, 2)]
    for c in range(0, half, tile):
        out = None
        for m in range(0, classes, 2):
            right = jnp.concatenate(
                [
                    jnp.concatenate([quarters[m][side, c : c + tile, :], quarters[m + 1][side, c : c + tile, :]], 0)
                    for side in range(2)
                ],
                1,
            )
            term = stacked_two(left[m // 2], right)
            out = term if out is None else out + term
        for part, where in ((out[:, :tile], core), (out[:, tile:], 1 - core)):
            at = pl.ds(pl.multiple_of(where * half + c, tile), tile)
            updated_ref[:, at] = trail_ref[:, at] - part[:own]
            coupling_ref[:, at] = part[own:]


def finish(place, mixed, quarters, trailing):
    vmem = pl.BlockSpec(memory_space=pltpu.VMEM)
    own, trail = trailing.shape
    return pl.pallas_call(
        finish_kernel,
        out_shape=(
            jax.ShapeDtypeStruct((own, trail), jnp.float32),
            jax.ShapeDtypeStruct((mixed.shape[1] - own, trail), jnp.float32),
        ),
        in_specs=[pl.BlockSpec(memory_space=pltpu.SMEM)] + [vmem] * (2 + classes),
        out_specs=(vmem, vmem),
        compiler_params=pltpu.CompilerParams(vmem_limit_bytes=32 * 1024 * 1024),
    )(place, mixed, *quarters, trailing)


def kind_of(x, y, z):
    return (x % 2) ^ (2 * (y % 2)) ^ (3 * (z % 2))


def local(panel, trailing, counts):
    own, width = panel.shape
    half = trailing.shape[1] // 2
    depth = lax.axis_size("z")
    groups = lax.axis_size("grp")
    side = 4
    members = 2 * depth
    chip_count = groups * depth
    chunk = half // chip_count
    gram_chunk = sum(shares)
    kinds = [kind_of(g % side, g // side, z) for g in range(groups) for z in range(depth)]
    group, z, core = lax.axis_index("grp"), lax.axis_index("z"), lax.axis_index("core")
    kind = kind_of(group % side, group // side, z)
    picked = width // members
    start = (z * 2 + core) * picked
    place = jnp.stack([core] + [kind ^ m for m in range(classes)] + [start]).astype(jnp.int32)
    swap = [(0, 1), (1, 0)]
    count_row = counts[None, :]
    sent_trail = lax.dynamic_slice_in_dim(trailing, (1 - core) * half, half, 1)
    with jax.named_scope("swap_inputs"):
        far_counts = lax.ppermute(count_row, "core", swap)
        other_panel = lax.ppermute(panel, "core", swap)
        far_trail = lax.ppermute(sent_trail, "core", swap)
    with jax.named_scope("local_products"):
        terms = products(
            place, panel, other_panel, trailing, far_trail, count_row, far_counts, chip_count, own * groups * members
        )
    def pairs(before, after):
        out = []
        for a in range(before):
            for i in range(side):
                for b in range(after):
                    for c in range(2):
                        to = i ^ (3 if c else 1)
                        out.append((((a * side + i) * after + b) * 2 + c, ((a * side + to) * after + b) * 2 + c))
        return out

    along = (
        ("along_x", ("grp", "core"), groups // side, 1),
        ("along_y", ("grp", "core"), 1, side),
        ("along_z", ("z", "core"), 1, 1),
    )

    def exchange(rows):
        with jax.named_scope("exchange"):
            rows = lax.all_to_all(rows.reshape(chip_count, 1, -1), chips, 0, 0, tiled=True)
        return rows.reshape(-1, tile)

    parts = [terms[0]]
    for m, (name, axis, before, after) in enumerate(along):
        with jax.named_scope("terms_" + name):
            parts.append(lax.ppermute(terms[1 + m], axis, pairs(before, after)))
    with jax.named_scope("combine_terms"):
        pieces = combine(parts, chip_count, chunk)
    pieces = exchange(pieces)
    with jax.named_scope("sum_pieces"):
        copies = sum_pieces(pieces, chunk, kinds)
    copies = exchange(copies)
    with jax.named_scope("swap_copies"):
        far_copies = lax.ppermute(copies, "core", swap)
    with jax.named_scope("unpack_sums"):
        near_gram, far_gram, quarter = unpack(copies, far_copies, chip_count, gram_chunk, chunk)
    quarters = [quarter]
    for name, axis, before, after in along:
        with jax.named_scope("quarters_" + name):
            quarters.append(lax.ppermute(quarter, axis, pairs(before, after)))
    with jax.named_scope("factor_gram"):
        mixed, r_rows = factor(place, near_gram, far_gram, panel, picked)
    with jax.named_scope("apply_factor"):
        updated, coupling = finish(place, mixed, quarters, trailing)
    return (r_rows, coupling, updated)


def solution(mesh):
    groups, members = mesh.devices.shape
    split = Mesh(mesh.devices.reshape(groups, members // 2, 2), ("grp", "z", "core"))
    rows = P(("grp", "z", "core"))
    return jax.shard_map(
        local,
        mesh=split,
        in_specs=(P(("grp", "z", "core"), None), P(("grp", "z", "core"), None), rows),
        out_specs=(P(("z", "core"), None), P(("z", "core"), None), P(("grp", "z", "core"), None)),
        check_vma=False,
    )
```

```python
import functools

import jax
import jax.numpy as jnp
from jax import lax
from jax.experimental import pallas as pl
from jax.experimental.pallas import tpu as pltpu
from jax.sharding import Mesh, PartitionSpec as P

ridge_shift = 0.05
HIGHEST = lax.Precision.HIGHEST
tile = 128
strip = 32
half_strip = 16
chips = ("grp", "z")
classes = 4
shares = (3, 3, 2, 2)


def product(left, right, left_dim=1, right_dim=0):
    return lax.dot_general(
        left,
        right,
        (((left_dim,), (right_dim,)), ((), ())),
        precision=HIGHEST,
        preferred_element_type=jnp.float32,
    )


def three_parts(x):
    high = x.astype(jnp.bfloat16)
    rest = x - high.astype(jnp.float32)
    middle = rest.astype(jnp.bfloat16)
    return high, middle, (rest - middle.astype(jnp.float32)).astype(jnp.bfloat16)


def stacked(left, right, left_dim=1, right_dim=0):
    lh, lm, ll = three_parts(left)
    rh, rm, rl = three_parts(right)
    return lax.dot_general(
        jnp.concatenate([lh, lh, lm, lh, ll, lm], left_dim),
        jnp.concatenate([rh, rm, rh, rl, rh, rm], right_dim),
        (((left_dim,), (right_dim,)), ((), ())),
        preferred_element_type=jnp.float32,
    )


def stacked_two(left, right, left_dim=1, right_dim=0):
    lh, ll, _ = three_parts(left)
    rh, rl, _ = three_parts(right)
    return lax.dot_general(
        jnp.concatenate([lh, lh, ll], left_dim),
        jnp.concatenate([rh, rl, rh], right_dim),
        (((left_dim,), (right_dim,)), ((), ())),
        preferred_element_type=jnp.float32,
    )


def factor_diagonal(work, later):
    sub = lax.broadcasted_iota(jnp.int32, (8, tile), 0)
    groups = strip // 8

    def spread_row(array, row):
        return jnp.broadcast_to(array[row : row + 1, :], (8, tile))

    for r in range(0, tile, strip):
        left = [work[r + 8 * g : r + 8 * g + 8, 0:tile] for g in range(groups)]
        right = [work[r + 8 * g : r + 8 * g + 8, tile : 2 * tile] for g in range(groups)]
        pivots = [jnp.ones((8, tile), jnp.float32)] * groups
        if later:
            later.pop(0)()
        for first in range(0, strip, half_strip):
            col = {}
            for c in range(first, first + half_strip):
                for g in range(c // 8, groups):
                    col[c, g] = jnp.broadcast_to(left[g][:, r + c : r + c + 1], (8, tile))
            for k in range(first, first + half_strip):
                at, row = k // 8, k % 8
                pivot = spread_row(col[k, at], row)
                inv = 1.0 / pivot
                pivots[at] = jnp.where(sub == row, pivot, pivots[at])
                low = {g: col[k, g] * inv for g in range(at, groups)}
                for c in range(k + 1, first + half_strip):
                    factor_c = spread_row(col[k, c // 8], c % 8)
                    for g in range(c // 8, groups):
                        if c == k + 1 and g == c // 8:
                            col[c, g] = col[c, g] - (col[k, g] * factor_c) * inv
                        else:
                            col[c, g] = col[c, g] - low[g] * factor_c
                below = jnp.where(sub > row, low[at], 0.0)
                for side in (left, right):
                    pivot_row = spread_row(side[at], row)
                    side[at] = side[at] - below * pivot_row
                    for g in range(at + 1, groups):
                        side[g] = side[g] - low[g] * pivot_row
        for g in range(groups):
            scale = lax.rsqrt(pivots[g])
            left[g] = left[g] * scale
            right[g] = right[g] * scale
        new_left = jnp.concatenate(left, 0)
        new_right = jnp.concatenate(right, 0)
        work[r : r + strip, 0:tile] = new_left
        work[r : r + strip, tile : 2 * tile] = new_right
        if r + strip < tile:
            update = stacked(new_left, jnp.concatenate([new_left, new_right], 1), 0, 0)
            work[r + strip : tile, :] = work[r + strip : tile, :] - update[r + strip : tile, :]


gram_blocks = (((0, 0), (1, 1), (0, 1), (0, 2), (0, 3)), ((2, 2), (3, 3), (2, 3), (1, 2), (1, 3)))


def products_kernel(place_ref, panel_ref, other_ref, trail_ref, far_ref, counts_ref, far_counts_ref, *refs, total_rows):
    outs, (pt, wp, wt, quarters, gram, shared) = refs[:classes], refs[classes:]
    core = place_ref[0]
    own, width = panel_ref.shape
    half = trail_ref.shape[1]
    for at, rows, trail, count in ((0, panel_ref, trail_ref, counts_ref), (own, other_ref, far_ref, far_counts_ref)):
        weight = jnp.transpose(jnp.broadcast_to(count[...].astype(jnp.float32) / total_rows, (own, own)))
        for c in range(0, width, tile):
            block = rows[:, c : c + tile]
            pt[c : c + tile, at : at + own] = jnp.transpose(block)
            wp[at : at + own, c : c + tile] = block * weight
        for c in range(0, half, tile):
            wt[at : at + own, c : c + tile] = trail[:, c : c + tile] * weight
    step = 2 * tile
    for c in range(0, half, step):
        n = min(step, half - c)
        part = stacked_two(pt[...], wt[:, c : c + n])
        for k in range(classes):
            for j in range(0, n, tile):
                quarters[k, c + j : c + j + tile, :] = part[k * tile : (k + 1) * tile, j : j + tile]
    near = pl.multiple_of(core * step, tile)
    first = product(pt[pl.ds(near, tile), :], wp[:, pl.ds(near, step)])
    gram[0:tile, :] = first[:, :tile]
    gram[2 * tile : 3 * tile, :] = first[:, tile:]
    near = pl.multiple_of(core * step + tile, tile)
    gram[tile : 2 * tile, :] = product(pt[pl.ds(near, tile), :], wp[:, pl.ds(near, tile)])
    near = pl.multiple_of(core * tile, tile)
    last = product(pt[pl.ds(near, tile), :], wp[:, step:])
    gram[3 * tile : 4 * tile, :] = last[:, :tile]
    gram[4 * tile :, :] = last[:, tile:]
    most = max(shares)
    chip_count = shared.shape[1] // most
    first = 0
    for k, share in enumerate(shares):
        if share == most:
            shared[k] = gram[first : first + chip_count * share, :]
        else:
            shared[k] = jnp.zeros_like(shared[k])
            for q in range(chip_count):
                shared[k, q * most : q * most + share, :] = gram[first + q * share : first + (q + 1) * share, :]
        first += chip_count * share
    for m in range(classes):
        outs[m][0:half, :] = quarters[place_ref[1 + m]]
        outs[m][half:, :] = shared[place_ref[1 + m]]


def products(place, panel, other, trailing, far, counts, far_counts, chip_count, total_rows):
    own, width = panel.shape
    half = far.shape[1]
    gram_rows = len(gram_blocks[0]) * tile
    sent_rows = half + max(shares) * chip_count
    whole = lambda shape: pl.BlockSpec(shape, lambda i, place: (0, 0))
    return pl.pallas_call(
        functools.partial(products_kernel, total_rows=total_rows),
        out_shape=[jax.ShapeDtypeStruct((sent_rows, tile), jnp.float32)] * classes,
        grid_spec=pltpu.PrefetchScalarGridSpec(
            num_scalar_prefetch=1,
            grid=(1,),
            in_specs=[
                whole((own, width)),
                whole((own, width)),
                pl.BlockSpec((own, half), lambda i, place: (0, place[0])),
                whole((own, half)),
                whole((1, own)),
                whole((1, own)),
            ],
            out_specs=[whole((sent_rows, tile))] * classes,
            scratch_shapes=[
                pltpu.VMEM((width, 2 * own), jnp.float32),
                pltpu.VMEM((2 * own, width), jnp.float32),
                pltpu.VMEM((2 * own, half), jnp.float32),
                pltpu.VMEM((classes, half, tile), jnp.float32),
                pltpu.VMEM((gram_rows, tile), jnp.float32),
                pltpu.VMEM((classes, max(shares) * chip_count, tile), jnp.float32),
            ],
        ),
        compiler_params=pltpu.CompilerParams(vmem_limit_bytes=32 * 1024 * 1024),
    )(place, panel, other, trailing, far, counts, far_counts)


def combine_kernel(*refs, chip_count, chunk):
    parts, out_ref = refs[:classes], refs[classes]
    most = max(shares)
    piece = chunk + most

    def added(at, rows):
        side = slice(at, at + rows)
        return (parts[0][side, :] + parts[1][side, :]) + (parts[2][side, :] + parts[3][side, :])

    for q in range(chip_count):
        gram = added(chip_count * chunk + q * most, most)
        out_ref[q * piece : (q + 1) * piece, :] = jnp.concatenate([gram, added(q * chunk, chunk)], 0)


def combine(parts, chip_count, chunk):
    vmem = pl.BlockSpec(memory_space=pltpu.VMEM)
    return pl.pallas_call(
        functools.partial(combine_kernel, chip_count=chip_count, chunk=chunk),
        out_shape=jax.ShapeDtypeStruct(parts[0].shape, jnp.float32),
        in_specs=[vmem] * classes,
        out_specs=vmem,
        compiler_params=pltpu.CompilerParams(vmem_limit_bytes=16 * 1024 * 1024),
    )(*parts)


def sum_kernel(pieces_ref, copies_ref, total_ref, *, chunk, kinds):
    most = max(shares)
    piece = chunk + most
    both = chunk + sum(shares)
    for k in range(classes):
        total = None
        for q, kind in enumerate(kinds):
            if kind == k:
                part = pieces_ref[q * piece : (q + 1) * piece, :]
                total = part if total is None else total + part
        total_ref[k, 0:piece, :] = total
    gram = [total_ref[k, 0:share, :] for k, share in enumerate(shares)]
    for k in range(classes):
        copy = jnp.concatenate(gram + [total_ref[k, most:piece, :]], 0)
        for q, kind in enumerate(kinds):
            if kind == k:
                copies_ref[q * both : (q + 1) * both, :] = copy


def sum_pieces(pieces, chunk, kinds):
    vmem = pl.BlockSpec(memory_space=pltpu.VMEM)
    return pl.pallas_call(
        functools.partial(sum_kernel, chunk=chunk, kinds=kinds),
        out_shape=jax.ShapeDtypeStruct((len(kinds) * (chunk + sum(shares)), tile), jnp.float32),
        in_specs=[vmem],
        out_specs=vmem,
        scratch_shapes=[pltpu.VMEM((classes, chunk + max(shares) + 7, tile), jnp.float32)],
        compiler_params=pltpu.CompilerParams(vmem_limit_bytes=16 * 1024 * 1024),
    )(pieces)


def unpack_kernel(near_ref, far_ref, near_gram, far_gram, quarters_ref, *, chip_count):
    size = near_gram.shape[0] // chip_count
    chunk = quarters_ref.shape[1] // chip_count
    both = size + chunk
    for at, (copies_ref, gram_ref) in enumerate(((near_ref, near_gram), (far_ref, far_gram))):
        for q in range(chip_count):
            at_row, first = q * both, 0
            for share in shares:
                gram_ref[first + q * share : first + (q + 1) * share, :] = copies_ref[at_row : at_row + share, :]
                at_row += share
                first += chip_count * share
            quarters_ref[at, q * chunk : (q + 1) * chunk, :] = copies_ref[q * both + size : (q + 1) * both, :]


def unpack(near, far, chip_count, size, chunk):
    vmem = pl.BlockSpec(memory_space=pltpu.VMEM)
    gram = jax.ShapeDtypeStruct((chip_count * size, tile), jnp.float32)
    return pl.pallas_call(
        functools.partial(unpack_kernel, chip_count=chip_count),
        out_shape=(gram, gram, jax.ShapeDtypeStruct((2, chip_count * chunk, tile), jnp.float32)),
        in_specs=[vmem] * 2,
        out_specs=[vmem] * 3,
        compiler_params=pltpu.CompilerParams(vmem_limit_bytes=16 * 1024 * 1024),
    )(near, far)


def factor_kernel(place_ref, near_ref, far_ref, panel_ref, mixed_ref, r_ref, a_ref, upper, linv, rows_ref, y_ref, w_ref, z_ref, work):
    rows = lax.broadcasted_iota(jnp.int32, (tile, tile), 0)
    cols = lax.broadcasted_iota(jnp.int32, (tile, tile), 1)
    eye = jnp.where(rows == cols, 1.0, 0.0).astype(jnp.float32)
    own, width = panel_ref.shape
    picked = r_ref.shape[0]
    for core, blocks in enumerate(gram_blocks):
        for at, (i, j) in enumerate(blocks):
            side = slice(at * tile, (at + 1) * tile)
            block = jnp.where(place_ref[0] == core, near_ref[side, :], far_ref[side, :])
            if i == j:
                block = block + ridge_shift * eye
            a_ref[i * tile : (i + 1) * tile, j * tile : (j + 1) * tile] = block
    upper[...] = jnp.zeros_like(upper)
    linv[...] = jnp.zeros_like(linv)
    z_ref[...] = jnp.zeros_like(z_ref)
    rows_ref[...] = panel_ref[...]
    work[:, 0:tile] = a_ref[0:tile, 0:tile]
    work[:, tile:] = eye
    later = []
    for b in range(0, width, tile):
        e = b + tile
        n = e + tile
        factor_diagonal(work, later)
        while later:
            later.pop(0)()
        inverse = work[:, tile:]
        diagonal = work[:, 0:tile]
        if e == width:
            upper[b:e, b:e] = jnp.where(cols >= rows, diagonal, 0.0)
            y = stacked(rows_ref[:, b:e], inverse, 1, 1)
            last = jnp.concatenate([-stacked(inverse, w_ref[:, 0:b]), inverse], 1)
            linv[b:e, :] = last
            z_ref[...] = z_ref[...] + stacked(y, last)
            break
        beside = stacked(inverse, a_ref[b:e, e:n])
        work[:, 0:tile] = a_ref[e:n, e:n] - stacked(beside, beside, 0, 0)
        work[:, tile:] = eye

        def rows_of_tiles(b=b, e=e, n=n, inverse=inverse, diagonal=diagonal, beside=beside):
            upper[b:e, b:e] = jnp.where(cols >= rows, diagonal, 0.0)
            upper[b:e, e:n] = beside
            linv[b:e, b:e] = inverse
            if b:
                linv[b:e, 0:b] = -stacked(inverse, w_ref[:, 0:b])
            y_ref[:, b:e] = stacked(rows_ref[:, b:e], inverse, 1, 1)
            if n < width:
                upper[b:e, n:] = stacked(inverse, a_ref[b:e, n:])

        def remainder(b=b, e=e, n=n, beside=beside):
            right = upper[b:e, e:]
            if n < width:
                a_ref[e:n, n:] = a_ref[e:n, n:] - stacked(beside, right[:, tile:], 0, 0)
            for c in range(n, width, tile):
                a_ref[c : c + tile, c:] = a_ref[c : c + tile, c:] - stacked(
                    right[:, c - e : c - e + tile], right[:, c - e :], 0, 0
                )
            rows_ref[:, e:] = rows_ref[:, e:] - stacked(y_ref[:, b:e], right)

        def inverses(b=b, e=e, n=n):
            w_ref[:, 0:e] = stacked(upper[0:e, e:n], linv[0:e, 0:e], 0, 0)
            z_ref[:, 0:e] = z_ref[:, 0:e] + stacked(y_ref[:, b:e], linv[b:e, 0:e])

        later = [rows_of_tiles, remainder, inverses]
    at = pl.ds(pl.multiple_of(place_ref[1 + classes], picked), picked)
    r_ref[...] = upper[at, :]
    for b in range(0, width, tile):
        mixed_ref[b // tile, 0:own, :] = z_ref[:, b : b + tile]
        mixed_ref[b // tile, own:, :] = linv[at, b : b + tile]


def factor(place, near, far, panel, picked):
    own, width = panel.shape
    vmem = pl.BlockSpec(memory_space=pltpu.VMEM)
    square = pltpu.VMEM((width, width), jnp.float32)
    flat = pltpu.VMEM((own, width), jnp.float32)
    return pl.pallas_call(
        factor_kernel,
        out_shape=(
            jax.ShapeDtypeStruct((width // tile, own + picked, tile), jnp.float32),
            jax.ShapeDtypeStruct((picked, width), jnp.float32),
        ),
        in_specs=[pl.BlockSpec(memory_space=pltpu.SMEM), vmem, vmem, vmem],
        out_specs=(vmem, vmem),
        scratch_shapes=[
            square,
            square,
            square,
            flat,
            flat,
            pltpu.VMEM((tile, width - tile), jnp.float32),
            flat,
            pltpu.VMEM((tile, 2 * tile), jnp.float32),
        ],
        compiler_params=pltpu.CompilerParams(vmem_limit_bytes=20 * 1024 * 1024),
        cost_estimate=pl.CostEstimate(flops=20 * 10**9, bytes_accessed=4 * 10**6, transcendentals=0),
    )(place, near, far, panel)


def finish_kernel(place_ref, mixed_ref, *refs):
    quarters = refs[:classes]
    trail_ref, updated_ref, coupling_ref = refs[classes:]
    own = trail_ref.shape[0]
    half = quarters[0].shape[1]
    core = place_ref[0]
    left = [mixed_ref[place_ref[1 + m]] for m in range(classes)]
    left = [jnp.concatenate(left[m : m + 2], 1) for m in range(0, classes, 2)]
    for c in range(0, half, tile):
        out = None
        for m in range(0, classes, 2):
            right = jnp.concatenate(
                [
                    jnp.concatenate([quarters[m][side, c : c + tile, :], quarters[m + 1][side, c : c + tile, :]], 0)
                    for side in range(2)
                ],
                1,
            )
            term = stacked_two(left[m // 2], right)
            out = term if out is None else out + term
        for part, where in ((out[:, :tile], core), (out[:, tile:], 1 - core)):
            at = pl.ds(pl.multiple_of(where * half + c, tile), tile)
            updated_ref[:, at] = trail_ref[:, at] - part[:own]
            coupling_ref[:, at] = part[own:]


def finish(place, mixed, quarters, trailing):
    vmem = pl.BlockSpec(memory_space=pltpu.VMEM)
    own, trail = trailing.shape
    return pl.pallas_call(
        finish_kernel,
        out_shape=(
            jax.ShapeDtypeStruct((own, trail), jnp.float32),
            jax.ShapeDtypeStruct((mixed.shape[1] - own, trail), jnp.float32),
        ),
        in_specs=[pl.BlockSpec(memory_space=pltpu.SMEM)] + [vmem] * (2 + classes),
        out_specs=(vmem, vmem),
        compiler_params=pltpu.CompilerParams(vmem_limit_bytes=32 * 1024 * 1024),
    )(place, mixed, *quarters, trailing)


def kind_of(x, y, z):
    return (x % 2) ^ (2 * (y % 2)) ^ (3 * (z % 2))


def local(panel, trailing, counts):
    own, width = panel.shape
    half = trailing.shape[1] // 2
    depth = lax.axis_size("z")
    groups = lax.axis_size("grp")
    side = 4
    members = 2 * depth
    chip_count = groups * depth
    chunk = half // chip_count
    gram_chunk = sum(shares)
    kinds = [kind_of(g % side, g // side, z) for g in range(groups) for z in range(depth)]
    group, z, core = lax.axis_index("grp"), lax.axis_index("z"), lax.axis_index("core")
    kind = kind_of(group % side, group // side, z)
    picked = width // members
    start = (z * 2 + core) * picked
    place = jnp.stack([core] + [kind ^ m for m in range(classes)] + [start]).astype(jnp.int32)
    swap = [(0, 1), (1, 0)]
    count_row = counts[None, :]
    sent_trail = lax.dynamic_slice_in_dim(trailing, (1 - core) * half, half, 1)
    with jax.named_scope("swap_inputs"):
        far_counts = lax.ppermute(count_row, "core", swap)
        other_panel = lax.ppermute(panel, "core", swap)
        far_trail = lax.ppermute(sent_trail, "core", swap)
    with jax.named_scope("local_products"):
        terms = products(
            place, panel, other_panel, trailing, far_trail, count_row, far_counts, chip_count, own * groups * members
        )
    def pairs(before, after):
        out = []
        for a in range(before):
            for i in range(side):
                for b in range(after):
                    for c in range(2):
                        to = i ^ (3 if c else 1)
                        out.append((((a * side + i) * after + b) * 2 + c, ((a * side + to) * after + b) * 2 + c))
        return out

    along = (
        ("along_x", ("grp", "core"), groups // side, 1),
        ("along_y", ("grp", "core"), 1, side),
        ("along_z", ("z", "core"), 1, 1),
    )

    def exchange(rows):
        with jax.named_scope("exchange"):
            rows = lax.all_to_all(rows.reshape(chip_count, 1, -1), chips, 0, 0, tiled=True)
        return rows.reshape(-1, tile)

    parts = [terms[0]]
    for m, (name, axis, before, after) in enumerate(along):
        with jax.named_scope("terms_" + name):
            parts.append(lax.ppermute(terms[1 + m], axis, pairs(before, after)))
    with jax.named_scope("combine_terms"):
        pieces = combine(parts, chip_count, chunk)
    pieces = exchange(pieces)
    with jax.named_scope("sum_pieces"):
        copies = sum_pieces(pieces, chunk, kinds)
    copies = exchange(copies)
    with jax.named_scope("swap_copies"):
        far_copies = lax.ppermute(copies, "core", swap)
    with jax.named_scope("unpack_sums"):
        near_gram, far_gram, quarter = unpack(copies, far_copies, chip_count, gram_chunk, chunk)
    quarters = [quarter]
    for name, axis, before, after in along:
        with jax.named_scope("quarters_" + name):
            quarters.append(lax.ppermute(quarter, axis, pairs(before, after)))
    with jax.named_scope("factor_gram"):
        mixed, r_rows = factor(place, near_gram, far_gram, panel, picked)
    with jax.named_scope("apply_factor"):
        updated, coupling = finish(place, mixed, quarters, trailing)
    return (r_rows, coupling, updated)


def solution(mesh):
    groups, members = mesh.devices.shape
    split = Mesh(mesh.devices.reshape(groups, members // 2, 2), ("grp", "z", "core"))
    rows = P(("grp", "z", "core"))
    return jax.shard_map(
        local,
        mesh=split,
        in_specs=(P(("grp", "z", "core"), None), P(("grp", "z", "core"), None), rows),
        out_specs=(P(("z", "core"), None), P(("z", "core"), None), P(("grp", "z", "core"), None)),
        check_vma=False,
    )
```

```python
import functools

import jax
import jax.numpy as jnp
from jax import lax
from jax.experimental import pallas as pl
from jax.experimental.pallas import tpu as pltpu
from jax.sharding import Mesh, PartitionSpec as P

ridge_shift = 0.05
HIGHEST = lax.Precision.HIGHEST
tile = 128
strip = 32
half_strip = 16
chips = ("grp", "z")
classes = 4
shares = (3, 3, 2, 2)


def product(left, right, left_dim=1, right_dim=0):
    return lax.dot_general(
        left,
        right,
        (((left_dim,), (right_dim,)), ((), ())),
        precision=HIGHEST,
        preferred_element_type=jnp.float32,
    )


def three_parts(x):
    high = x.astype(jnp.bfloat16)
    rest = x - high.astype(jnp.float32)
    middle = rest.astype(jnp.bfloat16)
    return high, middle, (rest - middle.astype(jnp.float32)).astype(jnp.bfloat16)


def stacked(left, right, left_dim=1, right_dim=0):
    lh, lm, ll = three_parts(left)
    rh, rm, rl = three_parts(right)
    return lax.dot_general(
        jnp.concatenate([lh, lh, lm, lh, ll, lm], left_dim),
        jnp.concatenate([rh, rm, rh, rl, rh, rm], right_dim),
        (((left_dim,), (right_dim,)), ((), ())),
        preferred_element_type=jnp.float32,
    )


def stacked_two(left, right, left_dim=1, right_dim=0):
    lh, ll, _ = three_parts(left)
    rh, rl, _ = three_parts(right)
    return lax.dot_general(
        jnp.concatenate([lh, lh, ll], left_dim),
        jnp.concatenate([rh, rl, rh], right_dim),
        (((left_dim,), (right_dim,)), ((), ())),
        preferred_element_type=jnp.float32,
    )


def factor_diagonal(work, later):
    sub = lax.broadcasted_iota(jnp.int32, (8, tile), 0)
    groups = strip // 8

    def spread_row(array, row):
        return jnp.broadcast_to(array[row : row + 1, :], (8, tile))

    for r in range(0, tile, strip):
        left = [work[r + 8 * g : r + 8 * g + 8, 0:tile] for g in range(groups)]
        right = [work[r + 8 * g : r + 8 * g + 8, tile : 2 * tile] for g in range(groups)]
        pivots = [jnp.ones((8, tile), jnp.float32)] * groups
        if later:
            later.pop(0)()
        for first in range(0, strip, half_strip):
            col = {}
            for c in range(first, first + half_strip):
                for g in range(c // 8, groups):
                    col[c, g] = jnp.broadcast_to(left[g][:, r + c : r + c + 1], (8, tile))
            for k in range(first, first + half_strip):
                at, row = k // 8, k % 8
                pivot = spread_row(col[k, at], row)
                inv = 1.0 / pivot
                pivots[at] = jnp.where(sub == row, pivot, pivots[at])
                low = {g: col[k, g] * inv for g in range(at, groups)}
                for c in range(k + 1, first + half_strip):
                    factor_c = spread_row(col[k, c // 8], c % 8)
                    for g in range(c // 8, groups):
                        if c == k + 1 and g == c // 8:
                            col[c, g] = col[c, g] - (col[k, g] * factor_c) * inv
                        else:
                            col[c, g] = col[c, g] - low[g] * factor_c
                below = jnp.where(sub > row, low[at], 0.0)
                for side in (left, right):
                    pivot_row = spread_row(side[at], row)
                    side[at] = side[at] - below * pivot_row
                    for g in range(at + 1, groups):
                        side[g] = side[g] - low[g] * pivot_row
        for g in range(groups):
            scale = lax.rsqrt(pivots[g])
            left[g] = left[g] * scale
            right[g] = right[g] * scale
        new_left = jnp.concatenate(left, 0)
        new_right = jnp.concatenate(right, 0)
        work[r : r + strip, 0:tile] = new_left
        work[r : r + strip, tile : 2 * tile] = new_right
        if r + strip < tile:
            update = stacked(new_left, jnp.concatenate([new_left, new_right], 1), 0, 0)
            work[r + strip : tile, :] = work[r + strip : tile, :] - update[r + strip : tile, :]


gram_blocks = (((0, 0), (1, 1), (0, 1), (0, 2), (0, 3)), ((2, 2), (3, 3), (2, 3), (1, 2), (1, 3)))


def weigh(rows, trail, count, total_rows, at, pt, wp, wt):
    own, width = rows.shape
    weight = jnp.transpose(jnp.broadcast_to(count[...].astype(jnp.float32) / total_rows, (own, own)))
    for c in range(0, width, tile):
        block = rows[:, c : c + tile]
        pt[c : c + tile, at : at + own] = jnp.transpose(block)
        wp[at : at + own, c : c + tile] = block * weight
    for c in range(0, trail.shape[1], tile):
        wt[at : at + own, c : c + tile] = trail[:, c : c + tile] * weight


def prepare_kernel(place_ref, panel_ref, trail_ref, counts_ref, pt, wp, wt, *, total_rows):
    weigh(panel_ref, trail_ref, counts_ref, total_rows, 0, pt, wp, wt)


def prepare(place, panel, trailing, counts, total_rows):
    own, width = panel.shape
    half = trailing.shape[1] // 2
    whole = lambda shape: pl.BlockSpec(shape, lambda i, place: (0, 0))
    shapes = [(width, own), (own, width), (own, half)]
    return pl.pallas_call(
        functools.partial(prepare_kernel, total_rows=total_rows),
        out_shape=[jax.ShapeDtypeStruct(shape, jnp.float32) for shape in shapes],
        grid_spec=pltpu.PrefetchScalarGridSpec(
            num_scalar_prefetch=1,
            grid=(1,),
            in_specs=[
                whole((own, width)),
                pl.BlockSpec((own, half), lambda i, place: (0, place[0])),
                whole((1, own)),
            ],
            out_specs=[whole(shape) for shape in shapes],
        ),
        compiler_params=pltpu.CompilerParams(vmem_limit_bytes=16 * 1024 * 1024),
    )(place, panel, trailing, counts)


def products_kernel(place_ref, own_pt, own_wp, own_wt, other_ref, far_ref, far_counts_ref, *refs, total_rows):
    outs, (pt, wp, wt, quarters, gram, shared) = refs[:classes], refs[classes:]
    core = place_ref[0]
    own = other_ref.shape[0]
    half = far_ref.shape[1]
    pt[:, 0:own] = own_pt[...]
    wp[0:own, :] = own_wp[...]
    wt[0:own, :] = own_wt[...]
    weigh(other_ref, far_ref, far_counts_ref, total_rows, own, pt, wp, wt)
    step = 2 * tile
    for c in range(0, half, step):
        n = min(step, half - c)
        part = stacked_two(pt[...], wt[:, c : c + n])
        for k in range(classes):
            for j in range(0, n, tile):
                quarters[k, c + j : c + j + tile, :] = part[k * tile : (k + 1) * tile, j : j + tile]
    near = pl.multiple_of(core * step, tile)
    first = product(pt[pl.ds(near, tile), :], wp[:, pl.ds(near, step)])
    gram[0:tile, :] = first[:, :tile]
    gram[2 * tile : 3 * tile, :] = first[:, tile:]
    near = pl.multiple_of(core * step + tile, tile)
    gram[tile : 2 * tile, :] = product(pt[pl.ds(near, tile), :], wp[:, pl.ds(near, tile)])
    near = pl.multiple_of(core * tile, tile)
    last = product(pt[pl.ds(near, tile), :], wp[:, step:])
    gram[3 * tile : 4 * tile, :] = last[:, :tile]
    gram[4 * tile :, :] = last[:, tile:]
    most = max(shares)
    chip_count = shared.shape[1] // most
    first = 0
    for k, share in enumerate(shares):
        if share == most:
            shared[k] = gram[first : first + chip_count * share, :]
        else:
            shared[k] = jnp.zeros_like(shared[k])
            for q in range(chip_count):
                shared[k, q * most : q * most + share, :] = gram[first + q * share : first + (q + 1) * share, :]
        first += chip_count * share
    for m in range(classes):
        outs[m][0:half, :] = quarters[place_ref[1 + m]]
        outs[m][half:, :] = shared[place_ref[1 + m]]


def products(place, prepared, other, far, far_counts, chip_count, total_rows):
    own, width = other.shape
    half = far.shape[1]
    gram_rows = len(gram_blocks[0]) * tile
    sent_rows = half + max(shares) * chip_count
    whole = lambda shape: pl.BlockSpec(shape, lambda i, place: (0, 0))
    return pl.pallas_call(
        functools.partial(products_kernel, total_rows=total_rows),
        out_shape=[jax.ShapeDtypeStruct((sent_rows, tile), jnp.float32)] * classes,
        grid_spec=pltpu.PrefetchScalarGridSpec(
            num_scalar_prefetch=1,
            grid=(1,),
            in_specs=[
                whole((width, own)),
                whole((own, width)),
                whole((own, half)),
                whole((own, width)),
                whole((own, half)),
                whole((1, own)),
            ],
            out_specs=[whole((sent_rows, tile))] * classes,
            scratch_shapes=[
                pltpu.VMEM((width, 2 * own), jnp.float32),
                pltpu.VMEM((2 * own, width), jnp.float32),
                pltpu.VMEM((2 * own, half), jnp.float32),
                pltpu.VMEM((classes, half, tile), jnp.float32),
                pltpu.VMEM((gram_rows, tile), jnp.float32),
                pltpu.VMEM((classes, max(shares) * chip_count, tile), jnp.float32),
            ],
        ),
        compiler_params=pltpu.CompilerParams(vmem_limit_bytes=32 * 1024 * 1024),
    )(place, *prepared, other, far, far_counts)


def combine_kernel(*refs, chip_count, chunk):
    parts, out_ref = refs[:classes], refs[classes]
    most = max(shares)
    piece = chunk + most

    def added(at, rows):
        side = slice(at, at + rows)
        return (parts[0][side, :] + parts[1][side, :]) + (parts[2][side, :] + parts[3][side, :])

    for q in range(chip_count):
        gram = added(chip_count * chunk + q * most, most)
        out_ref[q * piece : (q + 1) * piece, :] = jnp.concatenate([gram, added(q * chunk, chunk)], 0)


def combine(parts, chip_count, chunk):
    vmem = pl.BlockSpec(memory_space=pltpu.VMEM)
    return pl.pallas_call(
        functools.partial(combine_kernel, chip_count=chip_count, chunk=chunk),
        out_shape=jax.ShapeDtypeStruct(parts[0].shape, jnp.float32),
        in_specs=[vmem] * classes,
        out_specs=vmem,
        compiler_params=pltpu.CompilerParams(vmem_limit_bytes=16 * 1024 * 1024),
    )(*parts)


def sum_kernel(pieces_ref, copies_ref, total_ref, *, chunk, kinds):
    most = max(shares)
    piece = chunk + most
    both = chunk + sum(shares)
    for k in range(classes):
        total = None
        for q, kind in enumerate(kinds):
            if kind == k:
                part = pieces_ref[q * piece : (q + 1) * piece, :]
                total = part if total is None else total + part
        total_ref[k, 0:piece, :] = total
    gram = [total_ref[k, 0:share, :] for k, share in enumerate(shares)]
    for k in range(classes):
        copy = jnp.concatenate(gram + [total_ref[k, most:piece, :]], 0)
        for q, kind in enumerate(kinds):
            if kind == k:
                copies_ref[q * both : (q + 1) * both, :] = copy


def sum_pieces(pieces, chunk, kinds):
    vmem = pl.BlockSpec(memory_space=pltpu.VMEM)
    return pl.pallas_call(
        functools.partial(sum_kernel, chunk=chunk, kinds=kinds),
        out_shape=jax.ShapeDtypeStruct((len(kinds) * (chunk + sum(shares)), tile), jnp.float32),
        in_specs=[vmem],
        out_specs=vmem,
        scratch_shapes=[pltpu.VMEM((classes, chunk + max(shares) + 7, tile), jnp.float32)],
        compiler_params=pltpu.CompilerParams(vmem_limit_bytes=16 * 1024 * 1024),
    )(pieces)


def unpack_kernel(near_ref, far_ref, near_gram, far_gram, quarters_ref, *, chip_count):
    size = near_gram.shape[0] // chip_count
    chunk = quarters_ref.shape[1] // chip_count
    both = size + chunk
    for at, (copies_ref, gram_ref) in enumerate(((near_ref, near_gram), (far_ref, far_gram))):
        for q in range(chip_count):
            at_row, first = q * both, 0
            for share in shares:
                gram_ref[first + q * share : first + (q + 1) * share, :] = copies_ref[at_row : at_row + share, :]
                at_row += share
                first += chip_count * share
            quarters_ref[at, q * chunk : (q + 1) * chunk, :] = copies_ref[q * both + size : (q + 1) * both, :]


def unpack(near, far, chip_count, size, chunk):
    vmem = pl.BlockSpec(memory_space=pltpu.VMEM)
    gram = jax.ShapeDtypeStruct((chip_count * size, tile), jnp.float32)
    return pl.pallas_call(
        functools.partial(unpack_kernel, chip_count=chip_count),
        out_shape=(gram, gram, jax.ShapeDtypeStruct((2, chip_count * chunk, tile), jnp.float32)),
        in_specs=[vmem] * 2,
        out_specs=[vmem] * 3,
        compiler_params=pltpu.CompilerParams(vmem_limit_bytes=16 * 1024 * 1024),
    )(near, far)


def factor_kernel(place_ref, near_ref, far_ref, panel_ref, mixed_ref, r_ref, a_ref, upper, linv, rows_ref, y_ref, w_ref, z_ref, work):
    rows = lax.broadcasted_iota(jnp.int32, (tile, tile), 0)
    cols = lax.broadcasted_iota(jnp.int32, (tile, tile), 1)
    eye = jnp.where(rows == cols, 1.0, 0.0).astype(jnp.float32)
    own, width = panel_ref.shape
    picked = r_ref.shape[0]
    for core, blocks in enumerate(gram_blocks):
        for at, (i, j) in enumerate(blocks):
            side = slice(at * tile, (at + 1) * tile)
            block = jnp.where(place_ref[0] == core, near_ref[side, :], far_ref[side, :])
            if i == j:
                block = block + ridge_shift * eye
            a_ref[i * tile : (i + 1) * tile, j * tile : (j + 1) * tile] = block
    upper[...] = jnp.zeros_like(upper)
    linv[...] = jnp.zeros_like(linv)
    z_ref[...] = jnp.zeros_like(z_ref)
    rows_ref[...] = panel_ref[...]
    work[:, 0:tile] = a_ref[0:tile, 0:tile]
    work[:, tile:] = eye
    later = []
    for b in range(0, width, tile):
        e = b + tile
        n = e + tile
        factor_diagonal(work, later)
        while later:
            later.pop(0)()
        inverse = work[:, tile:]
        diagonal = work[:, 0:tile]
        if e == width:
            upper[b:e, b:e] = jnp.where(cols >= rows, diagonal, 0.0)
            y = stacked(rows_ref[:, b:e], inverse, 1, 1)
            last = jnp.concatenate([-stacked(inverse, w_ref[:, 0:b]), inverse], 1)
            linv[b:e, :] = last
            z_ref[...] = z_ref[...] + stacked(y, last)
            break
        beside = stacked(inverse, a_ref[b:e, e:n])
        work[:, 0:tile] = a_ref[e:n, e:n] - stacked(beside, beside, 0, 0)
        work[:, tile:] = eye

        def rows_of_tiles(b=b, e=e, n=n, inverse=inverse, diagonal=diagonal, beside=beside):
            upper[b:e, b:e] = jnp.where(cols >= rows, diagonal, 0.0)
            upper[b:e, e:n] = beside
            linv[b:e, b:e] = inverse
            if b:
                linv[b:e, 0:b] = -stacked(inverse, w_ref[:, 0:b])
            y_ref[:, b:e] = stacked(rows_ref[:, b:e], inverse, 1, 1)
            if n < width:
                upper[b:e, n:] = stacked(inverse, a_ref[b:e, n:])

        def remainder(b=b, e=e, n=n, beside=beside):
            right = upper[b:e, e:]
            if n < width:
                a_ref[e:n, n:] = a_ref[e:n, n:] - stacked(beside, right[:, tile:], 0, 0)
            for c in range(n, width, tile):
                a_ref[c : c + tile, c:] = a_ref[c : c + tile, c:] - stacked(
                    right[:, c - e : c - e + tile], right[:, c - e :], 0, 0
                )
            rows_ref[:, e:] = rows_ref[:, e:] - stacked(y_ref[:, b:e], right)

        def inverses(b=b, e=e, n=n):
            w_ref[:, 0:e] = stacked(upper[0:e, e:n], linv[0:e, 0:e], 0, 0)
            z_ref[:, 0:e] = z_ref[:, 0:e] + stacked(y_ref[:, b:e], linv[b:e, 0:e])

        later = [rows_of_tiles, remainder, inverses]
    at = pl.ds(pl.multiple_of(place_ref[1 + classes], picked), picked)
    r_ref[...] = upper[at, :]
    for b in range(0, width, tile):
        mixed_ref[b // tile, 0:own, :] = z_ref[:, b : b + tile]
        mixed_ref[b // tile, own:, :] = linv[at, b : b + tile]


def factor(place, near, far, panel, picked):
    own, width = panel.shape
    vmem = pl.BlockSpec(memory_space=pltpu.VMEM)
    square = pltpu.VMEM((width, width), jnp.float32)
    flat = pltpu.VMEM((own, width), jnp.float32)
    return pl.pallas_call(
        factor_kernel,
        out_shape=(
            jax.ShapeDtypeStruct((width // tile, own + picked, tile), jnp.float32),
            jax.ShapeDtypeStruct((picked, width), jnp.float32),
        ),
        in_specs=[pl.BlockSpec(memory_space=pltpu.SMEM), vmem, vmem, vmem],
        out_specs=(vmem, vmem),
        scratch_shapes=[
            square,
            square,
            square,
            flat,
            flat,
            pltpu.VMEM((tile, width - tile), jnp.float32),
            flat,
            pltpu.VMEM((tile, 2 * tile), jnp.float32),
        ],
        compiler_params=pltpu.CompilerParams(vmem_limit_bytes=20 * 1024 * 1024),
        cost_estimate=pl.CostEstimate(flops=20 * 10**9, bytes_accessed=4 * 10**6, transcendentals=0),
    )(place, near, far, panel)


def finish_kernel(place_ref, mixed_ref, *refs):
    quarters = refs[:classes]
    trail_ref, updated_ref, coupling_ref = refs[classes:]
    own = trail_ref.shape[0]
    half = quarters[0].shape[1]
    core = place_ref[0]
    left = [mixed_ref[place_ref[1 + m]] for m in range(classes)]
    left = [jnp.concatenate(left[m : m + 2], 1) for m in range(0, classes, 2)]
    for c in range(0, half, tile):
        out = None
        for m in range(0, classes, 2):
            right = jnp.concatenate(
                [
                    jnp.concatenate([quarters[m][side, c : c + tile, :], quarters[m + 1][side, c : c + tile, :]], 0)
                    for side in range(2)
                ],
                1,
            )
            term = stacked_two(left[m // 2], right)
            out = term if out is None else out + term
        for part, where in ((out[:, :tile], core), (out[:, tile:], 1 - core)):
            at = pl.ds(pl.multiple_of(where * half + c, tile), tile)
            updated_ref[:, at] = trail_ref[:, at] - part[:own]
            coupling_ref[:, at] = part[own:]


def finish(place, mixed, quarters, trailing):
    vmem = pl.BlockSpec(memory_space=pltpu.VMEM)
    own, trail = trailing.shape
    return pl.pallas_call(
        finish_kernel,
        out_shape=(
            jax.ShapeDtypeStruct((own, trail), jnp.float32),
            jax.ShapeDtypeStruct((mixed.shape[1] - own, trail), jnp.float32),
        ),
        in_specs=[pl.BlockSpec(memory_space=pltpu.SMEM)] + [vmem] * (2 + classes),
        out_specs=(vmem, vmem),
        compiler_params=pltpu.CompilerParams(vmem_limit_bytes=32 * 1024 * 1024),
    )(place, mixed, *quarters, trailing)


def kind_of(x, y, z):
    return (x % 2) ^ (2 * (y % 2)) ^ (3 * (z % 2))


def local(panel, trailing, counts):
    own, width = panel.shape
    half = trailing.shape[1] // 2
    depth = lax.axis_size("z")
    groups = lax.axis_size("grp")
    side = 4
    members = 2 * depth
    chip_count = groups * depth
    chunk = half // chip_count
    gram_chunk = sum(shares)
    kinds = [kind_of(g % side, g // side, z) for g in range(groups) for z in range(depth)]
    group, z, core = lax.axis_index("grp"), lax.axis_index("z"), lax.axis_index("core")
    kind = kind_of(group % side, group // side, z)
    picked = width // members
    start = (z * 2 + core) * picked
    place = jnp.stack([core] + [kind ^ m for m in range(classes)] + [start]).astype(jnp.int32)
    swap = [(0, 1), (1, 0)]
    count_row = counts[None, :]
    sent_trail = lax.dynamic_slice_in_dim(trailing, (1 - core) * half, half, 1)
    with jax.named_scope("swap_inputs"):
        far_counts = lax.ppermute(count_row, "core", swap)
        other_panel = lax.ppermute(panel, "core", swap)
        far_trail = lax.ppermute(sent_trail, "core", swap)
    with jax.named_scope("own_operands"):
        prepared = prepare(place, panel, trailing, count_row, own * groups * members)
    with jax.named_scope("local_products"):
        terms = products(place, prepared, other_panel, far_trail, far_counts, chip_count, own * groups * members)
    def pairs(before, after):
        out = []
        for a in range(before):
            for i in range(side):
                for b in range(after):
                    for c in range(2):
                        to = i ^ (3 if c else 1)
                        out.append((((a * side + i) * after + b) * 2 + c, ((a * side + to) * after + b) * 2 + c))
        return out

    along = (
        ("along_x", ("grp", "core"), groups // side, 1),
        ("along_y", ("grp", "core"), 1, side),
        ("along_z", ("z", "core"), 1, 1),
    )

    def exchange(rows):
        with jax.named_scope("exchange"):
            rows = lax.all_to_all(rows.reshape(chip_count, 1, -1), chips, 0, 0, tiled=True)
        return rows.reshape(-1, tile)

    parts = [terms[0]]
    for m, (name, axis, before, after) in enumerate(along):
        with jax.named_scope("terms_" + name):
            parts.append(lax.ppermute(terms[1 + m], axis, pairs(before, after)))
    with jax.named_scope("combine_terms"):
        pieces = combine(parts, chip_count, chunk)
    pieces = exchange(pieces)
    with jax.named_scope("sum_pieces"):
        copies = sum_pieces(pieces, chunk, kinds)
    copies = exchange(copies)
    with jax.named_scope("swap_copies"):
        far_copies = lax.ppermute(copies, "core", swap)
    with jax.named_scope("unpack_sums"):
        near_gram, far_gram, quarter = unpack(copies, far_copies, chip_count, gram_chunk, chunk)
    quarters = [quarter]
    for name, axis, before, after in along:
        with jax.named_scope("quarters_" + name):
            quarters.append(lax.ppermute(quarter, axis, pairs(before, after)))
    with jax.named_scope("factor_gram"):
        mixed, r_rows = factor(place, near_gram, far_gram, panel, picked)
    with jax.named_scope("apply_factor"):
        updated, coupling = finish(place, mixed, quarters, trailing)
    return (r_rows, coupling, updated)


def solution(mesh):
    groups, members = mesh.devices.shape
    split = Mesh(mesh.devices.reshape(groups, members // 2, 2), ("grp", "z", "core"))
    rows = P(("grp", "z", "core"))
    return jax.shard_map(
        local,
        mesh=split,
        in_specs=(P(("grp", "z", "core"), None), P(("grp", "z", "core"), None), rows),
        out_specs=(P(("z", "core"), None), P(("z", "core"), None), P(("grp", "z", "core"), None)),
        check_vma=False,
    )
```

```python
import functools

import jax
import jax.numpy as jnp
from jax import lax
from jax.experimental import pallas as pl
from jax.experimental.pallas import tpu as pltpu
from jax.sharding import Mesh, PartitionSpec as P

ridge_shift = 0.05
tile = 128
strip = 32
half_strip = 16
chips = ("grp", "z")
classes = 4
shares = (3, 3, 2, 2)


def three_parts(x):
    high = x.astype(jnp.bfloat16)
    rest = x - high.astype(jnp.float32)
    middle = rest.astype(jnp.bfloat16)
    return high, middle, (rest - middle.astype(jnp.float32)).astype(jnp.bfloat16)


def stacked(left, right, left_dim=1, right_dim=0):
    lh, lm, ll = three_parts(left)
    rh, rm, rl = three_parts(right)
    return lax.dot_general(
        jnp.concatenate([lh, lh, lm, lh, ll, lm], left_dim),
        jnp.concatenate([rh, rm, rh, rl, rh, rm], right_dim),
        (((left_dim,), (right_dim,)), ((), ())),
        preferred_element_type=jnp.float32,
    )


def stacked_two(left, right, left_dim=1, right_dim=0):
    lh, ll, _ = three_parts(left)
    rh, rl, _ = three_parts(right)
    return lax.dot_general(
        jnp.concatenate([lh, lh, ll], left_dim),
        jnp.concatenate([rh, rl, rh], right_dim),
        (((left_dim,), (right_dim,)), ((), ())),
        preferred_element_type=jnp.float32,
    )


def factor_diagonal(work, later):
    sub = lax.broadcasted_iota(jnp.int32, (8, tile), 0)
    groups = strip // 8

    def spread_row(array, row):
        return jnp.broadcast_to(array[row : row + 1, :], (8, tile))

    for r in range(0, tile, strip):
        left = [work[r + 8 * g : r + 8 * g + 8, 0:tile] for g in range(groups)]
        right = [work[r + 8 * g : r + 8 * g + 8, tile : 2 * tile] for g in range(groups)]
        pivots = [jnp.ones((8, tile), jnp.float32)] * groups
        if later:
            later.pop(0)()
        for first in range(0, strip, half_strip):
            col = {}
            for c in range(first, first + half_strip):
                for g in range(c // 8, groups):
                    col[c, g] = jnp.broadcast_to(left[g][:, r + c : r + c + 1], (8, tile))
            for k in range(first, first + half_strip):
                at, row = k // 8, k % 8
                pivot = spread_row(col[k, at], row)
                inv = 1.0 / pivot
                pivots[at] = jnp.where(sub == row, pivot, pivots[at])
                low = {g: col[k, g] * inv for g in range(at, groups)}
                for c in range(k + 1, first + half_strip):
                    factor_c = spread_row(col[k, c // 8], c % 8)
                    for g in range(c // 8, groups):
                        if c == k + 1 and g == c // 8:
                            col[c, g] = col[c, g] - (col[k, g] * factor_c) * inv
                        else:
                            col[c, g] = col[c, g] - low[g] * factor_c
                below = jnp.where(sub > row, low[at], 0.0)
                for side in (left, right):
                    pivot_row = spread_row(side[at], row)
                    side[at] = side[at] - below * pivot_row
                    for g in range(at + 1, groups):
                        side[g] = side[g] - low[g] * pivot_row
        for g in range(groups):
            scale = lax.rsqrt(pivots[g])
            left[g] = left[g] * scale
            right[g] = right[g] * scale
        new_left = jnp.concatenate(left, 0)
        new_right = jnp.concatenate(right, 0)
        work[r : r + strip, 0:tile] = new_left
        work[r : r + strip, tile : 2 * tile] = new_right
        if r + strip < tile:
            update = stacked(new_left, jnp.concatenate([new_left, new_right], 1), 0, 0)
            work[r + strip : tile, :] = work[r + strip : tile, :] - update[r + strip : tile, :]


gram_blocks = (((0, 0), (1, 1), (0, 1), (0, 2), (0, 3)), ((2, 2), (3, 3), (2, 3), (1, 2), (1, 3)))


def weigh(rows, trail, count, total_rows, at, pt, wp, wt):
    own, width = rows.shape
    weight = jnp.transpose(jnp.broadcast_to(count[...].astype(jnp.float32) / total_rows, (own, own)))
    for c in range(0, width, tile):
        block = rows[:, c : c + tile]
        pt[c : c + tile, at : at + own] = jnp.transpose(block)
        wp[at : at + own, c : c + tile] = block * weight
    for c in range(0, trail.shape[1], tile):
        wt[at : at + own, c : c + tile] = trail[:, c : c + tile] * weight


def prepare_kernel(place_ref, panel_ref, trail_ref, counts_ref, pt, wp, wt, *, total_rows):
    weigh(panel_ref, trail_ref, counts_ref, total_rows, 0, pt, wp, wt)


def prepare(place, panel, trailing, counts, total_rows):
    own, width = panel.shape
    half = trailing.shape[1] // 2
    whole = lambda shape: pl.BlockSpec(shape, lambda i, place: (0, 0))
    shapes = [(width, own), (own, width), (own, half)]
    return pl.pallas_call(
        functools.partial(prepare_kernel, total_rows=total_rows),
        out_shape=[jax.ShapeDtypeStruct(shape, jnp.float32) for shape in shapes],
        grid_spec=pltpu.PrefetchScalarGridSpec(
            num_scalar_prefetch=1,
            grid=(1,),
            in_specs=[
                whole((own, width)),
                pl.BlockSpec((own, half), lambda i, place: (0, place[0])),
                whole((1, own)),
            ],
            out_specs=[whole(shape) for shape in shapes],
        ),
        compiler_params=pltpu.CompilerParams(vmem_limit_bytes=16 * 1024 * 1024),
    )(place, panel, trailing, counts)


def products_kernel(place_ref, own_pt, own_wp, own_wt, other_ref, far_ref, far_counts_ref, *refs, total_rows):
    outs, (pt, wp, wt, quarters, gram, shared) = refs[:classes], refs[classes:]
    core = place_ref[0]
    own = other_ref.shape[0]
    half = far_ref.shape[1]
    pt[:, 0:own] = own_pt[...]
    wp[0:own, :] = own_wp[...]
    wt[0:own, :] = own_wt[...]
    weigh(other_ref, far_ref, far_counts_ref, total_rows, own, pt, wp, wt)
    step = 2 * tile
    for c in range(0, half, step):
        n = min(step, half - c)
        part = stacked_two(pt[...], wt[:, c : c + n])
        for k in range(classes):
            for j in range(0, n, tile):
                quarters[k, c + j : c + j + tile, :] = part[k * tile : (k + 1) * tile, j : j + tile]
    near = pl.multiple_of(core * step, tile)
    first = stacked(pt[pl.ds(near, tile), :], wp[:, pl.ds(near, step)])
    gram[0:tile, :] = first[:, :tile]
    gram[2 * tile : 3 * tile, :] = first[:, tile:]
    near = pl.multiple_of(core * step + tile, tile)
    gram[tile : 2 * tile, :] = stacked(pt[pl.ds(near, tile), :], wp[:, pl.ds(near, tile)])
    near = pl.multiple_of(core * tile, tile)
    last = stacked(pt[pl.ds(near, tile), :], wp[:, step:])
    gram[3 * tile : 4 * tile, :] = last[:, :tile]
    gram[4 * tile :, :] = last[:, tile:]
    most = max(shares)
    chip_count = shared.shape[1] // most
    first = 0
    for k, share in enumerate(shares):
        if share == most:
            shared[k] = gram[first : first + chip_count * share, :]
        else:
            shared[k] = jnp.zeros_like(shared[k])
            for q in range(chip_count):
                shared[k, q * most : q * most + share, :] = gram[first + q * share : first + (q + 1) * share, :]
        first += chip_count * share
    for m in range(classes):
        outs[m][0:half, :] = quarters[place_ref[1 + m]]
        outs[m][half:, :] = shared[place_ref[1 + m]]


def products(place, prepared, other, far, far_counts, chip_count, total_rows):
    own, width = other.shape
    half = far.shape[1]
    gram_rows = len(gram_blocks[0]) * tile
    sent_rows = half + max(shares) * chip_count
    whole = lambda shape: pl.BlockSpec(shape, lambda i, place: (0, 0))
    return pl.pallas_call(
        functools.partial(products_kernel, total_rows=total_rows),
        out_shape=[jax.ShapeDtypeStruct((sent_rows, tile), jnp.float32)] * classes,
        grid_spec=pltpu.PrefetchScalarGridSpec(
            num_scalar_prefetch=1,
            grid=(1,),
            in_specs=[
                whole((width, own)),
                whole((own, width)),
                whole((own, half)),
                whole((own, width)),
                whole((own, half)),
                whole((1, own)),
            ],
            out_specs=[whole((sent_rows, tile))] * classes,
            scratch_shapes=[
                pltpu.VMEM((width, 2 * own), jnp.float32),
                pltpu.VMEM((2 * own, width), jnp.float32),
                pltpu.VMEM((2 * own, half), jnp.float32),
                pltpu.VMEM((classes, half, tile), jnp.float32),
                pltpu.VMEM((gram_rows, tile), jnp.float32),
                pltpu.VMEM((classes, max(shares) * chip_count, tile), jnp.float32),
            ],
        ),
        compiler_params=pltpu.CompilerParams(vmem_limit_bytes=32 * 1024 * 1024),
    )(place, *prepared, other, far, far_counts)


def combine_kernel(*refs, chip_count, chunk):
    parts, out_ref = refs[:classes], refs[classes]
    most = max(shares)
    piece = chunk + most

    def added(at, rows):
        side = slice(at, at + rows)
        return (parts[0][side, :] + parts[1][side, :]) + (parts[2][side, :] + parts[3][side, :])

    for q in range(chip_count):
        gram = added(chip_count * chunk + q * most, most)
        out_ref[q * piece : (q + 1) * piece, :] = jnp.concatenate([gram, added(q * chunk, chunk)], 0)


def combine(parts, chip_count, chunk):
    vmem = pl.BlockSpec(memory_space=pltpu.VMEM)
    return pl.pallas_call(
        functools.partial(combine_kernel, chip_count=chip_count, chunk=chunk),
        out_shape=jax.ShapeDtypeStruct(parts[0].shape, jnp.float32),
        in_specs=[vmem] * classes,
        out_specs=vmem,
        compiler_params=pltpu.CompilerParams(vmem_limit_bytes=16 * 1024 * 1024),
    )(*parts)


def sum_kernel(pieces_ref, copies_ref, total_ref, *, chunk, kinds):
    most = max(shares)
    piece = chunk + most
    both = chunk + sum(shares)
    for k in range(classes):
        total = None
        for q, kind in enumerate(kinds):
            if kind == k:
                part = pieces_ref[q * piece : (q + 1) * piece, :]
                total = part if total is None else total + part
        total_ref[k, 0:piece, :] = total
    gram = [total_ref[k, 0:share, :] for k, share in enumerate(shares)]
    for k in range(classes):
        copy = jnp.concatenate(gram + [total_ref[k, most:piece, :]], 0)
        for q, kind in enumerate(kinds):
            if kind == k:
                copies_ref[q * both : (q + 1) * both, :] = copy


def sum_pieces(pieces, chunk, kinds):
    vmem = pl.BlockSpec(memory_space=pltpu.VMEM)
    return pl.pallas_call(
        functools.partial(sum_kernel, chunk=chunk, kinds=kinds),
        out_shape=jax.ShapeDtypeStruct((len(kinds) * (chunk + sum(shares)), tile), jnp.float32),
        in_specs=[vmem],
        out_specs=vmem,
        scratch_shapes=[pltpu.VMEM((classes, chunk + max(shares) + 7, tile), jnp.float32)],
        compiler_params=pltpu.CompilerParams(vmem_limit_bytes=16 * 1024 * 1024),
    )(pieces)


def unpack_kernel(near_ref, far_ref, near_gram, far_gram, quarters_ref, *, chip_count):
    size = near_gram.shape[0] // chip_count
    chunk = quarters_ref.shape[1] // chip_count
    both = size + chunk
    for at, (copies_ref, gram_ref) in enumerate(((near_ref, near_gram), (far_ref, far_gram))):
        for q in range(chip_count):
            at_row, first = q * both, 0
            for share in shares:
                gram_ref[first + q * share : first + (q + 1) * share, :] = copies_ref[at_row : at_row + share, :]
                at_row += share
                first += chip_count * share
            quarters_ref[at, q * chunk : (q + 1) * chunk, :] = copies_ref[q * both + size : (q + 1) * both, :]


def unpack(near, far, chip_count, size, chunk):
    vmem = pl.BlockSpec(memory_space=pltpu.VMEM)
    gram = jax.ShapeDtypeStruct((chip_count * size, tile), jnp.float32)
    return pl.pallas_call(
        functools.partial(unpack_kernel, chip_count=chip_count),
        out_shape=(gram, gram, jax.ShapeDtypeStruct((2, chip_count * chunk, tile), jnp.float32)),
        in_specs=[vmem] * 2,
        out_specs=[vmem] * 3,
        compiler_params=pltpu.CompilerParams(vmem_limit_bytes=16 * 1024 * 1024),
    )(near, far)


def factor_kernel(place_ref, near_ref, far_ref, panel_ref, mixed_ref, r_ref, a_ref, upper, linv, rows_ref, y_ref, w_ref, z_ref, work):
    rows = lax.broadcasted_iota(jnp.int32, (tile, tile), 0)
    cols = lax.broadcasted_iota(jnp.int32, (tile, tile), 1)
    eye = jnp.where(rows == cols, 1.0, 0.0).astype(jnp.float32)
    own, width = panel_ref.shape
    picked = r_ref.shape[0]
    def block_of(core, at):
        side = slice(at * tile, (at + 1) * tile)
        block = jnp.where(place_ref[0] == core, near_ref[side, :], far_ref[side, :])
        i, j = gram_blocks[core][at]
        return block + ridge_shift * eye if i == j else block

    def prepare():
        for core, blocks in enumerate(gram_blocks):
            for at, (i, j) in enumerate(blocks):
                if j:
                    a_ref[i * tile : (i + 1) * tile, j * tile : (j + 1) * tile] = block_of(core, at)
        rows_ref[...] = panel_ref[...]
        upper[...] = jnp.zeros_like(upper)
        linv[...] = jnp.zeros_like(linv)
        z_ref[...] = jnp.zeros_like(z_ref)

    work[:, 0:tile] = block_of(0, 0)
    work[:, tile:] = eye
    later = [prepare]
    for b in range(0, width, tile):
        e = b + tile
        n = e + tile
        factor_diagonal(work, later)
        while later:
            later.pop(0)()
        inverse = work[:, tile:]
        diagonal = work[:, 0:tile]
        if e == width:
            upper[b:e, b:e] = jnp.where(cols >= rows, diagonal, 0.0)
            y = stacked(rows_ref[:, b:e], inverse, 1, 1)
            last = jnp.concatenate([-stacked(inverse, w_ref[:, 0:b]), inverse], 1)
            linv[b:e, :] = last
            z_ref[...] = z_ref[...] + stacked_two(y, last)
            break
        beside = stacked(inverse, a_ref[b:e, e:n])
        work[:, 0:tile] = a_ref[e:n, e:n] - stacked(beside, beside, 0, 0)
        work[:, tile:] = eye

        def rows_of_tiles(b=b, e=e, n=n, inverse=inverse, diagonal=diagonal, beside=beside):
            upper[b:e, b:e] = jnp.where(cols >= rows, diagonal, 0.0)
            upper[b:e, e:n] = beside
            linv[b:e, b:e] = inverse
            if b:
                linv[b:e, 0:b] = -stacked(inverse, w_ref[:, 0:b])
            y_ref[:, b:e] = stacked(rows_ref[:, b:e], inverse, 1, 1)
            if n < width:
                upper[b:e, n:] = stacked(inverse, a_ref[b:e, n:])

        def remainder(b=b, e=e, n=n, beside=beside):
            right = upper[b:e, e:]
            if n < width:
                a_ref[e:n, n:] = a_ref[e:n, n:] - stacked(beside, right[:, tile:], 0, 0)
            for c in range(n, width, tile):
                a_ref[c : c + tile, c:] = a_ref[c : c + tile, c:] - stacked(
                    right[:, c - e : c - e + tile], right[:, c - e :], 0, 0
                )
            rows_ref[:, e:] = rows_ref[:, e:] - stacked(y_ref[:, b:e], right)

        def inverses(b=b, e=e, n=n):
            w_ref[:, 0:e] = stacked(upper[0:e, e:n], linv[0:e, 0:e], 0, 0)
            z_ref[:, 0:e] = z_ref[:, 0:e] + stacked_two(y_ref[:, b:e], linv[b:e, 0:e])

        later = [rows_of_tiles, remainder, inverses]
    at = pl.ds(pl.multiple_of(place_ref[1 + classes], picked), picked)
    r_ref[...] = upper[at, :]
    for b in range(0, width, tile):
        mixed_ref[b // tile, 0:own, :] = z_ref[:, b : b + tile]
        mixed_ref[b // tile, own:, :] = linv[at, b : b + tile]


def factor(place, near, far, panel, picked):
    own, width = panel.shape
    vmem = pl.BlockSpec(memory_space=pltpu.VMEM)
    square = pltpu.VMEM((width, width), jnp.float32)
    flat = pltpu.VMEM((own, width), jnp.float32)
    return pl.pallas_call(
        factor_kernel,
        out_shape=(
            jax.ShapeDtypeStruct((width // tile, own + picked, tile), jnp.float32),
            jax.ShapeDtypeStruct((picked, width), jnp.float32),
        ),
        in_specs=[pl.BlockSpec(memory_space=pltpu.SMEM), vmem, vmem, vmem],
        out_specs=(vmem, vmem),
        scratch_shapes=[
            square,
            square,
            square,
            flat,
            flat,
            pltpu.VMEM((tile, width - tile), jnp.float32),
            flat,
            pltpu.VMEM((tile, 2 * tile), jnp.float32),
        ],
        compiler_params=pltpu.CompilerParams(vmem_limit_bytes=20 * 1024 * 1024),
        cost_estimate=pl.CostEstimate(flops=20 * 10**9, bytes_accessed=4 * 10**6, transcendentals=0),
    )(place, near, far, panel)


def finish_kernel(place_ref, mixed_ref, *refs):
    quarters = refs[:classes]
    trail_ref, updated_ref, coupling_ref = refs[classes:]
    own = trail_ref.shape[0]
    half = quarters[0].shape[1]
    core = place_ref[0]
    left = [mixed_ref[place_ref[1 + m]] for m in range(classes)]
    left = [jnp.concatenate(left[m : m + 2], 1) for m in range(0, classes, 2)]
    for c in range(0, half, tile):
        out = None
        for m in range(0, classes, 2):
            right = jnp.concatenate(
                [
                    jnp.concatenate([quarters[m][side, c : c + tile, :], quarters[m + 1][side, c : c + tile, :]], 0)
                    for side in range(2)
                ],
                1,
            )
            term = stacked_two(left[m // 2], right)
            out = term if out is None else out + term
        for part, where in ((out[:, :tile], core), (out[:, tile:], 1 - core)):
            at = pl.ds(pl.multiple_of(where * half + c, tile), tile)
            updated_ref[:, at] = trail_ref[:, at] - part[:own]
            coupling_ref[:, at] = part[own:]


def finish(place, mixed, quarters, trailing):
    vmem = pl.BlockSpec(memory_space=pltpu.VMEM)
    own, trail = trailing.shape
    return pl.pallas_call(
        finish_kernel,
        out_shape=(
            jax.ShapeDtypeStruct((own, trail), jnp.float32),
            jax.ShapeDtypeStruct((mixed.shape[1] - own, trail), jnp.float32),
        ),
        in_specs=[pl.BlockSpec(memory_space=pltpu.SMEM)] + [vmem] * (2 + classes),
        out_specs=(vmem, vmem),
        compiler_params=pltpu.CompilerParams(vmem_limit_bytes=32 * 1024 * 1024),
    )(place, mixed, *quarters, trailing)


def kind_of(x, y, z):
    return (x % 2) ^ (2 * (y % 2)) ^ (3 * (z % 2))


def local(panel, trailing, counts):
    own, width = panel.shape
    half = trailing.shape[1] // 2
    depth = lax.axis_size("z")
    groups = lax.axis_size("grp")
    side = 4
    members = 2 * depth
    chip_count = groups * depth
    chunk = half // chip_count
    gram_chunk = sum(shares)
    kinds = [kind_of(g % side, g // side, z) for g in range(groups) for z in range(depth)]
    group, z, core = lax.axis_index("grp"), lax.axis_index("z"), lax.axis_index("core")
    kind = kind_of(group % side, group // side, z)
    picked = width // members
    start = (z * 2 + core) * picked
    place = jnp.stack([core] + [kind ^ m for m in range(classes)] + [start]).astype(jnp.int32)
    swap = [(0, 1), (1, 0)]
    count_row = counts[None, :]
    sent_trail = lax.dynamic_slice_in_dim(trailing, (1 - core) * half, half, 1)
    with jax.named_scope("swap_inputs"):
        far_counts = lax.ppermute(count_row, "core", swap)
        other_panel = lax.ppermute(panel, "core", swap)
        far_trail = lax.ppermute(sent_trail, "core", swap)
    with jax.named_scope("own_operands"):
        prepared = prepare(place, panel, trailing, count_row, own * groups * members)
    with jax.named_scope("local_products"):
        terms = products(place, prepared, other_panel, far_trail, far_counts, chip_count, own * groups * members)
    def pairs(before, after):
        out = []
        for a in range(before):
            for i in range(side):
                for b in range(after):
                    for c in range(2):
                        to = i ^ (3 if c else 1)
                        out.append((((a * side + i) * after + b) * 2 + c, ((a * side + to) * after + b) * 2 + c))
        return out

    along = (
        ("along_x", ("grp", "core"), groups // side, 1),
        ("along_y", ("grp", "core"), 1, side),
        ("along_z", ("z", "core"), 1, 1),
    )

    def exchange(rows):
        with jax.named_scope("exchange"):
            rows = lax.all_to_all(rows.reshape(chip_count, 1, -1), chips, 0, 0, tiled=True)
        return rows.reshape(-1, tile)

    parts = [terms[0]]
    for m, (name, axis, before, after) in enumerate(along):
        with jax.named_scope("terms_" + name):
            parts.append(lax.ppermute(terms[1 + m], axis, pairs(before, after)))
    with jax.named_scope("combine_terms"):
        pieces = combine(parts, chip_count, chunk)
    pieces = exchange(pieces)
    with jax.named_scope("sum_pieces"):
        copies = sum_pieces(pieces, chunk, kinds)
    copies = exchange(copies)
    with jax.named_scope("swap_copies"):
        far_copies = lax.ppermute(copies, "core", swap)
    with jax.named_scope("unpack_sums"):
        near_gram, far_gram, quarter = unpack(copies, far_copies, chip_count, gram_chunk, chunk)
    quarters = [quarter]
    for name, axis, before, after in along:
        with jax.named_scope("quarters_" + name):
            quarters.append(lax.ppermute(quarter, axis, pairs(before, after)))
    with jax.named_scope("factor_gram"):
        mixed, r_rows = factor(place, near_gram, far_gram, panel, picked)
    with jax.named_scope("apply_factor"):
        updated, coupling = finish(place, mixed, quarters, trailing)
    return (r_rows, coupling, updated)


def solution(mesh):
    groups, members = mesh.devices.shape
    split = Mesh(mesh.devices.reshape(groups, members // 2, 2), ("grp", "z", "core"))
    rows = P(("grp", "z", "core"))
    return jax.shard_map(
        local,
        mesh=split,
        in_specs=(P(("grp", "z", "core"), None), P(("grp", "z", "core"), None), rows),
        out_specs=(P(("z", "core"), None), P(("z", "core"), None), P(("grp", "z", "core"), None)),
        check_vma=False,
    )
```
